32 devices in a mesh: pts: 8 (over z, y), blk: 4 (over x, core).
Axes of the slice: x: 2, y: 2, z: 4, core: 2. Of those that a mesh axis runs over, the one named last changes fastest.
Arguments:
- points: bfloat16 [16384, 512], P('pts', 'blk'), may hold values from -6 to 6
- neighbours: int32 [16384, 27], P('pts'), may hold values from 0 to 16383, as said below
- patch_ids: int32 [16384], P('pts'), may hold values from 0 to 31, as said below
- conv_weight: bfloat16 [27, 512, 512], P(None, 'blk'), may hold values from -0.0546875 to 0.0546875
- conv_bias: float32 [512], P('blk'), may hold values from -3 to 3
- cpe_weight: bfloat16 [512, 512], P('blk'), may hold values from -0.25 to 0.25
- cpe_bias: float32 [512], P('blk'), may hold values from -3 to 3
- cpe_gain: float32 [512], P('blk'), may hold values from 0.1 to 1.9
- cpe_shift: float32 [512], P('blk'), may hold values from -1.75 to 1.75
- first_gain: float32 [512], P('blk'), may hold values from 0.1 to 1.9
- first_shift: float32 [512], P('blk'), may hold values from -1.75 to 1.75
- qkv_weight: bfloat16 [512, 3, 512], P(None, None, 'blk'), may hold values from -0.25 to 0.25
- query_value_bias: float32 [2, 512], P(None, 'blk'), may hold values from -3 to 3
- proj_weight: bfloat16 [512, 512], P('blk'), may hold values from -4 to 4
- proj_bias: float32 [512], P('blk'), may hold values from -3 to 3
- second_gain: float32 [512], P('blk'), may hold values from 0.1 to 1.9
- second_shift: float32 [512], P('blk'), may hold values from -1.75 to 1.75
- hidden_weight: bfloat16 [512, 2048], P(None, 'blk'), may hold values from -0.25 to 0.25
- hidden_bias: float32 [2048], P('blk'), may hold values from -3 to 3
- output_weight: bfloat16 [2048, 512], P('blk'), may hold values from -0.125 to 0.125
- output_bias: float32 [512], P('blk'), may hold values from -3 to 3
- out_grad: bfloat16 [16384, 512], P('pts', 'blk'), may hold values from -8 to 8
Outputs:
- block_out: bfloat16 [16384, 512], P('pts', 'blk')
- grad_points: float32 [16384, 512], P('pts', 'blk')
- grad_conv_weight: float32 [27, 512, 512], P(None, 'blk', 'pts')
- grad_conv_bias: float32 [512], P('blk')
- grad_cpe_weight: float32 [512, 512], P('blk', 'pts')
- grad_cpe_bias: float32 [512], P('blk')
- grad_cpe_gain: float32 [512], P('blk')
- grad_cpe_shift: float32 [512], P('blk')
- grad_first_gain: float32 [512], P('blk')
- grad_first_shift: float32 [512], P('blk')
- grad_qkv_weight: float32 [512, 3, 512], P('pts', None, 'blk')
- grad_query_value_bias: float32 [2, 512], P(None, 'blk')
- grad_proj_weight: float32 [512, 512], P('blk', 'pts')
- grad_proj_bias: float32 [512], P('blk')
- grad_second_gain: float32 [512], P('blk')
- grad_second_shift: float32 [512], P('blk')
- grad_hidden_weight: float32 [512, 2048], P('pts', 'blk')
- grad_hidden_bias: float32 [2048], P('blk')
- grad_output_weight: float32 [2048, 512], P('blk', 'pts')
- grad_output_bias: float32 [512], P('blk')
The draws below stay inside these ranges and needn't reach their ends.
Inputs may be any that keep to these rules, and one draw needn't show every extreme that they name: Each neighbour lies at most 256 positions from its own point; in every draw some neighbours lie exactly 256 positions before and after their point. `patch_ids`: patch ids never fall along the points; each patch lies inside one aligned block of 1024 points and holds 1 to 1024 points, some exactly 1024; patches of different indices of pts have different ids.
All inputs are finite; a program needn't handle non-finite values.
Results may differ from the reference program's by a relative error of at most 0.02.
Values may be sent and summed in bfloat16 or wider, within the bound.
No kernel may reach another device: no remote copies, remote signals or barrier semaphores. Data moves between devices by JAX's collectives and lax.ppermute only.
A program may use at most 256 MiB of HBM per device.

```python
import jax
import jax.numpy as jnp
from jax import lax

D = 512
HEADS = 32
HEAD_DIM = 16
FF = 2048
PATCH = 1024
KERNEL = 27
PATCH_DEV = 2
REACH = 256
ROWS = 2048
POINTS = 16384


def draw_neighbours(key, part):
    key = jax.random.fold_in(key, 11)
    key_offsets, key_choose = jax.random.split(key)
    row_index = jnp.arange(POINTS, dtype=jnp.int32)[:, None]
    offsets = jax.random.randint(key_offsets, (POINTS, KERNEL), -REACH, REACH + 1).astype(jnp.int32)
    chosen = jax.random.randint(key_choose, (POINTS, 1), 0, 8) == 0
    column = jnp.arange(KERNEL, dtype=jnp.int32)[None, :]
    offsets = jnp.where(chosen & (column == 0), -REACH, offsets)
    offsets = jnp.where(chosen & (column == KERNEL - 1), REACH, offsets)
    return jnp.clip(row_index + offsets, 0, POINTS - 1).astype(jnp.int32)


def draw_patch_ids(key, part):
    key = jax.random.fold_in(key, 23)
    key_cuts, key_whole = jax.random.split(key)
    shards = POINTS // ROWS
    cuts = jax.random.randint(key_cuts, (shards, PATCH_DEV, 1), PATCH // 4, PATCH).astype(jnp.int32)
    whole = jax.random.randint(key_whole, (shards, 1, 1), 0, PATCH_DEV).astype(jnp.int32)
    blocks = jnp.arange(PATCH_DEV, dtype=jnp.int32)[None, :, None]
    cuts = jnp.where(blocks == whole, 0, cuts)
    places = jnp.arange(PATCH, dtype=jnp.int32)[None, None, :]
    shard_base = jnp.arange(shards, dtype=jnp.int32)[:, None, None] * (2 * PATCH_DEV)
    labels = shard_base + 2 * blocks + (places >= cuts).astype(jnp.int32)
    return labels.reshape(POINTS).astype(jnp.int32)


def raised(values, rng, source, target, blocks, factor):
    def block_of(position):
        return (jnp.arange(values.shape[position]) // (values.shape[position] // blocks)).reshape((-1,) + (1,) * (values.ndim - 1 - position))

    first = jax.random.permutation(rng, blocks)[block_of(target)]
    second = (block_of(target) + blocks // 2) % blocks
    return jnp.where((block_of(source) == first) | (block_of(source) == second), factor * values, values)


def level_of(key, extent, cuts, smallest, largest):
    loudness = 1.0
    for dim, parts in cuts:
        heights = jax.random.uniform(jax.random.fold_in(jax.random.fold_in(key, 6), dim), (parts,), jnp.float32, smallest / len(cuts), largest / len(cuts))
        loudness = loudness * jnp.repeat(jnp.exp(heights), extent[dim] // parts).reshape((-1,) + (1,) * (len(extent) - 1 - dim))
    return loudness


def centred(rng, dims, scale, bound, cuts=(), kind=jnp.bfloat16):
    gain = level_of(rng, dims, cuts, -0.22, 0.18) if cuts else 1.0
    result = jax.random.normal(rng, dims, jnp.float32) * scale * gain
    return jnp.minimum(jnp.maximum(result, -bound), bound).astype(kind)


def heavy_noise(key, dims, scale, bound, cuts, heavy, kind=jnp.bfloat16):
    entries = scale * jax.random.normal(key, dims, jnp.float32)
    if cuts:
        entries = entries * level_of(key, dims, cuts, -0.22, 0.18)
    return jnp.clip(raised(entries, jax.random.fold_in(key, 3), *heavy), -bound, bound).astype(kind)


def setup_inputs(seed: int = 0) -> dict:
    key_list = jax.random.split(jax.random.key(seed), 23)
    points = centred(key_list[0], (POINTS, D), 1.0, 6.0, ((0, 8), (1, 4)))
    neighbours = draw_neighbours(jax.random.fold_in(key_list[22], 71), 0)
    patch_ids = draw_patch_ids(jax.random.fold_in(key_list[22], 71), 0)
    conv_weight = centred(key_list[3], (KERNEL, D, D), (KERNEL * D) ** -0.5, 0.0546875, ((1, 4),))
    conv_bias = centred(key_list[4], (D,), 0.5, 3.0, ((0, 4),), jnp.float32)
    cpe_weight = centred(key_list[5], (D, D), D ** -0.5, 0.25, ((0, 4),))
    cpe_bias = centred(key_list[6], (D,), 0.5, 3.0, ((0, 4),), jnp.float32)
    cpe_gain = jnp.clip(1.0 + 0.18 * jax.random.normal(key_list[7], (D,), jnp.float32), 0.1, 1.9)
    cpe_shift = centred(key_list[8], (D,), 0.3, 1.75, ((0, 4),), jnp.float32)
    first_gain = jnp.clip(1.0 + 0.18 * jax.random.normal(key_list[9], (D,), jnp.float32), 0.1, 1.9)
    first_shift = centred(key_list[10], (D,), 0.3, 1.75, ((0, 4),), jnp.float32)
    qkv_weight = centred(key_list[11], (D, 3, D), D ** -0.5, 0.25, ((2, 4),))
    query_value_bias = centred(key_list[12], (2, D), 0.5, 3.0, ((1, 4),), jnp.float32)
    proj_weight = centred(key_list[13], (D, D), (max(D // 256, 1)) ** -0.5, 4.0, ((0, 4),))
    proj_bias = centred(key_list[14], (D,), 0.5, 3.0, ((0, 4),), jnp.float32)
    second_gain = jnp.clip(1.0 + 0.18 * jax.random.normal(key_list[15], (D,), jnp.float32), 0.1, 1.9)
    second_shift = centred(key_list[16], (D,), 0.3, 1.75, ((0, 4),), jnp.float32)
    hidden_weight = centred(key_list[17], (D, FF), D ** -0.5, 0.25, ((1, 4),))
    hidden_bias = centred(key_list[18], (FF,), 0.5, 3.0, ((0, 4),), jnp.float32)
    output_weight = centred(key_list[19], (FF, D), FF ** -0.5, 0.125, ((0, 4),))
    output_bias = centred(key_list[20], (D,), 0.5, 3.0, ((0, 4),), jnp.float32)
    out_grad = heavy_noise(key_list[21], (POINTS, D), 1.0, 8.0, ((0, 8), (1, 4)), (0, 1, 8, 2.0))
    return dict(points=points, neighbours=neighbours, patch_ids=patch_ids, conv_weight=conv_weight, conv_bias=conv_bias, cpe_weight=cpe_weight, cpe_bias=cpe_bias, cpe_gain=cpe_gain, cpe_shift=cpe_shift, first_gain=first_gain, first_shift=first_shift, qkv_weight=qkv_weight, query_value_bias=query_value_bias, proj_weight=proj_weight, proj_bias=proj_bias, second_gain=second_gain, second_shift=second_shift, hidden_weight=hidden_weight, hidden_bias=hidden_bias, output_weight=output_weight, output_bias=output_bias, out_grad=out_grad)


@jax.custom_vjp
def low(v):
    return lax.optimization_barrier(v.astype(jnp.bfloat16)).astype(jnp.float32)

@jax.custom_vjp
def low_back(v):
    return v

def low_keep(v):
    return (low(v), None)

def low_pass(kept, grad):
    return (grad,)

def back_keep(v):
    return (v, None)

def back_low(kept, grad):
    return (low(grad),)
low.defvjp(low_keep, low_pass)
low_back.defvjp(back_keep, back_low)
highest = lax.Precision.HIGHEST
norm_eps = 1e-05
masked_fill = -1e+30

def layer_norm(rows_in, gain_row, shifts):
    average = lax.optimization_barrier(jnp.mean(rows_in, axis=-1, keepdims=True))
    spread = lax.optimization_barrier(jnp.mean(rows_in * rows_in, axis=-1, keepdims=True)) - average * average
    return (rows_in - average) * lax.rsqrt(spread + norm_eps) * gain_row + shifts

def attend(pieces):
    query_rows, key_rows, value_rows, patch_row = pieces
    scores = jnp.einsum('qhe,khe->hqk', query_rows, key_rows, precision=highest) * HEAD_DIM ** (-0.5)
    scores = low_back(scores)
    same_patch = patch_row[:, None] == patch_row[None, :]
    scores = jnp.where(same_patch[None], scores, masked_fill)
    probability = low(jax.nn.softmax(scores, axis=-1))
    mixture = jnp.einsum('hqk,khe->qhe', probability, value_rows, precision=highest)
    return low_back(low(mixture))

def reference(points, neighbours, patch_ids, conv_weight, conv_bias, cpe_weight, cpe_bias, cpe_gain, cpe_shift, first_gain, first_shift, qkv_weight, query_value_bias, proj_weight, proj_bias, second_gain, second_shift, hidden_weight, hidden_bias, output_weight, output_bias, out_grad):
    float_args = (points, conv_weight, conv_bias, cpe_weight, cpe_bias, cpe_gain, cpe_shift, first_gain, first_shift, qkv_weight, query_value_bias, proj_weight, proj_bias, second_gain, second_shift, hidden_weight, hidden_bias, output_weight, output_bias)
    float_args = tuple((item.astype(jnp.float32) for item in float_args))

    def forward(points, conv_weight, conv_bias, cpe_weight, cpe_bias, cpe_gain, cpe_shift, first_gain, first_shift, qkv_weight, query_value_bias, proj_weight, proj_bias, second_gain, second_shift, hidden_weight, hidden_bias, output_weight, output_bias):
        conv_sum = jnp.zeros(points.shape, jnp.float32)
        for offset in range(KERNEL):
            conv_sum = conv_sum + jnp.dot(points[neighbours[:, offset]], conv_weight[offset], precision=highest)
        conv_mid = low(low_back(conv_sum) + conv_bias)
        cpe_pre = low_back(jnp.dot(conv_mid, cpe_weight, precision=highest)) + cpe_bias
        residual_one = points + layer_norm(cpe_pre, cpe_gain, cpe_shift)
        layer_one = low(layer_norm(residual_one, first_gain, first_shift))
        bias_full = jnp.stack([query_value_bias[0], jnp.zeros((D,), jnp.float32), query_value_bias[1]], axis=0)
        triple = low(low_back(jnp.einsum('pd,dtc->ptc', layer_one, qkv_weight, precision=highest) + bias_full))
        blocks = POINTS // PATCH
        shaped = triple.reshape(blocks, PATCH, 3, HEADS, HEAD_DIM)
        attended = lax.map(jax.checkpoint(attend), (shaped[:, :, 0], shaped[:, :, 1], shaped[:, :, 2], patch_ids.reshape(blocks, PATCH)))
        attended = attended.reshape(POINTS, D)
        residual_two = residual_one + low_back(jnp.dot(attended, proj_weight, precision=highest)) + proj_bias
        layer_two = low(layer_norm(residual_two, second_gain, second_shift))
        hidden_pre = low_back(jnp.dot(layer_two, hidden_weight, precision=highest)) + hidden_bias
        activated = low(jax.nn.gelu(hidden_pre, approximate=True))
        return residual_two + low_back(jnp.dot(activated, output_weight, precision=highest)) + output_bias
    block_out, pullback = jax.vjp(forward, *float_args)
    gradients = pullback(out_grad.astype(jnp.float32))
    return (block_out.astype(jnp.bfloat16), gradients[0], gradients[1], gradients[2], gradients[3], gradients[4], gradients[5], gradients[6], gradients[7], gradients[8], gradients[9], gradients[10], gradients[11], gradients[12], gradients[13], gradients[14], gradients[15], gradients[16], gradients[17], gradients[18])
```

```python
import functools
import math

import jax
import jax.numpy as jnp
from jax import lax
from jax.experimental import pallas as pl
from jax.experimental.pallas import tpu as pltpu
from jax.sharding import PartitionSpec as P

HEAD_DIM = 16
PATCH = 1024
KERNEL = 27
REACH = 256
EPS = 1e-05
LOG2E = math.log2(math.e)
BF = jnp.bfloat16
F32 = jnp.float32
VM = pltpu.VMEM
NN = ((1,), (0,))
NT = ((1,), (1,))
TN = ((0,), (0,))


def dot(a, b, dims):
    return lax.dot_general(a, b, (dims, ((), ())), preferred_element_type=F32)


def whole(count):
    return [pl.BlockSpec(memory_space=VM)] * count


def params(mib=48):
    return pltpu.CompilerParams(vmem_limit_bytes=mib * 2**20)


def cost(flops, size=4 * 2**20, exps=0):
    return pl.CostEstimate(flops=int(flops), bytes_accessed=int(size), transcendentals=int(exps))


def struct(shape, kind):
    return jax.ShapeDtypeStruct(shape, kind)


def one_hot(place):
    spots = lax.broadcasted_iota(jnp.int32, (256, 256), 0)
    return jnp.where(spots == jnp.broadcast_to(place, (256, 256)), 1.0, 0.0).astype(BF)


def conv_kernel(window, place, weight, conv, gathered, turned):
    width = window.shape[1]
    for j in range(window.shape[0] // 256):
        turned[j * width : (j + 1) * width, :] = window[j * 256 : (j + 1) * 256, :].T
    for b in range(place.shape[1] // 256):
        cols = slice(b * 256, (b + 1) * 256)
        left = turned[b * width : (b + 3) * width, :]
        for k in range(KERNEL):
            spot = place[k : k + 1, cols]
            part = jnp.broadcast_to(lax.shift_right_logical(spot, 8) - b, (width, 256))
            three = dot(left, one_hot(jnp.bitwise_and(spot, 255)), NN)
            rows = jnp.where(
                part == 0,
                three[:width],
                jnp.where(part == 1, three[width : 2 * width], three[2 * width :]),
            )
            gathered[k * width : (k + 1) * width, cols] = rows.astype(BF)
        conv[cols, :] = dot(gathered[:, cols], weight[...], TN).astype(conv.dtype)


def conv_forward(window, place, weight, kind):
    rows, width, wide = place.shape[1], window.shape[1], weight.shape[1]
    return pl.pallas_call(
        conv_kernel,
        out_shape=(struct((rows, wide), kind), struct((KERNEL * width, rows), BF)),
        in_specs=whole(3),
        out_specs=whole(2),
        scratch_shapes=[pltpu.VMEM((window.shape[0] // 256 * width, 256), BF)],
        compiler_params=params(),
        cost_estimate=cost(4 * rows * KERNEL * width * wide),
        name="conv_forward",
    )(window, place, weight)


def spread_kernel(place, weight, grads, out, upstream):
    width = out.shape[0]
    out[...] = jnp.zeros(out.shape, F32)
    step = 9
    for b in range(place.shape[1] // 256):
        cols = slice(b * 256, (b + 1) * 256)
        upstream[...] = dot(weight[...], grads[cols, :], NT)
        for s in range(KERNEL // step):
            left, right = [], []
            for k in range(s * step, (s + 1) * step):
                spot = place[k : k + 1, cols]
                part = jnp.broadcast_to(lax.shift_right_logical(spot, 8) - b, (width, 256))
                mine = upstream[k * width : (k + 1) * width, :]
                left.append(
                    jnp.concatenate(
                        [jnp.where(part == i, mine, 0.0).astype(BF) for i in range(3)], axis=0
                    )
                )
                right.append(one_hot(jnp.bitwise_and(spot, 255)))
            three = dot(jnp.concatenate(left, axis=1), jnp.concatenate(right, axis=1), NT)
            for i in range(3):
                at = slice((b + i) * 256, (b + i + 1) * 256)
                out[:, at] = out[:, at] + three[i * width : (i + 1) * width]


def spread(place, weight, grads):
    rows, wide = grads.shape
    width = weight.shape[0] // KERNEL
    return pl.pallas_call(
        spread_kernel,
        out_shape=struct((width, rows + 2 * REACH), F32),
        in_specs=whole(3),
        out_specs=pl.BlockSpec(memory_space=VM),
        scratch_shapes=[pltpu.VMEM((KERNEL * width, 256), F32)],
        compiler_params=params(),
        cost_estimate=cost(4 * rows * KERNEL * width * wide),
        name="spread",
    )(place, weight, grads)


def conv_weight_kernel(blocks, *refs):
    gathered, grads, out, turned = refs[:4], refs[4:8], refs[8], refs[9]
    rows = grads[0].shape[0]

    @pl.when(pl.program_id(0) == 0)
    def _():
        for q in range(4):
            turned[:, q * rows : (q + 1) * rows] = grads[q][...].T

    both = jnp.concatenate([g[...] for g in gathered], axis=1)
    total = dot(turned[...], both, NT).astype(BF)
    size = total.shape[0] // blocks
    for p in range(blocks):
        out[p] = total[p * size : (p + 1) * size]


def conv_weight_grad(gathered, grads, first, count, blocks):
    rows, wide = grads[0].shape
    tile = 384
    return pl.pallas_call(
        functools.partial(conv_weight_kernel, blocks),
        grid=(count // tile,),
        out_shape=struct((blocks, wide // blocks, count), BF),
        in_specs=[pl.BlockSpec((tile, rows), lambda i: (i + first // tile, 0))] * 4
        + [pl.BlockSpec((rows, wide), lambda i: (0, 0))] * 4,
        out_specs=pl.BlockSpec((blocks, wide // blocks, tile), lambda i: (0, 0, i)),
        scratch_shapes=[pltpu.VMEM((wide, 4 * rows), BF)],
        compiler_params=params(),
        cost_estimate=cost(8 * rows * wide * count),
        name="conv_weight_grad",
    )(*gathered, *grads)


def split3(values):
    high = values.astype(BF)
    rest = values - high.astype(F32)
    middle = rest.astype(BF)
    return high, middle, (rest - middle.astype(F32)).astype(BF)


def three_rows(high, middle, low):
    spots = lax.broadcasted_iota(jnp.int32, (16, high.shape[1]), 0)
    picked = jnp.where(
        spots == 0,
        high.astype(F32),
        jnp.where(spots == 1, middle.astype(F32), jnp.where(spots == 2, low.astype(F32), 0.0)),
    )
    return picked.astype(BF)


def one_rows(length, count):
    spots = lax.broadcasted_iota(jnp.int32, (16, length), 0)
    return jnp.where(spots < count, 1.0, 0.0).astype(BF)


def patch_codes(patch):
    shape = (32, patch.shape[1])
    spots = lax.broadcasted_iota(jnp.int32, shape, 0)
    bits = jnp.bitwise_and(
        lax.shift_right_logical(jnp.broadcast_to(patch, shape), jnp.bitwise_and(spots, 15)), 1
    )
    bits = jnp.where(spots < 16, bits, 1 - bits)
    return jnp.where(bits == 1, 1.0, 0.0).astype(BF), jnp.where(bits == 1, 0.0, -1e30).astype(BF)


def fixed_rows(patch, query_side, key_side):
    length = patch.shape[1]
    left, right = patch_codes(patch)
    key_side[48:64, :] = one_rows(length, 3)
    key_side[64:96, :] = left
    query_side[64:96, :] = right
    key_side[96:128, :] = jnp.zeros((32, length), BF)
    query_side[96:128, :] = jnp.zeros((32, length), BF)


def attend_forward_kernel(
    heads, tile, mine, other, weight, bias, patch, triple, total, keep, send, logs, query_side, key_side, value_side
):
    rows = mine.shape[0]
    length = 2 * rows
    for t in range(3):
        at = slice(t * weight.shape[0] // 3, (t + 1) * weight.shape[0] // 3)
        triple[t, :, :rows] = (dot(weight[at, :], mine[...], NT) + bias[at, :]).astype(BF)
        triple[t, :, rows:] = (dot(weight[at, :], other[...], NT) + bias[at, :]).astype(BF)
    fixed_rows(patch[...], query_side, key_side)
    value_side[16:32, :] = one_rows(length, 1)

    @pl.loop(0, heads)
    def _(h):
        at = pl.ds(pl.multiple_of(h * HEAD_DIM, HEAD_DIM), HEAD_DIM)
        query = triple[0, at, :].astype(F32) * (HEAD_DIM**-0.5 * LOG2E)
        key = triple[1, at, :]
        high, middle, low = split3(query)
        query_side[0:16, :] = high
        query_side[16:32, :] = middle
        query_side[32:48, :] = low
        query_side[48:64, :] = jnp.zeros((16, length), BF)
        key_side[0:16, :] = key
        key_side[16:32, :] = key
        key_side[32:48, :] = key
        value_side[0:16, :] = triple[2, at, :]
        wide_key = key.astype(F32)
        bound = jnp.max(jnp.sum(query * query, axis=0)) * jnp.max(
            jnp.sum(wide_key * wide_key, axis=0)
        )
        logs[pl.ds(h, 1), :] = jnp.zeros((1, length), F32)

        @pl.when(jnp.logical_not(bound < 4096.0))
        def _():
            for t in range(length // tile):
                cols = slice(t * tile, (t + 1) * tile)
                top = jnp.max(dot(key_side[...], query_side[:, cols], TN), axis=0, keepdims=True)
                query_side[48:64, cols] = three_rows(*split3(-top))
                logs[pl.ds(h, 1), cols] = top

        for t in range(length // tile):
            cols = slice(t * tile, (t + 1) * tile)
            weights = jnp.exp2(dot(key_side[...], query_side[:, cols], TN)).astype(BF)
            mixed = dot(value_side[...], weights, NN)
            sums = mixed[16:17, :]
            mixed = mixed[0:16, :] * (1.0 / sums)
            total[at, cols] = mixed
            if t * tile < rows:
                keep[at, cols] = mixed.astype(BF)
            else:
                send[at, t * tile - rows : (t + 1) * tile - rows] = mixed.astype(BF)
            logs[pl.ds(h, 1), cols] = logs[pl.ds(h, 1), cols] + jnp.log2(sums)


def attend_forward(mine, other, weight, bias, patch):
    rows, length = mine.shape[0], 2 * mine.shape[0]
    width = weight.shape[0] // 3
    heads = width // HEAD_DIM
    return pl.pallas_call(
        functools.partial(attend_forward_kernel, heads, 512),
        out_shape=(
            struct((3, width, length), BF),
            struct((width, length), F32),
            struct((width, rows), BF),
            struct((width, rows), BF),
            struct((heads, length), F32),
        ),
        in_specs=whole(5),
        out_specs=whole(5),
        scratch_shapes=[
            pltpu.VMEM((128, length), BF),
            pltpu.VMEM((128, length), BF),
            pltpu.VMEM((32, length), BF),
        ],
        compiler_params=params(),
        cost_estimate=cost(heads * length * length * 1200, 6 * 2**20, heads * length * length),
        name="attend_forward",
    )(mine, other, weight, bias, patch)


def attend_backward_kernel(
    heads, tile, triple, patch, mine, other, mixed, logs, out, query_side, key_side, value_side, grad_side, grad_value, grad_key
):
    length = triple.shape[2]
    fixed_rows(patch[...], query_side, key_side)
    value_side[16:32, :] = one_rows(length, 3)

    @pl.loop(0, heads)
    def _(h):
        at = pl.ds(pl.multiple_of(h * HEAD_DIM, HEAD_DIM), HEAD_DIM)
        query, key = triple[0, at, :], triple[1, at, :]
        upstream = jnp.concatenate([mine[at, :], other[at, :]], axis=1)
        high, middle, low = split3(query.astype(F32) * (HEAD_DIM**-0.5 * LOG2E))
        query_side[0:16, :] = high
        query_side[16:32, :] = middle
        query_side[32:48, :] = low
        query_side[48:64, :] = three_rows(*split3(-logs[pl.ds(h, 1), :]))
        key_side[0:16, :] = key
        key_side[16:32, :] = key
        key_side[32:48, :] = key
        value_side[0:16, :] = triple[2, at, :]
        inner = jnp.sum(upstream.astype(F32) * mixed[at, :], axis=0, keepdims=True)
        grad_side[0:16, :] = upstream
        grad_side[16:32, :] = three_rows(*split3(-inner))
        for t in range(length // tile):
            cols = slice(t * tile, (t + 1) * tile)
            prob = jnp.exp2(dot(query_side[:, cols], key_side[...], TN))
            grad_prob = dot(grad_side[:, cols], value_side[...], TN)
            grad_score = (prob * grad_prob).astype(BF)
            value_part = dot(upstream[:, cols], prob.astype(BF), NN)
            key_part = dot(query[:, cols], grad_score, NN)
            out[0, at, cols] = (dot(key, grad_score, NT) * HEAD_DIM**-0.5).astype(BF)
            if t == 0:
                grad_value[...] = value_part
                grad_key[...] = key_part
            else:
                grad_value[...] += value_part
                grad_key[...] += key_part
        out[1, at, :] = (grad_key[...] * HEAD_DIM**-0.5).astype(BF)
        out[2, at, :] = grad_value[...].astype(BF)


def attend_backward(triple, patch, mine, other, mixed, logs):
    width, length = triple.shape[1:]
    heads = width // HEAD_DIM
    return pl.pallas_call(
        functools.partial(attend_backward_kernel, heads, 512),
        out_shape=struct((3, width, length), BF),
        in_specs=whole(6),
        out_specs=pl.BlockSpec(memory_space=VM),
        scratch_shapes=[
            pltpu.VMEM((128, length), BF),
            pltpu.VMEM((128, length), BF),
            pltpu.VMEM((32, length), BF),
            pltpu.VMEM((32, length), BF),
            pltpu.VMEM((16, length), F32),
            pltpu.VMEM((16, length), F32),
        ],
        compiler_params=params(),
        cost_estimate=cost(heads * length * length * 2400, 6 * 2**20, heads * length * length),
        name="attend_backward",
    )(triple, patch, mine, other, mixed, logs)


def norm_rows(values):
    average = jnp.mean(values, axis=1, keepdims=True)
    scaling = lax.rsqrt(
        jnp.mean(values * values, axis=1, keepdims=True) - average * average + EPS
    )
    return (values - average) * scaling, scaling


def norm_rows_back(upstream, normed, scaling, gain):
    scaled = upstream * gain
    return scaling * (
        scaled
        - jnp.mean(scaled, axis=1, keepdims=True)
        - normed * jnp.mean(scaled * normed, axis=1, keepdims=True)
    )


def first_rows_kernel(
    me, part, near, far, features, weight, vectors, layer, middle, normed_cpe, scaling_cpe, residual, normed, scaling
):
    device = me[0]
    low = (
        part[...].astype(F32) + near[...].astype(F32) + far[...].astype(F32) + vectors[0:1, :]
    ).astype(BF)
    middle[...] = low
    width = features.shape[2]
    pre = vectors[1:2, :]
    for j in range(4):
        pre = pre + dot(low[:, j * width : (j + 1) * width], weight[j ^ device], NN)
    xhat, rate = norm_rows(pre)
    normed_cpe[...] = xhat
    scaling_cpe[...] = rate
    points = jnp.concatenate([features[j ^ device] for j in range(4)], axis=1)
    sums = points.astype(F32) + xhat * vectors[2:3, :] + vectors[3:4, :]
    residual[...] = sums
    xhat, rate = norm_rows(sums)
    normed[...] = xhat
    scaling[...] = rate
    layer[...] = (xhat * vectors[4:5, :] + vectors[5:6, :]).astype(BF)


def tiled(shape, tile, dim=0):
    block = list(shape)
    block[dim] = tile
    return pl.BlockSpec(tuple(block), lambda i: tuple(i if d == dim else 0 for d in range(len(shape))))


def fixed(shape):
    return pl.BlockSpec(shape, lambda i: (0,) * len(shape))


SMEM = pl.BlockSpec(memory_space=pltpu.SMEM)


def first_rows(me, part, near, far, features, weight, vectors):
    rows, wide = part.shape
    tile = 256
    outs = [
        struct((rows, wide), BF),
        struct((rows, wide), BF),
        struct((rows, wide), F32),
        struct((rows, 1), F32),
        struct((rows, wide), F32),
        struct((rows, wide), F32),
        struct((rows, 1), F32),
    ]
    return pl.pallas_call(
        first_rows_kernel,
        grid=(rows // tile,),
        out_shape=outs,
        in_specs=[
            SMEM,
            tiled(part.shape, tile),
            tiled(near.shape, tile),
            tiled(far.shape, tile),
            tiled(features.shape, tile, 1),
            fixed(weight.shape),
            fixed(vectors.shape),
        ],
        out_specs=[tiled(o.shape, tile) for o in outs],
        compiler_params=params(),
        cost_estimate=cost(6 * rows * wide * wide),
        name="first_rows",
    )(me, part, near, far, features, weight, vectors)


def gelu_parts(u):
    scale = math.sqrt(2 / math.pi)
    square = u * u
    bent = jnp.tanh(scale * u * (1.0 + 0.044715 * square))
    half = 0.5 * (1.0 + bent)
    slope = half + 0.5 * u * (1.0 - bent * bent) * (scale * (1.0 + 3 * 0.044715 * square))
    return u * half, slope


def second_rows_kernel(
    me, keep, got, residual, upstream, vectors, hidden_bias, w0, w1, w2, w3,
    block_out, active, before, layer, carried, low, grad_keep, grad_send, grad_hidden_bias, sums,
):
    device = me[0]
    packs = (w0, w1, w2, w3)
    wide = residual.shape[1]
    base = residual[...] + vectors[6:7, :]
    attended = (keep, got, keep, got)
    for e in range(4):
        spots = slice(e // 2 * 128, e // 2 * 128 + 128)
        base = base + dot(attended[e][spots, :], packs[e][2 * wide :, :], TN)
    normed, scaling = norm_rows(base)
    lower = (normed * vectors[7:8, :] + vectors[8:9, :]).astype(BF)
    layer[...] = lower
    grads = jnp.concatenate([upstream[j ^ device] for j in range(4)], axis=1)
    wide_grads = grads.astype(F32)
    result = base + vectors[9:10, :]
    grad_layer = jnp.zeros(residual.shape, F32)
    step = pl.program_id(0)

    def add(ref, index, value):
        @pl.when(step == 0)
        def _():
            ref[index, :] = value

        @pl.when(step != 0)
        def _():
            ref[index, :] = ref[index, :] + value

    for e in range(4):
        hidden, output = packs[e][0:wide, :], packs[e][wide : 2 * wide, :]
        act, slope = gelu_parts(dot(lower, hidden, NN) + hidden_bias[e : e + 1, :])
        act = act.astype(BF)
        active[e] = act
        result = result + dot(act, output, NN)
        pre = dot(grads, output, NT) * slope
        add(grad_hidden_bias, slice(e, e + 1), jnp.sum(pre, axis=0, keepdims=True))
        pre = pre.astype(BF)
        before[e] = pre
        grad_layer = grad_layer + dot(pre, hidden, NT)
    result = result.astype(BF)
    width = wide // 4
    for j in range(4):
        block_out[j ^ device] = result[:, j * width : (j + 1) * width]
    add(sums, slice(0, 1), jnp.sum(grad_layer * normed, axis=0, keepdims=True))
    add(sums, slice(1, 2), jnp.sum(grad_layer, axis=0, keepdims=True))
    add(sums, slice(3, 4), jnp.sum(wide_grads, axis=0, keepdims=True))
    carry = wide_grads + norm_rows_back(grad_layer, normed, scaling, vectors[7:8, :])
    carried[...] = carry
    add(sums, slice(2, 3), jnp.sum(carry, axis=0, keepdims=True))
    carry = carry.astype(BF)
    low[...] = carry
    for e in range(4):
        out = (grad_keep, grad_send, grad_keep, grad_send)[e]
        out[e // 2 * 128 : e // 2 * 128 + 128, :] = dot(packs[e][2 * wide :, :], carry, NT).astype(BF)


def second_rows(me, keep, got, residual, upstream, vectors, hidden_bias, packs):
    rows, wide = residual.shape
    tile = 256
    outs = [
        (struct((4, rows, wide // 4), BF), 1),
        (struct((4, rows, wide), BF), 1),
        (struct((4, rows, wide), BF), 1),
        (struct((rows, wide), BF), 0),
        (struct((rows, wide), F32), 0),
        (struct((rows, wide), BF), 0),
        (struct(keep.shape, BF), 1),
        (struct(keep.shape, BF), 1),
        (struct((4, wide), F32), None),
        (struct((4, wide), F32), None),
    ]
    return pl.pallas_call(
        second_rows_kernel,
        grid=(rows // tile,),
        out_shape=[o for o, dim in outs],
        in_specs=[
            SMEM,
            tiled(keep.shape, tile, 1),
            tiled(got.shape, tile, 1),
            tiled(residual.shape, tile),
            tiled(upstream.shape, tile, 1),
            fixed(vectors.shape),
            fixed(hidden_bias.shape),
        ]
        + [fixed(p.shape) for p in packs],
        out_specs=[fixed(o.shape) if dim is None else tiled(o.shape, tile, dim) for o, dim in outs],
        compiler_params=params(),
        cost_estimate=cost(36 * rows * wide * wide, 16 * 2**20),
        name="second_rows",
    )(me, keep, got, residual, upstream, vectors, hidden_bias, *packs)


def cut_rows(ref, index, cols, value, blocks):
    size = value.shape[0] // blocks
    for p in range(blocks):
        ref[index, p, :, cols] = value[p * size : (p + 1) * size].astype(ref.dtype)


def second_weights_kernel(blocks, which, upstream, active, before, layer, low, attended, out, wide_grads):
    wide = layer.shape[1]
    wide_grads[...] = upstream[...]
    for i, e in enumerate(which):
        cut_rows(out, i, slice(0, wide), dot(layer[...], before[e], TN), blocks)
        cut_rows(out, i, slice(wide, 2 * wide), dot(wide_grads[...], active[e], TN), blocks)
        part = dot(attended[i * 128 : (i + 1) * 128, :], low[...], NN)
        cut_rows(out, i, slice(2 * wide, 2 * wide + 128), part.T, blocks)


def second_weights(which, blocks, upstream, active, before, layer, low, attended):
    rows, wide = layer.shape
    return pl.pallas_call(
        functools.partial(second_weights_kernel, blocks, which),
        out_shape=struct((2, blocks, wide // blocks, 2 * wide + 128), BF),
        in_specs=whole(6),
        out_specs=pl.BlockSpec(memory_space=VM),
        scratch_shapes=[pltpu.VMEM((rows, wide), BF)],
        compiler_params=params(),
        cost_estimate=cost(9 * rows * wide * wide, 8 * 2**20),
        name="second_weights",
    )(upstream, active, before, layer, low, attended)


def triple_weights_kernel(blocks, grads, mine, other, out, sums):
    rows = mine.shape[0]
    width = grads.shape[1] // 2
    for t in range(3):
        for i in range(2):
            at = slice(i * width, (i + 1) * width)
            part = dot(grads[t, at, :rows], mine[...], NN) + dot(grads[t, at, rows:], other[...], NN)
            cut_rows(out, i, slice(t * width, (t + 1) * width), part.T, blocks)
        sums[t] = jnp.sum(grads[t].astype(F32), axis=1, keepdims=True)


def triple_weights(blocks, grads, mine, other):
    wide = mine.shape[1]
    width = grads.shape[1] // 2
    return pl.pallas_call(
        functools.partial(triple_weights_kernel, blocks),
        out_shape=(
            struct((2, blocks, wide // blocks, 3 * width), BF),
            struct((3, 2 * width, 1), F32),
        ),
        in_specs=whole(3),
        out_specs=whole(2),
        compiler_params=params(),
        cost_estimate=cost(12 * grads.shape[2] * wide * width),
        name="triple_weights",
    )(grads, mine, other)


def layer_grad_kernel(grads, weight, out):
    total = dot(grads[0], weight[0], TN) + dot(grads[1], weight[1], TN) + dot(grads[2], weight[2], TN)
    out[...] = total.astype(out.dtype)


def layer_grad(grads, weight, half, kind):
    width, length = grads.shape[1:]
    wide = weight.shape[1]
    rows = length // 2
    return pl.pallas_call(
        layer_grad_kernel,
        grid=(1,),
        out_shape=struct((rows, wide), kind),
        in_specs=[
            pl.BlockSpec((3, width, rows), lambda i: (0, 0, half)),
            fixed((3, width, wide)),
        ],
        out_specs=fixed((rows, wide)),
        compiler_params=params(),
        cost_estimate=cost(6 * rows * wide * width),
        name="layer_grad",
    )(grads, weight.reshape(3, width, wide))


def third_rows_kernel(
    me, part, near, carried, normed, scaling, normed_cpe, scaling_cpe, weight, vectors, conv_grad, points_grad, low, sums
):
    device = me[0]
    step = pl.program_id(0)

    def add(index, value):
        value = jnp.sum(value, axis=0, keepdims=True)

        @pl.when(step == 0)
        def _():
            sums[index, :] = value

        @pl.when(step != 0)
        def _():
            sums[index, :] = sums[index, :] + value

    upstream = part[...] + near[...].astype(F32)
    xhat = normed[...]
    add(slice(4, 5), upstream * xhat)
    add(slice(5, 6), upstream)
    grads = carried[...] + norm_rows_back(upstream, xhat, scaling[...], vectors[4:5, :])
    width = points_grad.shape[2]
    lower = grads.astype(BF)
    for j in range(4):
        points_grad[j ^ device] = lower[:, j * width : (j + 1) * width]
    xhat = normed_cpe[...]
    add(slice(2, 3), grads * xhat)
    add(slice(3, 4), grads)
    grads = norm_rows_back(grads, xhat, scaling_cpe[...], vectors[2:3, :])
    add(slice(1, 2), grads)
    lower = grads.astype(BF)
    low[...] = lower
    for j in range(4):
        at = slice(j * width, (j + 1) * width)
        piece = dot(lower, weight[j ^ device], NT)
        conv_grad[:, at] = piece.astype(BF)
        value = jnp.sum(piece, axis=0, keepdims=True)

        @pl.when(step == 0)
        def _():
            sums[0:1, at] = value

        @pl.when(step != 0)
        def _():
            sums[0:1, at] = sums[0:1, at] + value


def third_rows(me, part, near, carried, normed, scaling, normed_cpe, scaling_cpe, weight, vectors):
    rows, wide = part.shape
    tile = 256
    outs = [
        (struct((rows, wide), BF), 0),
        (struct((4, rows, wide // 4), BF), 1),
        (struct((rows, wide), BF), 0),
        (struct((6, wide), F32), None),
    ]
    return pl.pallas_call(
        third_rows_kernel,
        grid=(rows // tile,),
        out_shape=[o for o, dim in outs],
        in_specs=[SMEM]
        + [tiled(a.shape, tile) for a in (part, near, carried, normed, scaling, normed_cpe, scaling_cpe)]
        + [fixed(weight.shape), fixed(vectors.shape)],
        out_specs=[fixed(o.shape) if dim is None else tiled(o.shape, tile, dim) for o, dim in outs],
        compiler_params=params(),
        cost_estimate=cost(6 * rows * wide * wide),
        name="third_rows",
    )(me, part, near, carried, normed, scaling, normed_cpe, scaling_cpe, weight, vectors)


def cpe_weights_kernel(blocks, me, middle, low, out):
    device = me[0]
    for e in range(4):
        at = pl.ds(pl.multiple_of((e ^ device) * 128, 128), 128)
        cut_rows(out, e, slice(0, 128), dot(low[...], middle[:, at], TN), blocks)


def cpe_weights(blocks, me, middle, low):
    rows, wide = middle.shape
    return pl.pallas_call(
        functools.partial(cpe_weights_kernel, blocks),
        out_shape=struct((4, blocks, wide // blocks, 128), BF),
        in_specs=[SMEM] + whole(2),
        out_specs=pl.BlockSpec(memory_space=VM),
        compiler_params=params(),
        cost_estimate=cost(2 * rows * wide * wide),
        name="cpe_weights",
    )(me, middle, low)


def swap(values, e, axis="blk"):
    return lax.ppermute(values, axis, [(i, i ^ e) for i in range(lax.axis_size(axis))])


def pick(values, index):
    return lax.dynamic_index_in_dim(values, index, 0, keepdims=False)


def in_order(pieces, me):
    core, chip = (me & 1) == 1, (me >> 1) == 1
    a, b = jnp.where(core, pieces[1], pieces[0]), jnp.where(core, pieces[0], pieces[1])
    c, d = jnp.where(core, pieces[3], pieces[2]), jnp.where(core, pieces[2], pieces[3])
    return [
        jnp.where(chip, c, a),
        jnp.where(chip, d, b),
        jnp.where(chip, a, c),
        jnp.where(chip, b, d),
    ]


def scatter_sum(values, spot):
    count = values.shape[0]
    if count & (count - 1):
        return lax.psum_scatter(values, "pts", scatter_dimension=0, tiled=False).astype(F32)
    stage = 0
    while count > 1:
        values = values.reshape(count // 2, 2, *values.shape[1:])
        bit = (spot >> stage) & 1
        mine = lax.dynamic_index_in_dim(values, bit, 1, keepdims=False)
        theirs = lax.dynamic_index_in_dim(values, 1 - bit, 1, keepdims=False)
        count //= 2
        values = mine.astype(F32) + swap(theirs, 1 << stage, "pts").astype(F32)
        if count > 1:
            values = values.astype(BF)
        stage += 1
    return values[0]


def all_sum(values):
    count = lax.axis_size("pts")
    if count & (count - 1):
        return lax.psum(values, "pts")
    stage = 1
    while stage < count:
        values = values + swap(values, stage, "pts")
        stage *= 2
    return values


def shards(
    points, neighbours, patch_ids, conv_weight, conv_bias, cpe_weight, cpe_bias, cpe_gain, cpe_shift, first_gain,
    first_shift, qkv_weight, query_value_bias, proj_weight, proj_bias, second_gain, second_shift, hidden_weight,
    hidden_bias, output_weight, output_bias, out_grad,
):
    row_count, width = points.shape
    wide = conv_weight.shape[2]
    mine = row_count // 4
    shard_count = lax.axis_size("pts")
    me = lax.axis_index("blk")
    spot = lax.axis_index("pts")
    me_ref = me.astype(jnp.int32).reshape(1)
    ups = [(i, i + 1) for i in range(shard_count - 1)]
    downs = [(i + 1, i) for i in range(shard_count - 1)]

    low = lax.ppermute(points[row_count - REACH :], "pts", ups)
    high = lax.ppermute(points[:REACH], "pts", downs)
    padded = jnp.concatenate([low, points, high], axis=0)
    lookup = (neighbours - spot * row_count + REACH).T
    lookup = jnp.concatenate([lookup, jnp.zeros((5, row_count), jnp.int32)], axis=0)

    def quarter(values, e, dim=0, extra=0):
        return lax.dynamic_slice_in_dim(values, (me ^ e) * mine, mine + extra, dim)

    windows = [quarter(padded, e, 0, 2 * REACH) for e in range(4)]
    places = [quarter(lookup, e, 1) - (me ^ e) * mine for e in range(4)]
    kernel_rows = conv_weight.reshape(KERNEL * width, wide)

    def exchange(values):
        return [quarter(values, 0)] + [swap(quarter(values, e), e) for e in (1, 2, 3)]

    def collect(values):
        first = swap(values, 1)
        second = swap(values, 2)
        return [values, first, second, swap(second, 1)]

    small = jnp.stack(
        [conv_bias, cpe_bias, cpe_gain, cpe_shift, first_gain, first_shift, proj_bias, second_gain, second_shift, output_bias]
    )
    small = jnp.concatenate([small, hidden_bias.reshape(4, width), query_value_bias], axis=0)
    small = collect(small)
    vectors = jnp.concatenate([s for s in in_order(small, me)], axis=1)
    hidden_biases = jnp.stack([s[10:14].reshape(4 * width) for s in small])
    cpe_pieces = jnp.stack(collect(cpe_weight))
    features = jnp.stack(exchange(points))
    turned = qkv_weight.transpose(1, 2, 0)
    other_turned = swap(turned, 2)
    head_weight = jnp.concatenate([turned, other_turned], axis=1).reshape(6 * width, wide)
    head_bias = jnp.stack(
        [
            jnp.concatenate([small[0][14], small[2][14]]),
            jnp.zeros((2 * width,), F32),
            jnp.concatenate([small[0][15], small[2][15]]),
        ]
    ).reshape(6 * width, 1)

    part3, gathered3 = conv_forward(windows[3], places[3], kernel_rows, BF)
    got3 = swap(part3, 1)
    part2, gathered2 = conv_forward(windows[2], places[2], kernel_rows, BF)
    far = swap((part2.astype(F32) + got3.astype(F32)).astype(BF), 2)
    part1, gathered1 = conv_forward(windows[1], places[1], kernel_rows, BF)
    near = swap(part1, 1)
    part0, gathered0 = conv_forward(windows[0], places[0], kernel_rows, F32)

    layer_one, conv_low, normed_cpe, scaling_cpe, residual_one, normed_one, scaling_one = first_rows(
        me_ref, part0, near, far, features, cpe_pieces, vectors
    )
    other_one = swap(layer_one, 1)
    patch_row = jnp.concatenate([quarter(patch_ids, 0), quarter(patch_ids, 1)]).reshape(1, 2 * mine)

    packs = collect(jnp.concatenate([hidden_weight, output_weight, proj_weight], axis=0))
    upstream = jnp.stack(exchange(out_grad))

    triple, mixed, keep, send, logs = attend_forward(layer_one, other_one, head_weight, head_bias, patch_row)
    got = swap(send, 1)
    (
        block_pieces, active, before, layer_two, carried, carried_low, grad_keep, grad_send, sum_hidden_bias, sums_two,
    ) = second_rows(me_ref, keep, got, residual_one, upstream, vectors, hidden_biases, packs)
    grad_got = swap(grad_send, 1)

    grads_wide = jnp.concatenate(in_order(upstream, me), axis=1)
    weights_send = second_weights((1, 3), shard_count, grads_wide, active, before, layer_two, carried_low, got)
    weights_got = swap(weights_send, 1)
    weights_keep = second_weights((0, 2), shard_count, grads_wide, active, before, layer_two, carried_low, keep)
    weights_sum = (weights_keep.astype(F32) + weights_got.astype(F32)).astype(BF)
    weights_far = swap(weights_sum[1], 2)
    second_sum = (weights_sum[0].astype(F32) + weights_far.astype(F32)).astype(BF)

    grad_triple = attend_backward(triple, patch_row, grad_keep, grad_got, mixed, logs)
    layer_send = layer_grad(grad_triple, head_weight, 1, BF)
    layer_got = swap(layer_send, 1)
    layer_part = layer_grad(grad_triple, head_weight, 0, F32)
    conv_grad, points_pieces, cpe_low, sums_one = third_rows(
        me_ref, layer_part, layer_got, carried, normed_one, scaling_one, normed_cpe, scaling_cpe, cpe_pieces, vectors
    )

    grad0 = conv_grad
    grad1 = swap(grad0, 1)
    grad2 = swap(grad0, 2)
    grad3 = swap(grad2, 1)
    spread0 = spread(places[0], kernel_rows, grad0)
    spread1 = spread(places[1], kernel_rows, grad1)

    triple_grads, triple_sums = triple_weights(shard_count, grad_triple, layer_one, other_one)
    cpe_grads = cpe_weights(shard_count, me_ref, conv_low, cpe_low)
    cpe_got = swap(jnp.stack([cpe_grads[1], cpe_grads[3]]), 1)
    cpe_keep = (jnp.stack([cpe_grads[0], cpe_grads[2]]).astype(F32) + cpe_got.astype(F32)).astype(BF)
    third_grads = jnp.concatenate([triple_grads, cpe_keep], axis=3)
    third_sum = (third_grads[0].astype(F32) + swap(third_grads[1], 2).astype(F32)).astype(BF)

    gathered = (gathered0, gathered1, gathered2, gathered3)
    grads = (grad0, grad1, grad2, grad3)
    cuts = 3
    chunk = KERNEL // cuts * width
    conv_sums = []
    for i in range(cuts):
        piece = conv_weight_grad(gathered, grads, i * chunk, chunk, shard_count)
        conv_sums.append(scatter_sum(piece, spot))
    spread2 = spread(places[2], kernel_rows, grad2)
    spread3 = spread(places[3], kernel_rows, grad3)

    second_sum = scatter_sum(second_sum, spot)
    third_sum = scatter_sum(third_sum, spot)

    sums = jnp.concatenate([sums_one, sums_two], axis=0)
    width_pieces = [sums[:, j * width : (j + 1) * width] for j in range(4)]
    width_pieces = in_order(width_pieces, me)
    triple_sums = triple_sums[:, :, 0]
    empty = jnp.zeros((2, width), F32)
    heads_pieces = [
        jnp.stack([triple_sums[0, :width], triple_sums[2, :width]]),
        empty,
        jnp.stack([triple_sums[0, width:], triple_sums[2, width:]]),
        empty,
    ]
    small = jnp.stack(
        [
            jnp.concatenate([width_pieces[e], sum_hidden_bias[e].reshape(4, width), heads_pieces[e]], axis=0)
            for e in range(4)
        ]
    )
    small = jnp.stack([small[0], small[2]]) + swap(jnp.stack([small[1], small[3]]), 1)
    small = all_sum(small[0] + swap(small[1], 2))

    spreads = in_order([spread0, spread1, spread2, spread3], me)
    grad_padded = jnp.zeros((width, row_count + 2 * REACH), F32)
    for q in range(4):
        grad_padded = grad_padded + jnp.pad(spreads[q], ((0, 0), (q * mine, (3 - q) * mine)))
    from_above = lax.ppermute(grad_padded[:, :REACH].astype(BF), "pts", downs).astype(F32)
    from_below = lax.ppermute(grad_padded[:, row_count + REACH :].astype(BF), "pts", ups).astype(F32)
    inside = grad_padded[:, REACH : REACH + row_count]
    inside = inside + jnp.pad(from_below, ((0, 0), (0, row_count - REACH)))
    inside = inside + jnp.pad(from_above, ((0, 0), (row_count - REACH, 0)))
    points_rows = [points_pieces[0]] + [swap(points_pieces[e], e) for e in (1, 2, 3)]
    points_rows = jnp.concatenate(in_order(points_rows, me), axis=0)
    grad_points = points_rows.astype(F32) + inside.T
    block_rows = [block_pieces[0]] + [swap(block_pieces[e], e) for e in (1, 2, 3)]
    block_out = jnp.concatenate(in_order(block_rows, me), axis=0)

    cols = wide // shard_count
    grad_conv = jnp.concatenate(conv_sums, axis=1).T.reshape(KERNEL, width, cols)
    return (
        block_out,
        grad_points,
        grad_conv,
        small[0],
        third_sum[:, 3 * width :].T,
        small[1],
        small[2],
        small[3],
        small[4],
        small[5],
        third_sum[:, : 3 * width].reshape(cols, 3, width),
        small[14:16],
        second_sum[:, 2 * wide :].T,
        small[8],
        small[6],
        small[7],
        second_sum[:, :wide],
        small[10:14].reshape(4 * width),
        second_sum[:, wide : 2 * wide].T,
        small[9],
    )


def solution(mesh):
    return jax.shard_map(
        shards,
        mesh=mesh,
        in_specs=(
            P("pts", "blk"),
            P("pts", None),
            P("pts"),
            P(None, "blk", None),
            P("blk"),
            P("blk", None),
            P("blk"),
            P("blk"),
            P("blk"),
            P("blk"),
            P("blk"),
            P(None, None, "blk"),
            P(None, "blk"),
            P("blk", None),
            P("blk"),
            P("blk"),
            P("blk"),
            P(None, "blk"),
            P("blk"),
            P("blk", None),
            P("blk"),
            P("pts", "blk"),
        ),
        out_specs=(
            P("pts", "blk"),
            P("pts", "blk"),
            P(None, "blk", "pts"),
            P("blk"),
            P("blk", "pts"),
            P("blk"),
            P("blk"),
            P("blk"),
            P("blk"),
            P("blk"),
            P("pts", None, "blk"),
            P(None, "blk"),
            P("blk", "pts"),
            P("blk"),
            P("blk"),
            P("blk"),
            P("pts", "blk"),
            P("blk"),
            P("blk", "pts"),
            P("blk"),
        ),
        check_vma=False,
    )
```

```python
import functools
import math

import jax
import jax.numpy as jnp
from jax import lax
from jax.experimental import pallas as pl
from jax.experimental.pallas import tpu as pltpu
from jax.sharding import PartitionSpec as P

HEAD_DIM = 16
PATCH = 1024
KERNEL = 27
REACH = 256
EPS = 1e-05
LOG2E = math.log2(math.e)
BF = jnp.bfloat16
F32 = jnp.float32
NN = ((1,), (0,))
NT = ((1,), (1,))
TN = ((0,), (0,))
VMEM = pl.BlockSpec(memory_space=pltpu.VMEM)
SMEM = pl.BlockSpec(memory_space=pltpu.SMEM)
HBM = pl.BlockSpec(memory_space=pltpu.HBM)
ANY = pl.BlockSpec(memory_space=pl.ANY)
TILE = 256


def dot(a, b, dims):
    return lax.dot_general(a, b, (dims, ((), ())), preferred_element_type=F32)


def struct(shape, kind):
    return jax.ShapeDtypeStruct(shape, kind)


TIMES = {
    "prepare": 10, "small_parts": 1, "block_rows": 1, "conv_forward": 7.5, "first_rows": 2.5, "triple_half": 2, "attend_forward": 21, "second_rows": 10,
    "second_send": 1.5, "attend_backward": 19, "second_keep": 2.5, "layer_grad": 1, "third_rows": 2.3, "cpe_weights": 1.3,
    "spread": 7, "third_weights": 2.5, "conv_weight_grad": 3.2, "finish": 1.3, "points_grad": 1.9,
}
FACTOR = 0.3


def call(name, kernel, inputs, outputs, scratch=(), mib=16, grid=None, first=()):
    count, extra = len(inputs), len(first)

    def body(*refs):
        kernel(*refs[:count], *refs[count + extra :])

    options = {} if grid is None else {"grid": grid}
    result = pl.pallas_call(
        body,
        out_shape=[o for o, spec in outputs],
        in_specs=[spec for a, spec in inputs] + [ANY] * extra,
        out_specs=[spec for o, spec in outputs],
        scratch_shapes=list(scratch),
        compiler_params=pltpu.CompilerParams(vmem_limit_bytes=mib * 2**20),
        cost_estimate=pl.CostEstimate(flops=int(TIMES[name] * FACTOR * 1.15e9), bytes_accessed=0, transcendentals=0),
        name=name,
        **options,
    )(*[pltpu.with_memory_space_constraint(a, pltpu.HBM) if spec is HBM else a for a, spec in inputs], *first)
    return result[0] if len(result) == 1 else result


def vm(*arrays):
    return [(a, VMEM) for a in arrays]


def split3(values):
    high = values.astype(BF)
    rest = values - high.astype(F32)
    middle = rest.astype(BF)
    return high, middle, (rest - middle.astype(F32)).astype(BF)


def joined(rows, width):
    rows = rows.astype(F32)
    return (rows[:, :width] + rows[:, width : 2 * width]) + rows[:, 2 * width : 3 * width]


def in_order(pieces, me):
    core, chip = (me & 1) == 1, (me >> 1) == 1
    a, b = jnp.where(core, pieces[1], pieces[0]), jnp.where(core, pieces[0], pieces[1])
    c, d = jnp.where(core, pieces[3], pieces[2]), jnp.where(core, pieces[2], pieces[3])
    return [
        jnp.where(chip, c, a),
        jnp.where(chip, d, b),
        jnp.where(chip, a, c),
        jnp.where(chip, b, d),
    ]


def folded(source, start, target, row, sems, rows):
    part, width = rows // 4, source.shape[1]
    copies = []
    for j in range(4):
        copies.append(
            pltpu.make_async_copy(
                source.at[pl.ds(pl.multiple_of(start + j * part, 16), part), :],
                target.at[row : row + part, j * width : (j + 1) * width],
                sems(),
            )
        )
    return copies


def unfolded(pack, row, at, rows):
    part, width = rows // 4, pack.shape[1] // 4
    return jnp.concatenate(
        [
            pack[row : row + part, j * width : (j + 1) * width]
            for j in range(at.start // part, at.stop // part)
        ],
        axis=0,
    )


class Plan:
    def __init__(self, rows, width):
        fold = rows // 4
        self.first_cpe = 3 * width
        self.first_points = 4 * width
        self.first_small = 4 * width + 2 * fold
        self.first_rows = self.first_small + 16
        self.near_points = width
        self.near_small = width + fold
        self.near_rows = self.near_small + 16


def counter(sems):
    state = [0]

    def take():
        state[0] += 1
        return sems.at[state[0] - 1]

    return take


VECTORS = 10


def prepare_kernel(
    plan, rows, place_of, turned_in, cpe, points, patch, *refs
):
    vectors, refs = refs[:VECTORS], refs[VECTORS:]
    hidden_bias, query_bias, away, near, turned, small, patch_row, terms, lines, long_line, pair, sems = refs
    me = place_of[0]
    width = points.shape[1]
    take = counter(sems)
    copies = [
        pltpu.make_async_copy(cpe, away.at[plan.first_cpe : plan.first_cpe + width, :], take()),
        pltpu.make_async_copy(cpe, near.at[0:width, :], take()),
    ]
    for e in (2, 3):
        copies += folded(points, (me ^ e) * rows, away, plan.first_points + (e - 2) * rows // 4, take, rows)
    copies += folded(points, (me ^ 1) * rows, near, plan.near_points, take, rows)
    for copy in copies:
        copy.start()
    loads = [pltpu.make_async_copy(vector, lines.at[r], take()) for r, vector in enumerate(vectors)]
    loads.append(pltpu.make_async_copy(hidden_bias, long_line, take()))
    loads.append(pltpu.make_async_copy(query_bias, pair, take()))
    for copy in loads:
        copy.start()
    for t in range(3):
        turned[t * width : (t + 1) * width, :] = turned_in[t].T
    for copy in loads:
        copy.wait()
    for r in range(VECTORS):
        small[r : r + 1, :] = lines[r]
    for i in range(4):
        small[VECTORS + i : VECTORS + i + 1, :] = long_line[:, i * width : (i + 1) * width]
    small[VECTORS + 4 :, :] = pair[...]
    high, middle, low = split3(small[...])
    terms[...] = jnp.concatenate([high, middle, low, jnp.zeros_like(low)], axis=1)
    last = [
        pltpu.make_async_copy(turned, away.at[0 : 3 * width, :], take()),
        pltpu.make_async_copy(terms, away.at[plan.first_small :, :], take()),
        pltpu.make_async_copy(terms, near.at[plan.near_small :, :], take()),
    ]
    for copy in last:
        copy.start()
    for e in (0, 1):
        at = pl.ds(pl.multiple_of((me ^ e) * rows, rows), rows)
        patch_row[:, e * rows : (e + 1) * rows] = patch[:, at]
    for copy in copies + last:
        copy.wait()


def prepare(plan, place_of, turned, cpe, points, patch, vectors, hidden_bias, query_bias, first=()):
    row_count, width = points.shape
    wide = cpe.shape[1]
    lines = [v.reshape(1, -1) for v in (*vectors, hidden_bias)]
    return call(
        "prepare",
        functools.partial(prepare_kernel, plan, row_count // 4),
        [(place_of, SMEM), (turned, VMEM), (cpe, HBM), (points, HBM), (patch.reshape(1, -1), VMEM)]
        + [(v, HBM) for v in (*lines, query_bias)],
        [
            (struct((plan.first_rows, wide), BF), HBM),
            (struct((plan.near_rows, wide), BF), HBM),
            (struct((3 * width, wide), BF), VMEM),
            (struct((16, width), F32), VMEM),
            (struct((1, row_count // 2), jnp.int32), VMEM),
        ],
        [
            pltpu.VMEM((16, wide), BF),
            pltpu.VMEM((VECTORS, 1, width), F32),
            pltpu.VMEM((1, 4 * width), F32),
            pltpu.VMEM((2, width), F32),
            pltpu.SemaphoreType.DMA((17 + VECTORS + 2,)),
        ],
        first=first,
    )


def one_hot(place):
    spots = lax.broadcasted_iota(jnp.int32, (256, 256), 0)
    return jnp.where(spots == jnp.broadcast_to(place, (256, 256)), 1.0, 0.0).astype(BF)


def conv_kernel(e, packs, place_of, low, points, high, lookup, weight, *refs):
    sources, refs = refs[:packs], refs[packs:]
    conv, gathered = refs[:2]
    away, near = refs[2:4] if packs else (None, None)
    turned, picked, sems = refs[-3:]
    me = place_of[0]
    width = points.shape[1]
    rows = picked.shape[1]
    quarter = me ^ e
    take = counter(sems)
    copies = []
    if packs:
        hidden, output, proj, upstream = sources
        wide, fold = hidden.shape[1], rows // 4
        copies.append(pltpu.make_async_copy(hidden, near.at[wide + width : 2 * wide + width, :], take()))
        for target in (away, near):
            copies.append(pltpu.make_async_copy(output, target.at[0:wide, :], take()))
            copies.append(pltpu.make_async_copy(proj, target.at[wide : wide + width, :], take()))
        start = wide + width
        copies += folded(upstream, (me ^ 2) * rows, away, start, take, rows)
        copies += folded(upstream, (me ^ 3) * rows, away, start + fold, take, rows)
        copies += folded(upstream, (me ^ 1) * rows, near, start + wide, take, rows)
        for copy in copies:
            copy.start()
    base = place_of[1] * points.shape[0] + quarter * rows - REACH
    last = points.shape[0] // 256 - 1
    for j in range(rows // 256 + 2):
        spot = quarter * (rows // 256) - 1 + j
        at = pl.multiple_of(jnp.clip(spot, 0, last) * 256, 256)
        piece = points[pl.ds(at, 256), :]
        piece = jnp.where(spot < 0, low[...], jnp.where(spot > last, high[...], piece))
        turned[j * width : (j + 1) * width, :] = piece.T
    step = KERNEL // 3
    for b in range(rows // 256):
        cols = slice(b * 256, (b + 1) * 256)
        left = turned[b * width : (b + 3) * width, :]
        for k in range(KERNEL):
            spot = lookup[k : k + 1, pl.ds(pl.multiple_of(quarter * rows + b * 256, 256), 256)] - base
            part = jnp.broadcast_to(lax.shift_right_logical(spot, 8) - b, (width, 256))
            three = dot(left, one_hot(jnp.bitwise_and(spot, 255)), NN)
            values = jnp.where(
                part == 0,
                three[:width],
                jnp.where(part == 1, three[width : 2 * width], three[2 * width :]),
            )
            picked[k * width : (k + 1) * width, cols] = values.astype(BF)
            if k % step == step - 1:
                at = slice((k + 1 - step) * width, (k + 1) * width)
                copies.append(pltpu.make_async_copy(picked.at[at, cols], gathered.at[at, cols], take()))
                copies[-1].start()
        conv[cols, :] = dot(picked[:, cols], weight[...], TN).astype(conv.dtype)
    for copy in copies:
        copy.wait()


def conv_forward(e, place_of, low, points, high, lookup, weight, kind, packs=(), first=()):
    rows, width, wide = points.shape[0] // 4, points.shape[1], weight.shape[1]
    outputs = [(struct((rows, wide), kind), VMEM), (struct((KERNEL * width, rows), BF), HBM)]
    if packs:
        size = wide + width + rows // 4
        outputs += [(struct((size + rows // 4, wide), BF), HBM), (struct((size + wide, wide), BF), HBM)]
    return call(
        "conv_forward",
        functools.partial(conv_kernel, e, len(packs)),
        [(place_of, SMEM)] + vm(low, points, high, lookup, weight) + [(p, HBM) for p in packs],
        outputs,
        [
            pltpu.VMEM(((rows // 256 + 2) * width, 256), BF),
            pltpu.VMEM((KERNEL * width, rows), BF),
            pltpu.SemaphoreType.DMA((6 * rows // 512 + (18 if packs else 0),)),
        ],
        first=first,
    )


def spread_kernel(e, place_of, lookup, weight, grads, out, upstream):
    width = out.shape[0]
    rows = grads.shape[0]
    quarter = place_of[0] ^ e
    base = place_of[1] * lookup.shape[1] + quarter * rows - REACH
    out[...] = jnp.zeros(out.shape, F32)
    step = 9
    for b in range(rows // 256):
        cols = slice(b * 256, (b + 1) * 256)
        upstream[...] = dot(weight[...], grads[cols, :], NT)
        for s in range(KERNEL // step):
            left, right = [], []
            for k in range(s * step, (s + 1) * step):
                spot = lookup[k : k + 1, pl.ds(pl.multiple_of(quarter * rows + b * 256, 256), 256)] - base
                part = jnp.broadcast_to(lax.shift_right_logical(spot, 8) - b, (width, 256))
                mine = upstream[k * width : (k + 1) * width, :]
                left.append(
                    jnp.concatenate(
                        [jnp.where(part == i, mine, 0.0).astype(BF) for i in range(3)], axis=0
                    )
                )
                right.append(one_hot(jnp.bitwise_and(spot, 255)))
            three = dot(jnp.concatenate(left, axis=1), jnp.concatenate(right, axis=1), NT)
            for i in range(3):
                at = slice((b + i) * 256, (b + i + 1) * 256)
                out[:, at] = out[:, at] + three[i * width : (i + 1) * width]


def spread(e, place_of, lookup, weight, grads, first=()):
    rows = grads.shape[0]
    width = weight.shape[0] // KERNEL
    return call(
        "spread",
        functools.partial(spread_kernel, e),
        [(place_of, SMEM)] + vm(lookup, weight, grads),
        [(struct((width, rows + 2 * REACH), F32), VMEM)],
        [pltpu.VMEM((KERNEL * width, 256), F32)],
        first=first,
    )


def halves(count, stage):
    keep = [r for r in range(count) if not (r >> stage) & 1]
    return keep, [r ^ (1 << stage) for r in keep]


def conv_weight_kernel(blocks, stage, place_of, *refs):
    gathered, grads, mine, theirs, total = refs[:4], refs[4:8], refs[8], refs[9], refs[10]
    total[...] = sum(dot(a[...], g[...], NN) for a, g in zip(gathered, grads)).T.astype(BF)
    size = total.shape[0] // blocks
    for out, slots in zip((mine, theirs), halves(blocks, stage)):
        for i, r in enumerate(slots):
            at = pl.multiple_of((place_of[1] ^ r) * size, size)
            out[i] = total[pl.ds(at, size), :]


def conv_weight_grad(place_of, gathered, grads, start, count, blocks, stage, first=()):
    rows, wide = grads[0].shape
    tile = 384
    half = struct((blocks // 2, wide // blocks, count), BF)
    spec = pl.BlockSpec((blocks // 2, wide // blocks, tile), lambda i: (0, 0, i))
    return call(
        "conv_weight_grad",
        functools.partial(conv_weight_kernel, blocks, stage),
        [(place_of, SMEM)]
        + [(g, pl.BlockSpec((tile, rows), lambda i: (i + start // tile, 0))) for g in gathered]
        + vm(*grads),
        [(half, spec), (half, spec)],
        [pltpu.VMEM((wide, tile), BF)],
        grid=(count // tile,),
        first=first,
    )


def finish_kernel(place_of, s0, s1, s2, s3, out, low, high):
    ordered = in_order([s[...] for s in (s0, s1, s2, s3)], place_of[0])
    rows = s0.shape[1] - 2 * REACH
    out[...] = jnp.zeros(out.shape, F32)
    for q in range(4):
        at = slice(q * rows, (q + 1) * rows + 2 * REACH)
        out[:, at] = out[:, at] + ordered[q]
    low[...] = out[:, :REACH].astype(BF)
    high[...] = out[:, out.shape[1] - REACH :].astype(BF)


def finish(place_of, spreads, first=()):
    width, span = spreads[0].shape
    total = 4 * (span - 2 * REACH) + 2 * REACH
    return call(
        "finish",
        finish_kernel,
        [(place_of, SMEM)] + vm(*spreads),
        [(struct((width, total), F32), VMEM)] + [(struct((width, REACH), BF), VMEM)] * 2,
        first=first,
    )


def points_grad_kernel(place_of, inside, below, above, own, near, far, cross, out):
    rows = own.shape[0]
    width = out.shape[1]
    pieces = [own[...], near[...], far[:, :width], cross[:, width:]]
    pieces = in_order(pieces, place_of[0])
    for q in range(4):
        total = inside[:, REACH + q * rows : REACH + (q + 1) * rows].T + pieces[q].astype(F32)
        out[q * rows : (q + 1) * rows, :] = total
    out[:REACH, :] = out[:REACH, :] + below[...].astype(F32).T
    last = out.shape[0] - REACH
    out[last:, :] = out[last:, :] + above[...].astype(F32).T


def points_grad(place_of, inside, below, above, own, near, far, cross):
    width = inside.shape[0]
    return call(
        "points_grad",
        points_grad_kernel,
        [(place_of, SMEM)] + vm(inside, below, above, own, near, far, cross),
        [(struct((4 * own.shape[0], width), F32), VMEM)],
    )


def block_rows_kernel(place_of, own, near, far, cross, out):
    rows, width = own.shape
    pieces = in_order([own[...], near[...], far[:, :width], cross[:, width:]], place_of[0])
    for q in range(4):
        out[q * rows : (q + 1) * rows, :] = pieces[q]


def block_rows(place_of, own, near, far, cross, first=()):
    rows, width = own.shape
    return call(
        "block_rows",
        block_rows_kernel,
        [(place_of, SMEM)] + vm(own, near, far, cross),
        vm(struct((4 * rows, width), BF)),
        first=first,
    )


def three_rows(high, middle, low):
    spots = lax.broadcasted_iota(jnp.int32, (16, high.shape[1]), 0)
    picked = jnp.where(
        spots == 0,
        high.astype(F32),
        jnp.where(spots == 1, middle.astype(F32), jnp.where(spots == 2, low.astype(F32), 0.0)),
    )
    return picked.astype(BF)


def one_rows(length, count):
    spots = lax.broadcasted_iota(jnp.int32, (16, length), 0)
    return jnp.where(spots < count, 1.0, 0.0).astype(BF)


def patch_codes(patch):
    shape = (32, patch.shape[1])
    spots = lax.broadcasted_iota(jnp.int32, shape, 0)
    bits = jnp.bitwise_and(
        lax.shift_right_logical(jnp.broadcast_to(patch, shape), jnp.bitwise_and(spots, 15)), 1
    )
    bits = jnp.where(spots < 16, bits, 1 - bits)
    return jnp.where(bits == 1, 1.0, 0.0).astype(BF), jnp.where(bits == 1, 0.0, -1e30).astype(BF)


def fixed_rows(patch, query_side, key_side):
    length = patch.shape[1]
    left, right = patch_codes(patch)
    key_side[48:64, :] = one_rows(length, 3)
    key_side[64:96, :] = left
    query_side[64:96, :] = right
    key_side[96:128, :] = jnp.zeros((32, length), BF)
    query_side[96:128, :] = jnp.zeros((32, length), BF)


def column(row):
    return jnp.broadcast_to(row, (128, 128)).T[:, 0:1]


def triple_rows(values, weights, smalls, out, cols):
    width = out.shape[1] // 2
    for t in range(3):
        for i in range(2):
            piece = dot(weights[i][t * width : (t + 1) * width, :], values, NT)
            if t != 1:
                piece = piece + column(smalls[i][14 + t // 2 : 15 + t // 2, :])
            out[t, i * width : (i + 1) * width, cols] = piece.astype(BF)


def triple_half_kernel(plan, values, turned, away, small, out):
    smalls = (small[...], joined(away[plan.first_small :, :], small.shape[1]))
    triple_rows(values[...], (turned, away), smalls, out, slice(0, values.shape[0]))


def triple_half(plan, values, turned, away, small):
    return call(
        "triple_half",
        functools.partial(triple_half_kernel, plan),
        vm(values, turned, away, small),
        [(struct((3, 2 * small.shape[1], values.shape[0]), BF), VMEM)],
    )


def attend_forward_kernel(
    plan, heads, tile, mine, other, turned, away, small, patch, triple, total, keep, send, logs, query_side, key_side, value_side
):
    rows = mine.shape[2]
    length = 2 * rows
    for t in range(3):
        triple[t, :, :rows] = mine[t]
    smalls = (small[...], joined(away[plan.first_small :, :], small.shape[1]))
    triple_rows(other[...], (turned, away), smalls, triple, slice(rows, length))
    fixed_rows(patch[...], query_side, key_side)
    value_side[16:32, :] = one_rows(length, 1)

    @pl.loop(0, heads)
    def _(h):
        at = pl.ds(pl.multiple_of(h * HEAD_DIM, HEAD_DIM), HEAD_DIM)
        query = triple[0, at, :].astype(F32) * (HEAD_DIM**-0.5 * LOG2E)
        key = triple[1, at, :]
        high, middle, low = split3(query)
        query_side[0:16, :] = high
        query_side[16:32, :] = middle
        query_side[32:48, :] = low
        query_side[48:64, :] = jnp.zeros((16, length), BF)
        key_side[0:16, :] = key
        key_side[16:32, :] = key
        key_side[32:48, :] = key
        value_side[0:16, :] = triple[2, at, :]
        wide_key = key.astype(F32)
        bound = jnp.max(jnp.sum(query * query, axis=0)) * jnp.max(
            jnp.sum(wide_key * wide_key, axis=0)
        )
        logs[pl.ds(h, 1), :] = jnp.zeros((1, length), F32)

        @pl.when(jnp.logical_not(bound < 4096.0))
        def _():
            for t in range(length // tile):
                cols = slice(t * tile, (t + 1) * tile)
                top = jnp.max(dot(key_side[...], query_side[:, cols], TN), axis=0, keepdims=True)
                query_side[48:64, cols] = three_rows(*split3(-top))
                logs[pl.ds(h, 1), cols] = top

        for t in range(length // tile):
            cols = slice(t * tile, (t + 1) * tile)
            weights = jnp.exp2(dot(key_side[...], query_side[:, cols], TN)).astype(BF)
            mixed = dot(value_side[...], weights, NN)
            sums = mixed[16:17, :]
            mixed = mixed[0:16, :] * (1.0 / sums)
            total[at, cols] = mixed
            if t * tile < rows:
                keep[at, cols] = mixed.astype(BF)
            else:
                send[at, t * tile - rows : (t + 1) * tile - rows] = mixed.astype(BF)
            logs[pl.ds(h, 1), cols] = logs[pl.ds(h, 1), cols] + jnp.log2(sums)


def attend_forward(plan, mine, other, turned, away, small, patch):
    width, rows = mine.shape[1:]
    length = 2 * rows
    heads = width // HEAD_DIM
    return call(
        "attend_forward",
        functools.partial(attend_forward_kernel, plan, heads, 512),
        vm(mine, other, turned, away, small, patch),
        [
            (struct((3, width, length), BF), VMEM),
            (struct((width, length), F32), VMEM),
            (struct((width, rows), BF), VMEM),
            (struct((width, rows), BF), VMEM),
            (struct((heads, length), F32), VMEM),
        ],
        [
            pltpu.VMEM((128, length), BF),
            pltpu.VMEM((128, length), BF),
            pltpu.VMEM((32, length), BF),
        ],
    )


def attend_backward_kernel(
    first, heads, tile, triple, patch, mine, other, mixed, logs, out, query_side, key_side, value_side, grad_side, grad_value, grad_key
):
    length = triple.shape[2]
    fixed_rows(patch[...], query_side, key_side)
    value_side[16:32, :] = one_rows(length, 3)

    @pl.loop(0, heads)
    def _(h):
        at = pl.ds(pl.multiple_of((h + first) * HEAD_DIM, HEAD_DIM), HEAD_DIM)
        to = pl.ds(pl.multiple_of(h * HEAD_DIM, HEAD_DIM), HEAD_DIM)
        query, key = triple[0, at, :], triple[1, at, :]
        upstream = jnp.concatenate([mine[at, :], other[at, :]], axis=1)
        high, middle, low = split3(query.astype(F32) * (HEAD_DIM**-0.5 * LOG2E))
        query_side[0:16, :] = high
        query_side[16:32, :] = middle
        query_side[32:48, :] = low
        query_side[48:64, :] = three_rows(*split3(-logs[pl.ds(h + first, 1), :]))
        key_side[0:16, :] = key
        key_side[16:32, :] = key
        key_side[32:48, :] = key
        value_side[0:16, :] = triple[2, at, :]
        inner = jnp.sum(upstream.astype(F32) * mixed[at, :], axis=0, keepdims=True)
        grad_side[0:16, :] = upstream
        grad_side[16:32, :] = three_rows(*split3(-inner))
        for t in range(length // tile):
            cols = slice(t * tile, (t + 1) * tile)
            prob = jnp.exp2(dot(query_side[:, cols], key_side[...], TN))
            grad_prob = dot(grad_side[:, cols], value_side[...], TN)
            grad_score = (prob * grad_prob).astype(BF)
            value_part = dot(upstream[:, cols], prob.astype(BF), NN)
            key_part = dot(query[:, cols], grad_score, NN)
            out[0, to, cols] = (dot(key, grad_score, NT) * HEAD_DIM**-0.5).astype(BF)
            if t == 0:
                grad_value[...] = value_part
                grad_key[...] = key_part
            else:
                grad_value[...] += value_part
                grad_key[...] += key_part
        out[1, to, :] = (grad_key[...] * HEAD_DIM**-0.5).astype(BF)
        out[2, to, :] = grad_value[...].astype(BF)


def attend_backward(first_head, heads, triple, patch, mine, other, mixed, logs, first=()):
    length = triple.shape[2]
    return call(
        "attend_backward",
        functools.partial(attend_backward_kernel, first_head, heads, 512),
        vm(triple, patch, mine, other, mixed, logs),
        [(struct((3, heads * HEAD_DIM, length), BF), VMEM)],
        [
            pltpu.VMEM((128, length), BF),
            pltpu.VMEM((128, length), BF),
            pltpu.VMEM((32, length), BF),
            pltpu.VMEM((32, length), BF),
            pltpu.VMEM((16, length), F32),
            pltpu.VMEM((16, length), F32),
        ],
        mib=24,
        first=first,
    )


def norm_rows(values):
    average = jnp.mean(values, axis=1, keepdims=True)
    scaling = lax.rsqrt(
        jnp.mean(values * values, axis=1, keepdims=True) - average * average + EPS
    )
    return (values - average) * scaling, scaling


def norm_rows_back(upstream, normed, scaling, gain):
    scaled = upstream * gain
    return scaling * (
        scaled
        - jnp.mean(scaled, axis=1, keepdims=True)
        - normed * jnp.mean(scaled * normed, axis=1, keepdims=True)
    )


def cut(values):
    width = values.shape[1] // 4
    return [values[:, j * width : (j + 1) * width] for j in range(4)]


def add_rows(ref, row, values, first):
    total = jnp.sum(values, axis=0, keepdims=True)
    ref[row : row + 1, :] = total if first else ref[row : row + 1, :] + total


def small_vectors(plan, small, near, far, cross):
    width = small.shape[1]
    return [
        small[...],
        joined(near[plan.near_small :, :], width),
        joined(far[plan.first_small :, :], width),
        joined(cross[plan.first_small :, :], width),
    ]


def vectors(smalls, me):
    return jnp.concatenate(in_order(smalls, me), axis=1)


def cpe_rows(plan, weight, near, far, cross, me):
    width = weight.shape[0]
    at = slice(plan.first_cpe, plan.first_cpe + width)
    pieces = [weight[...], near[:width, :], far[at, :], cross[at, :]]
    return jnp.concatenate(in_order(pieces, me), axis=0)


def own_rows(ref, me, rows, at):
    return ref[pl.ds(pl.multiple_of(me * rows + at.start, at.stop - at.start), at.stop - at.start), :]


def first_rows_kernel(
    plan, place_of, part, close, away, points, small, weight, near, far, cross,
    layer, middle, normed_cpe, scaling_cpe, residual, normed, scaling,
):
    me = place_of[0]
    rows = part.shape[0]
    vec = vectors(small_vectors(plan, small, near, far, cross), me)
    vec = [vec[r : r + 1, :] for r in range(6)]
    weights = cpe_rows(plan, weight, near, far, cross, me)
    for t in range(rows // TILE):
        at = slice(t * TILE, (t + 1) * TILE)
        low = (part[at, :] + close[at, :].astype(F32) + away[at, :].astype(F32) + vec[0]).astype(BF)
        middle[at, :] = low
        xhat, rate = norm_rows(dot(low, weights, NN) + vec[1])
        normed_cpe[at, :] = xhat
        scaling_cpe[at, :] = rate
        features = [
            own_rows(points, me, rows, at),
            unfolded(near, plan.near_points, at, rows),
            unfolded(far, plan.first_points, at, rows),
            unfolded(cross, plan.first_points + rows // 4, at, rows),
        ]
        features = jnp.concatenate(in_order(features, me), axis=1)
        sums = features.astype(F32) + xhat * vec[2] + vec[3]
        residual[at, :] = sums
        xhat, rate = norm_rows(sums)
        normed[at, :] = xhat
        scaling[at, :] = rate
        layer[at, :] = (xhat * vec[4] + vec[5]).astype(BF)


def first_rows(plan, place_of, part, close, away, points, small, weight, near, far, cross):
    rows, wide = part.shape
    full, thin, lower = struct((rows, wide), F32), struct((rows, 1), F32), struct((rows, wide), BF)
    return call(
        "first_rows",
        functools.partial(first_rows_kernel, plan),
        [(place_of, SMEM)] + vm(part, close, away, points, small, weight, near, far, cross),
        vm(lower, lower, full, thin, full, full, thin),
    )


def gelu_parts(u):
    scale = math.sqrt(2 / math.pi)
    square = u * u
    bent = jnp.tanh(u * (scale + (scale * 0.044715) * square))
    half = 0.5 + 0.5 * bent
    slope = half + u * (1.0 - bent * bent) * (0.5 * scale + (1.5 * 0.044715 * scale) * square)
    return u * half, slope


def second_rows_kernel(
    plan, place_of, keep, got, residual, out_grad, hidden, output, proj, small, near, far, cross, near2, far2, cross2,
    hidden_far, hidden_cross, block0, block1, block_far, active, before, layer, upstream, carried, low, grad_keep, grad_send, hidden_sums, sums,
):
    me = place_of[0]
    rows, wide = residual.shape
    smalls = small_vectors(plan, small, near, far, cross)
    vec = vectors(smalls, me)
    vec = {r: vec[r : r + 1, :] for r in (6, 7, 8, 9)}
    biases = [jnp.concatenate([s[10 + i : 11 + i, :] for i in range(4)], axis=1) for s in smalls]
    width = keep.shape[0] // 2
    packs = (near2, far2, cross2)
    end = wide + width
    hiddens = [hidden, near2.at[end : end + wide, :], hidden_far, hidden_cross]
    outputs = [output] + [p.at[0:wide, :] for p in packs]
    projs = [proj[...]] + [p[wide:end, :] for p in packs]
    mine = jnp.concatenate([projs[0], projs[2]], axis=0)
    others = jnp.concatenate([projs[1], projs[3]], axis=0)
    for t in range(rows // TILE):
        at = slice(t * TILE, (t + 1) * TILE)
        base = residual[at, :] + vec[6] + dot(keep[:, at], mine, TN) + dot(got[:, at], others, TN)
        normed, scaling = norm_rows(base)
        lower = (normed * vec[7] + vec[8]).astype(BF)
        layer[at, :] = lower
        grads = [
            own_rows(out_grad, me, rows, at),
            unfolded(near2, end + wide, at, rows),
            unfolded(far2, end, at, rows),
            unfolded(cross2, end + rows // 4, at, rows),
        ]
        grads = jnp.concatenate(in_order(grads, me), axis=1)
        upstream[at, :] = grads
        result = base + vec[9]
        grad_layer = None
        for e in range(4):
            act, slope = gelu_parts(dot(lower, hiddens[e][...], NN) + biases[e])
            act = act.astype(BF)
            active[e, at, :] = act
            result = result + dot(act, outputs[e][...], NN)
            pre = dot(grads, outputs[e][...], NT) * slope
            add_rows(hidden_sums, e, pre, t == 0)
            pre = pre.astype(BF)
            before[e, at, :] = pre
            piece = dot(pre, hiddens[e][...], NT)
            grad_layer = piece if e == 0 else grad_layer + piece
        result = in_order(cut(result.astype(BF)), me)
        block0[at, :] = result[0]
        block1[at, :] = result[1]
        block_far[at, 0:width] = result[2]
        block_far[at, width:] = result[3]
        wide_grads = grads.astype(F32)
        add_rows(sums, 0, grad_layer * normed, t == 0)
        add_rows(sums, 1, grad_layer, t == 0)
        add_rows(sums, 3, wide_grads, t == 0)
        carry = wide_grads + norm_rows_back(grad_layer, normed, scaling, vec[7])
        carried[at, :] = carry
        add_rows(sums, 2, carry, t == 0)
        carry = carry.astype(BF)
        low[at, :] = carry
        grad_keep[:, at] = dot(mine, carry, NT).astype(BF)
        grad_send[:, at] = dot(others, carry, NT).astype(BF)


def second_rows(plan, place_of, keep, got, residual, out_grad, weights, small, firsts, seconds):
    rows, wide = residual.shape
    lower, piece = struct((rows, wide), BF), struct((rows, wide // 4), BF)
    heads = struct(keep.shape, BF)
    return call(
        "second_rows",
        functools.partial(second_rows_kernel, plan),
        [(place_of, SMEM)] + vm(keep, got, residual, out_grad, *weights, small, *firsts, *seconds),
        vm(
            piece,
            piece,
            struct((rows, wide // 2), BF),
            struct((4, rows, wide), BF),
            struct((4, rows, wide), BF),
            lower,
            lower,
            struct((rows, wide), F32),
            lower,
            heads,
            heads,
            struct((4, wide), F32),
            struct((4, wide), F32),
        ),
        mib=24,
    )


def cut_rows(store, spot, cols, value, blocks):
    size = value.shape[0] // blocks
    for p in range(blocks):
        store(p ^ spot, cols, value[p * size : (p + 1) * size])


def second_weight_parts(i, e, blocks, spot, upstream, active, before, layer, low, attended, store):
    wide = layer.shape[1]
    width = attended.shape[0] // 2
    cut_rows(store, spot, slice(0, wide), dot(layer[...], before[e], TN), blocks)
    cut_rows(store, spot, slice(wide, 2 * wide), dot(upstream[...], active[e], TN), blocks)
    part = dot(attended[i * width : (i + 1) * width, :], low[...], NN)
    cut_rows(store, spot, slice(2 * wide, 2 * wide + width), part.T, blocks)


def second_send_kernel(blocks, place_of, upstream, active, before, layer, low, attended, out):
    for i, e in enumerate((1, 3)):

        def store(p, cols, value):
            out[i, p, :, cols] = value.astype(BF)

        second_weight_parts(i, e, blocks, place_of[1], upstream, active, before, layer, low, attended, store)


def second_send(place_of, blocks, upstream, active, before, layer, low, attended):
    wide = layer.shape[1]
    return call(
        "second_send",
        functools.partial(second_send_kernel, blocks),
        [(place_of, SMEM)] + vm(upstream, active, before, layer, low, attended),
        [(struct((2, blocks, wide // blocks, 2 * wide + attended.shape[0] // 2), BF), VMEM)],
    )


def second_keep_kernel(blocks, place_of, upstream, active, before, layer, low, attended, got, mine, far):
    for i, out in enumerate((mine, far)):

        def store(p, cols, value):
            out[p, :, cols] = (value + got[i, p, :, cols].astype(F32)).astype(BF)

        second_weight_parts(i, 2 * i, blocks, place_of[1], upstream, active, before, layer, low, attended, store)


def second_keep(place_of, blocks, upstream, active, before, layer, low, attended, got, first=()):
    out = struct(got.shape[1:], BF)
    return call(
        "second_keep",
        functools.partial(second_keep_kernel, blocks),
        [(place_of, SMEM)] + vm(upstream, active, before, layer, low, attended, got),
        vm(out, out),
        first=first,
    )


def third_weights_kernel(blocks, place_of, first_half, second_half, mine, other, cpe_keep, cpe_got, own, far, sums):
    rows = mine.shape[0]
    width = first_half.shape[1]
    for i, (grads, out) in enumerate(((first_half, own), (second_half, far))):

        def store(p, cols, value):
            out[p, :, cols] = value.astype(BF)

        for t in range(3):
            part = dot(grads[t, :, :rows], mine[...], NN) + dot(grads[t, :, rows:], other[...], NN)
            cut_rows(store, place_of[1], slice(t * width, (t + 1) * width), part.T, blocks)
        for p in range(blocks):
            out[p, :, 3 * width :] = (cpe_keep[i, p].astype(F32) + cpe_got[i, p].astype(F32)).astype(BF)
        for row, t in enumerate((0, 2)):
            sums[i, row : row + 1, :] = jnp.sum(grads[t].astype(F32).T, axis=0, keepdims=True)


def third_weights(place_of, blocks, first_half, second_half, mine, other, cpe_keep, cpe_got, first=()):
    wide = mine.shape[1]
    width = first_half.shape[1]
    out = struct((blocks, wide // blocks, 4 * width), BF)
    return call(
        "third_weights",
        functools.partial(third_weights_kernel, blocks),
        [(place_of, SMEM)] + vm(first_half, second_half, mine, other, cpe_keep, cpe_got),
        vm(out, out, struct((2, 2, width), F32)),
        first=first,
    )


def layer_grad_kernel(half, first_half, second_half, turned, away, out):
    width = first_half.shape[1]
    rows = first_half.shape[2] // 2
    cols = slice(half * rows, (half + 1) * rows)
    total = None
    for t in range(3):
        at = slice(t * width, (t + 1) * width)
        for grads, weight in ((first_half, turned), (second_half, away)):
            piece = dot(grads[t, :, cols], weight[at, :], TN)
            total = piece if total is None else total + piece
    out[...] = total.astype(out.dtype)


def layer_grad(half, first_half, second_half, turned, away, kind, first=()):
    return call(
        "layer_grad",
        functools.partial(layer_grad_kernel, half),
        vm(first_half, second_half, turned, away),
        [(struct((first_half.shape[2] // 2, turned.shape[1]), kind), VMEM)],
        first=first,
    )


def third_rows_kernel(
    plan, place_of, part, close, carried, normed, scaling, normed_cpe, scaling_cpe, small, weight, near, far, cross,
    conv_grad, points0, points1, points_far, low, sums,
):
    me = place_of[0]
    vec = vectors(small_vectors(plan, small, near, far, cross), me)
    weights = cpe_rows(plan, weight, near, far, cross, me)
    width = points0.shape[1]
    for t in range(part.shape[0] // TILE):
        at = slice(t * TILE, (t + 1) * TILE)
        upstream = part[at, :] + close[at, :].astype(F32)
        xhat = normed[at, :]
        add_rows(sums, 4, upstream * xhat, t == 0)
        add_rows(sums, 5, upstream, t == 0)
        grads = carried[at, :] + norm_rows_back(upstream, xhat, scaling[at, :], vec[4:5, :])
        pieces = in_order(cut(grads.astype(BF)), me)
        points0[at, :] = pieces[0]
        points1[at, :] = pieces[1]
        points_far[at, 0:width] = pieces[2]
        points_far[at, width:] = pieces[3]
        xhat = normed_cpe[at, :]
        add_rows(sums, 2, grads * xhat, t == 0)
        add_rows(sums, 3, grads, t == 0)
        grads = norm_rows_back(grads, xhat, scaling_cpe[at, :], vec[2:3, :])
        add_rows(sums, 1, grads, t == 0)
        lower = grads.astype(BF)
        low[at, :] = lower
        result = dot(lower, weights, NT)
        add_rows(sums, 0, result, t == 0)
        conv_grad[at, :] = result.astype(BF)


def third_rows(plan, place_of, part, close, carried, normed, scaling, normed_cpe, scaling_cpe, small, weight, firsts):
    rows, wide = part.shape
    lower, piece = struct((rows, wide), BF), struct((rows, wide // 4), BF)
    return call(
        "third_rows",
        functools.partial(third_rows_kernel, plan),
        [(place_of, SMEM)]
        + vm(part, close, carried, normed, scaling, normed_cpe, scaling_cpe, small, weight, *firsts),
        vm(lower, piece, piece, struct((rows, wide // 2), BF), lower, struct((6, wide), F32)),
    )


def cpe_weights_kernel(blocks, place_of, middle, low, send, keep):
    width = middle.shape[1] // 4
    for e in range(4):
        out = (keep, send, keep, send)[e]

        def store(p, cols, value):
            out[e // 2, p, :, cols] = value.astype(BF)

        at = pl.ds(pl.multiple_of((e ^ place_of[0]) * width, width), width)
        cut_rows(store, place_of[1], slice(0, width), dot(low[...], middle[:, at], TN), blocks)


def cpe_weights(blocks, place_of, middle, low):
    wide = middle.shape[1]
    out = struct((2, blocks, wide // blocks, wide // 4), BF)
    return call(
        "cpe_weights",
        functools.partial(cpe_weights_kernel, blocks),
        [(place_of, SMEM)] + vm(middle, low),
        vm(out, out),
    )


def small_parts_kernel(place_of, sums_one, sums_two, hidden_sums, triple_sums, keep, send):
    me = place_of[0]
    width = keep.shape[2]
    ones, twos = in_order(cut(sums_one[...]), me), in_order(cut(sums_two[...]), me)
    for e in range(4):
        out = (keep, send, keep, send)[e]
        out[e // 2, 0:6, :] = ones[e]
        out[e // 2, 6:10, :] = twos[e]
        for i in range(4):
            out[e // 2, 10 + i : 11 + i, :] = hidden_sums[e : e + 1, i * width : (i + 1) * width]
    keep[0, 14:16, :] = triple_sums[0]
    keep[1, 14:16, :] = triple_sums[1]
    send[:, 14:16, :] = jnp.zeros((2, 2, width), F32)


def small_parts(place_of, sums_one, sums_two, hidden_sums, triple_sums):
    out = struct((2, 16, triple_sums.shape[2]), F32)
    return call(
        "small_parts",
        small_parts_kernel,
        [(place_of, SMEM)] + vm(sums_one, sums_two, hidden_sums, triple_sums),
        vm(out, out),
    )


def swap(values, e, axis="blk"):
    return lax.ppermute(values, axis, [(i, i ^ e) for i in range(lax.axis_size(axis))])


def after(values, *first):
    return lax.optimization_barrier((values, *first))[0]


def total_of(first, second):
    return (first.astype(F32) + second.astype(F32)).astype(BF)


def chosen(values, slots):
    return jnp.concatenate([values[i : i + 1] for i in slots], axis=0) if len(slots) > 1 else values[slots[0] : slots[0] + 1]


def scatter_sum(mine, theirs, count, stage, waits=()):
    numbers, _ = halves(count, stage)
    steps = []
    order = [stage] + [b for b in range(count.bit_length() - 1) if b != stage]
    for i, bit in enumerate(order):
        got = swap(theirs, 1 << bit, "pts")
        if i + 1 == len(order):
            steps.append(mine.astype(F32) + got.astype(F32))
            break
        after_bit = order[i + 1]
        keep = [j for j, r in enumerate(numbers) if not (r >> after_bit) & 1]
        send = [numbers.index(numbers[j] ^ (1 << after_bit)) for j in keep]
        theirs = total_of(chosen(mine, send), chosen(got, send))
        mine = total_of(chosen(mine, keep), chosen(got, keep))
        numbers = [numbers[j] for j in keep]
        steps.append(theirs)
    return steps


def split_sum(first, second, stage=0):
    keep, send = halves(first.shape[0], stage)
    theirs = total_of(chosen(first, send), chosen(second, send))
    return total_of(chosen(first, keep), chosen(second, keep)), theirs


def all_sum(values, waits):
    count = lax.axis_size("pts")
    for stage in range(count.bit_length() - 1):
        values = values + swap(after(values, waits[min(stage, len(waits) - 1)]), 1 << stage, "pts")
    return values


def shards(
    points, neighbours, patch_ids, conv_weight, conv_bias, cpe_weight, cpe_bias, cpe_gain, cpe_shift, first_gain,
    first_shift, qkv_weight, query_value_bias, proj_weight, proj_bias, second_gain, second_shift, hidden_weight,
    hidden_bias, output_weight, output_bias, out_grad,
):
    row_count, width = points.shape
    wide = conv_weight.shape[2]
    mine = row_count // 4
    shard_count = lax.axis_size("pts")
    me = lax.axis_index("blk")
    place_of = jnp.stack([me, lax.axis_index("pts")]).astype(jnp.int32)
    plan = Plan(mine, width)
    ups = [(i, i + 1) for i in range(shard_count - 1)]
    downs = [(i + 1, i) for i in range(shard_count - 1)]

    low = lax.ppermute(points[row_count - REACH :], "pts", ups)
    high = lax.ppermute(points[:REACH], "pts", downs)
    kernel_rows = conv_weight.reshape(KERNEL * width, wide)
    lookup = neighbours.T
    away_pack, near_pack, turned, small, patch_row = prepare(
        plan,
        place_of,
        qkv_weight.transpose(1, 0, 2),
        cpe_weight,
        points,
        patch_ids,
        (conv_bias, cpe_bias, cpe_gain, cpe_shift, first_gain, first_shift, proj_bias, second_gain, second_shift, output_bias),
        hidden_bias,
        query_value_bias,
        first=(low, high),
    )
    hidden_far = swap(hidden_weight, 2)
    far = swap(away_pack, 2)
    near = swap(near_pack, 1)

    part3, gathered3, away_pack, near_pack = conv_forward(
        3, place_of, low, points, high, lookup, kernel_rows, BF, (hidden_weight, output_weight, proj_weight, out_grad)
    )
    got3 = swap(part3, 1)
    part2, gathered2 = conv_forward(2, place_of, low, points, high, lookup, kernel_rows, BF, first=(part3, hidden_far))
    far_part = swap(total_of(part2, got3), 2)
    part1, gathered1 = conv_forward(1, place_of, low, points, high, lookup, kernel_rows, BF, first=(part2,))
    close_part = swap(part1, 1)
    cross = swap(after(far, part1), 1)
    firsts = (near, far, cross)
    hidden_cross = swap(after(hidden_far, part1), 1)
    part0, gathered0 = conv_forward(0, place_of, low, points, high, lookup, kernel_rows, F32, first=(part1,))
    layer_one, conv_low, normed_cpe, scaling_cpe, residual_one, normed_one, scaling_one = first_rows(
        plan, place_of, part0, close_part, far_part, points, small, cpe_weight, *firsts
    )
    other_one = swap(layer_one, 1)
    far2 = swap(after(away_pack, layer_one), 2)
    near2 = swap(near_pack, 1)


    half = triple_half(plan, layer_one, turned, far, small)
    triple, mixed, keep, send, logs = attend_forward(plan, half, other_one, turned, far, small, patch_row)
    got = swap(send, 1)
    cross2 = swap(after(far2, send), 1)
    (
        block0, block1, block_far, active, before, layer_two, upstream, carried, carried_low, grad_keep, grad_send,
        sum_hidden_bias, sums_two,
    ) = second_rows(
        plan, place_of, keep, got, residual_one, out_grad, (hidden_weight, output_weight, proj_weight), small, firsts,
        (near2, far2, cross2, hidden_far, hidden_cross),
    )
    grad_got = swap(grad_send, 1)
    block_far = swap(block_far, 2)

    weights_send = second_send(place_of, shard_count, upstream, active, before, layer_two, carried_low, got)
    weights_got = swap(after(weights_send, grad_got), 1)
    heads = width // HEAD_DIM
    grad_first = attend_backward(
        0, heads, triple, patch_row, grad_keep, grad_got, mixed, logs, first=(weights_send,)
    )
    weights_mine, weights_far = second_keep(
        place_of, shard_count, upstream, active, before, layer_two, carried_low, keep, weights_got, first=(grad_first,)
    )
    weights_far = swap(weights_far, 2)
    grad_second = attend_backward(
        heads, heads, triple, patch_row, grad_keep, grad_got, mixed, logs, first=(weights_mine, block_far)
    )
    layer_send = layer_grad(1, grad_first, grad_second, turned, far, BF)
    layer_got = swap(layer_send, 1)
    layer_part = layer_grad(0, grad_first, grad_second, turned, far, F32, first=(layer_send,))
    conv_grad, points0, points1, points_far, cpe_low, sums_one = third_rows(
        plan, place_of, layer_part, layer_got, carried, normed_one, scaling_one, normed_cpe, scaling_cpe, small, cpe_weight, firsts
    )
    grad0 = conv_grad
    grad2 = swap(grad0, 2)
    grad1 = swap(grad0, 1)
    cpe_send, cpe_keep = cpe_weights(shard_count, place_of, conv_low, cpe_low)
    cpe_got = swap(cpe_send, 1)
    second_mine, second_theirs = split_sum(weights_mine, weights_far)
    second_steps = scatter_sum(second_mine, second_theirs, shard_count, 0)
    spread0 = spread(0, place_of, lookup, kernel_rows, grad0, first=(cpe_send, weights_far))
    spread1 = spread(1, place_of, lookup, kernel_rows, grad1, first=(spread0,))
    grad3 = swap(after(grad2, spread1), 1)
    third_mine, third_far, triple_sums = third_weights(
        place_of, shard_count, grad_first, grad_second, layer_one, other_one, cpe_keep, cpe_got, first=(spread1,)
    )

    gathered = (gathered0, gathered1, gathered2, gathered3)
    grads = (grad0, grad1, grad2, grad3)
    cuts = 3
    chunk = KERNEL // cuts * width
    conv_sums = []
    waits = [(third_mine, second_steps[0]), (), (second_steps[1],)]
    pieces = []
    for i in range(cuts):
        stage = i % 2
        piece, piece_theirs = conv_weight_grad(
            place_of, gathered, grads, i * chunk, chunk, shard_count, stage, first=(*pieces[-1:], *waits[i])
        )
        pieces.append(piece)
        conv_sums.append(scatter_sum(piece, piece_theirs, shard_count, stage))
    spread2 = spread(2, place_of, lookup, kernel_rows, grad2, first=(pieces[-1],))
    spread3 = spread(3, place_of, lookup, kernel_rows, grad3, first=(spread2, conv_sums[0][0], conv_sums[1][0]))

    third_far = swap(after(third_far, pieces[0]), 2)
    third_mine, third_theirs = split_sum(third_mine, third_far, 1)
    third_sum = scatter_sum(third_mine, after(third_theirs, spread3), shard_count, 1)[-1]
    second_sum = second_steps[-1]

    small_keep, small_send = small_parts(place_of, sums_one, sums_two, sum_hidden_bias, triple_sums)
    small_keep = small_keep + swap(after(small_send, pieces[0]), 1)
    small = small_keep[0] + swap(after(small_keep[1], pieces[1]), 2)
    small = all_sum(small, (pieces[2], spread2, spread3))

    points_far = swap(after(points_far, spread3), 2)
    points_near = swap(after(points1, spread3), 1)
    points_cross = swap(points_far, 1)
    block_near = swap(after(block1, spread3), 1)
    block_cross = swap(after(block_far, spread3), 1)
    grad_padded, to_below, to_above = finish(place_of, (spread0, spread1, spread2, spread3), first=(conv_sums[0][1], conv_sums[2][0]))
    from_above = lax.ppermute(to_below, "pts", downs)
    from_below = lax.ppermute(to_above, "pts", ups)
    grad_points = points_grad(place_of, grad_padded, from_below, from_above, points0, points_near, points_far, points_cross)
    block_out = block_rows(place_of, block0, block_near, block_far, block_cross, first=(spread3,))

    cols = wide // shard_count
    conv_sums = [c[-1].reshape(cols, chunk) for c in conv_sums]
    second_sum = second_sum.reshape(cols, -1)
    third_sum = third_sum.reshape(cols, -1)
    grad_conv = jnp.concatenate(conv_sums, axis=1).T.reshape(KERNEL, width, cols)
    return (
        block_out,
        grad_points,
        grad_conv,
        small[0],
        third_sum[:, 3 * width :].T,
        small[1],
        small[2],
        small[3],
        small[4],
        small[5],
        third_sum[:, : 3 * width].reshape(cols, 3, width),
        small[14:16],
        second_sum[:, 2 * wide :].T,
        small[8],
        small[6],
        small[7],
        second_sum[:, :wide],
        small[10:14].reshape(4 * width),
        second_sum[:, wide : 2 * wide].T,
        small[9],
    )


def solution(mesh):
    return jax.shard_map(
        shards,
        mesh=mesh,
        in_specs=(
            P("pts", "blk"),
            P("pts", None),
            P("pts"),
            P(None, "blk", None),
            P("blk"),
            P("blk", None),
            P("blk"),
            P("blk"),
            P("blk"),
            P("blk"),
            P("blk"),
            P(None, None, "blk"),
            P(None, "blk"),
            P("blk", None),
            P("blk"),
            P("blk"),
            P("blk"),
            P(None, "blk"),
            P("blk"),
            P("blk", None),
            P("blk"),
            P("pts", "blk"),
        ),
        out_specs=(
            P("pts", "blk"),
            P("pts", "blk"),
            P(None, "blk", "pts"),
            P("blk"),
            P("blk", "pts"),
            P("blk"),
            P("blk"),
            P("blk"),
            P("blk"),
            P("blk"),
            P("pts", None, "blk"),
            P(None, "blk"),
            P("blk", "pts"),
            P("blk"),
            P("blk"),
            P("blk"),
            P("pts", "blk"),
            P("blk"),
            P("blk", "pts"),
            P("blk"),
        ),
        check_vma=False,
    )
```

```python
import functools
import math

import jax
import jax.numpy as jnp
from jax import lax
from jax.experimental import pallas as pl
from jax.experimental.pallas import tpu as pltpu
from jax.sharding import PartitionSpec as P

HEAD_DIM = 16
PATCH = 1024
KERNEL = 27
REACH = 256
EPS = 1e-05
LOG2E = math.log2(math.e)
BF = jnp.bfloat16
F32 = jnp.float32
NN = ((1,), (0,))
NT = ((1,), (1,))
TN = ((0,), (0,))
VMEM = pl.BlockSpec(memory_space=pltpu.VMEM)
SMEM = pl.BlockSpec(memory_space=pltpu.SMEM)
HBM = pl.BlockSpec(memory_space=pltpu.HBM)
ANY = pl.BlockSpec(memory_space=pl.ANY)
TILE = 256


def dot(a, b, dims):
    return lax.dot_general(a, b, (dims, ((), ())), preferred_element_type=F32)


def struct(shape, kind):
    return jax.ShapeDtypeStruct(shape, kind)


TIMES = {
    "prepare": 10,  "conv_forward": 7.5, "first_rows": 2.5, "triple_half": 2, "attend_forward": 21, "second_rows": 10,
    "second_send": 1.5, "attend_backward": 19, "second_keep": 2.5, "layer_grad": 1, "third_rows": 2.3, "cpe_weights": 0.1,
    "spread": 7, "third_weights": 0.1, "conv_weight_grad": 0.1, "finish": 1.0, "rows_out": 2.0, "fold": 0.05, "second_out": 0.1, "grads_out": 0.1,
}
FACTOR = 0.3
TINY = 0.1
BLOCK = 4.2


def call(name, kernel, inputs, outputs, scratch=(), mib=8, grid=None, first=(), time=None):
    count, extra = len(inputs), len(first)

    def body(*refs):
        kernel(*refs[:count], *refs[count + extra :])

    options = {} if grid is None else {"grid": grid}
    result = pl.pallas_call(
        body,
        out_shape=[o for o, spec in outputs],
        in_specs=[spec for a, spec in inputs] + [ANY] * extra,
        out_specs=[spec for o, spec in outputs],
        scratch_shapes=list(scratch),
        compiler_params=pltpu.CompilerParams(vmem_limit_bytes=mib * 2**20),
        cost_estimate=pl.CostEstimate(flops=int((time or TIMES[name]) * FACTOR * 1.15e9), bytes_accessed=0, transcendentals=0),
        name=name,
        **options,
    )(*[pltpu.with_memory_space_constraint(a, pltpu.HBM) if spec is HBM else a for a, spec in inputs], *first)
    return result[0] if len(result) == 1 else result


def vm(*arrays):
    return [(a, VMEM) for a in arrays]


def split3(values):
    high = values.astype(BF)
    rest = values - high.astype(F32)
    middle = rest.astype(BF)
    return high, middle, (rest - middle.astype(F32)).astype(BF)


def joined(rows, width):
    rows = rows.astype(F32)
    return (rows[:, :width] + rows[:, width : 2 * width]) + rows[:, 2 * width : 3 * width]


def in_order(pieces, me):
    core, chip = (me & 1) == 1, (me >> 1) == 1
    a, b = jnp.where(core, pieces[1], pieces[0]), jnp.where(core, pieces[0], pieces[1])
    c, d = jnp.where(core, pieces[3], pieces[2]), jnp.where(core, pieces[2], pieces[3])
    return [
        jnp.where(chip, c, a),
        jnp.where(chip, d, b),
        jnp.where(chip, a, c),
        jnp.where(chip, b, d),
    ]


def folded(source, start, target, row, sems, rows):
    part, width = rows // 4, source.shape[1]
    copies = []
    for j in range(4):
        copies.append(
            pltpu.make_async_copy(
                source.at[pl.ds(pl.multiple_of(start + j * part, 16), part), :],
                target.at[row : row + part, j * width : (j + 1) * width],
                sems(),
            )
        )
    return copies


def unfolded(pack, row, at, rows):
    part, width = rows // 4, pack.shape[1] // 4
    return jnp.concatenate(
        [
            pack[row : row + part, j * width : (j + 1) * width]
            for j in range(at.start // part, at.stop // part)
        ],
        axis=0,
    )


class Plan:
    def __init__(self, rows, width):
        fold = rows // 4
        self.first_cpe = 3 * width
        self.first_points = 4 * width
        self.first_small = 4 * width + 2 * fold
        self.first_rows = self.first_small + 16
        self.near_points = width
        self.near_small = width + fold
        self.near_rows = self.near_small + 16


def counter(sems):
    state = [0]

    def take():
        state[0] += 1
        return sems.at[state[0] - 1]

    return take


VECTORS = 10


def prepare_kernel(
    plan, rows, place_of, turned_in, cpe, points, patch, *refs
):
    vectors, refs = refs[:VECTORS], refs[VECTORS:]
    hidden_bias, query_bias, away, near, turned, small, patch_row, terms, lines, long_line, pair, sems = refs
    me = place_of[0]
    width = points.shape[1]
    take = counter(sems)
    copies = [
        pltpu.make_async_copy(cpe, away.at[plan.first_cpe : plan.first_cpe + width, :], take()),
        pltpu.make_async_copy(cpe, near.at[0:width, :], take()),
    ]
    for e in (2, 3):
        copies += folded(points, (me ^ e) * rows, away, plan.first_points + (e - 2) * rows // 4, take, rows)
    copies += folded(points, (me ^ 1) * rows, near, plan.near_points, take, rows)
    for copy in copies:
        copy.start()
    loads = [pltpu.make_async_copy(vector, lines.at[r], take()) for r, vector in enumerate(vectors)]
    loads.append(pltpu.make_async_copy(hidden_bias, long_line, take()))
    loads.append(pltpu.make_async_copy(query_bias, pair, take()))
    for copy in loads:
        copy.start()
    for t in range(3):
        turned[t * width : (t + 1) * width, :] = turned_in[t].T
    for copy in loads:
        copy.wait()
    for r in range(VECTORS):
        small[r : r + 1, :] = lines[r]
    for i in range(4):
        small[VECTORS + i : VECTORS + i + 1, :] = long_line[:, i * width : (i + 1) * width]
    small[VECTORS + 4 :, :] = pair[...]
    high, middle, low = split3(small[...])
    terms[...] = jnp.concatenate([high, middle, low, jnp.zeros_like(low)], axis=1)
    last = [
        pltpu.make_async_copy(turned, away.at[0 : 3 * width, :], take()),
        pltpu.make_async_copy(terms, away.at[plan.first_small :, :], take()),
        pltpu.make_async_copy(terms, near.at[plan.near_small :, :], take()),
    ]
    for copy in last:
        copy.start()
    for e in (0, 1):
        at = pl.ds(pl.multiple_of((me ^ e) * rows, rows), rows)
        patch_row[:, e * rows : (e + 1) * rows] = patch[:, at]
    for copy in copies + last:
        copy.wait()


def prepare(plan, place_of, turned, cpe, points, patch, vectors, hidden_bias, query_bias, first=()):
    row_count, width = points.shape
    wide = cpe.shape[1]
    lines = [v.reshape(1, -1) for v in (*vectors, hidden_bias)]
    return call(
        "prepare",
        functools.partial(prepare_kernel, plan, row_count // 4),
        [(place_of, SMEM), (turned, VMEM), (cpe, HBM), (points, HBM), (patch.reshape(1, -1), VMEM)]
        + [(v, HBM) for v in (*lines, query_bias)],
        [
            (struct((plan.first_rows, wide), BF), HBM),
            (struct((plan.near_rows, wide), BF), HBM),
            (struct((3 * width, wide), BF), VMEM),
            (struct((16, width), F32), VMEM),
            (struct((1, row_count // 2), jnp.int32), VMEM),
        ],
        [
            pltpu.VMEM((16, wide), BF),
            pltpu.VMEM((VECTORS, 1, width), F32),
            pltpu.VMEM((1, 4 * width), F32),
            pltpu.VMEM((2, width), F32),
            pltpu.SemaphoreType.DMA((17 + VECTORS + 2,)),
        ],
        first=first,
    )


def one_hot(place):
    spots = lax.broadcasted_iota(jnp.int32, (256, 256), 0)
    return jnp.where(spots == jnp.broadcast_to(place, (256, 256)), 1.0, 0.0).astype(BF)


def conv_kernel(e, packs, place_of, low, points, high, lookup, weight, *refs):
    sources, refs = refs[:packs], refs[packs:]
    conv, conv_after, gathered = refs[:3]
    away, near = refs[3:5] if packs else (None, None)
    turned, picked, sems = refs[-3:]
    me = place_of[0]
    width = points.shape[1]
    rows = picked.shape[1]
    quarter = me ^ e
    take = counter(sems)
    copies = []
    if packs:
        hidden, output, proj, upstream = sources
        wide, fold = hidden.shape[1], rows // 4
        half, start = wide // 2, wide + width + wide // 2
        for target in (away, near):
            copies.append(pltpu.make_async_copy(output, target.at[0:wide, :], take()))
            copies.append(pltpu.make_async_copy(proj, target.at[wide : wide + width, :], take()))
            copies.append(pltpu.make_async_copy(hidden.at[half:, :], target.at[wide + width : start, :], take()))
        copies.append(pltpu.make_async_copy(hidden.at[:half, :], near.at[start : start + half, :], take()))
        copies += folded(upstream, (me ^ 2) * rows, away, start, take, rows)
        copies += folded(upstream, (me ^ 3) * rows, away, start + fold, take, rows)
        copies += folded(upstream, (me ^ 1) * rows, near, start + half, take, rows)
        for copy in copies:
            copy.start()
    base = place_of[1] * points.shape[0] + quarter * rows - REACH
    last = points.shape[0] // 256 - 1
    for j in range(rows // 256 + 2):
        spot = quarter * (rows // 256) - 1 + j
        at = pl.multiple_of(jnp.clip(spot, 0, last) * 256, 256)
        piece = points[pl.ds(at, 256), :]
        piece = jnp.where(spot < 0, low[...], jnp.where(spot > last, high[...], piece))
        turned[j * width : (j + 1) * width, :] = piece.T
    step = KERNEL // 3
    for b in range(rows // 256):
        cols = slice(b * 256, (b + 1) * 256)
        left = turned[b * width : (b + 3) * width, :]
        for k in range(KERNEL):
            spot = lookup[k : k + 1, pl.ds(pl.multiple_of(quarter * rows + b * 256, 256), 256)] - base
            part = jnp.broadcast_to(lax.shift_right_logical(spot, 8) - b, (width, 256))
            three = dot(left, one_hot(jnp.bitwise_and(spot, 255)), NN)
            values = jnp.where(
                part == 0,
                three[:width],
                jnp.where(part == 1, three[width : 2 * width], three[2 * width :]),
            )
            picked[k * width : (k + 1) * width, cols] = values.astype(BF)
            if k % step == step - 1:
                at = slice((k + 1 - step) * width, (k + 1) * width)
                copies.append(pltpu.make_async_copy(picked.at[at, cols], gathered.at[at, cols], take()))
                copies[-1].start()
        (conv, conv_after)[b][...] = dot(picked[:, cols], weight[...], TN).astype(conv.dtype)
    for copy in copies:
        copy.wait()


def conv_forward(e, place_of, low, points, high, lookup, weight, kind, packs=(), first=(), time=None):
    rows, width, wide = points.shape[0] // 4, points.shape[1], weight.shape[1]
    outputs = [(struct((rows // 2, wide), kind), VMEM)] * 2 + [(struct((KERNEL * width, rows), BF), HBM)]
    if packs:
        size = wide + width + wide // 2 + rows // 4
        outputs += [(struct((size + rows // 4, wide), BF), HBM), (struct((size + wide // 2, wide), BF), HBM)]
    return call(
        "conv_forward",
        functools.partial(conv_kernel, e, len(packs)),
        [(place_of, SMEM)] + vm(low, points, high, lookup, weight) + [(p, HBM) for p in packs],
        outputs,
        [
            pltpu.VMEM(((rows // 256 + 2) * width, 256), BF),
            pltpu.VMEM((KERNEL * width, rows), BF),
            pltpu.SemaphoreType.DMA((6 * rows // 512 + (19 if packs else 0),)),
        ],
        first=first,
        time=time,
    )


def spread_kernel(e, blocks, place_of, lookup, weight, grads, out, upstream):
    width = out.shape[0]
    rows = grads.shape[0]
    quarter = place_of[0] ^ e
    base = place_of[1] * lookup.shape[1] + quarter * rows - REACH
    out[...] = jnp.zeros(out.shape, F32)
    step = 9
    for n, b in enumerate(blocks):
        cols = slice(b * 256, (b + 1) * 256)
        upstream[...] = dot(weight[...], grads[cols, :], NT)
        for s in range(KERNEL // step):
            left, right = [], []
            for k in range(s * step, (s + 1) * step):
                spot = lookup[k : k + 1, pl.ds(pl.multiple_of(quarter * rows + b * 256, 256), 256)] - base
                part = jnp.broadcast_to(lax.shift_right_logical(spot, 8) - b, (width, 256))
                mine = upstream[k * width : (k + 1) * width, :]
                left.append(
                    jnp.concatenate(
                        [jnp.where(part == i, mine, 0.0).astype(BF) for i in range(3)], axis=0
                    )
                )
                right.append(one_hot(jnp.bitwise_and(spot, 255)))
            three = dot(jnp.concatenate(left, axis=1), jnp.concatenate(right, axis=1), NT)
            for i in range(3):
                at = slice((n + i) * 256, (n + i + 1) * 256)
                out[:, at] = out[:, at] + three[i * width : (i + 1) * width]


def spread(e, blocks, place_of, lookup, weight, grads, first=(), time=None):
    width = weight.shape[0] // KERNEL
    return call(
        "spread",
        functools.partial(spread_kernel, e, blocks),
        [(place_of, SMEM)] + vm(lookup, weight, grads),
        [(struct((width, 256 * len(blocks) + 2 * REACH), F32), VMEM)],
        [pltpu.VMEM((KERNEL * width, 256), F32)],
        first=first,
        time=time,
    )


def halves(count, stage):
    keep = [r for r in range(count) if not (r >> stage) & 1]
    return keep, [r ^ (1 << stage) for r in keep]


def conv_weight_kernel(blocks, stage, start, count, extra, place_of, *refs):
    gathered, grads, refs = refs[:4], refs[4:8], refs[8:]
    thirds, (mine, theirs, total) = refs[:extra], refs[extra:]
    tile = 384
    for i in range(count // tile):
        rows = slice(start + i * tile, start + (i + 1) * tile)
        cols = slice(i * tile, (i + 1) * tile)
        total[:, cols] = sum(dot(a[rows, :], g[...], NN) for a, g in zip(gathered, grads)).T.astype(BF)
    size = total.shape[0] // blocks
    for out, slots in zip((mine, theirs), halves(blocks, stage)):
        for i, r in enumerate(slots):
            at = pl.multiple_of((place_of[1] ^ r) * size, size)
            out[i, :, 0:count] = total[pl.ds(at, size), :]
            if extra:
                out[i, :, count:] = (thirds[0][r].astype(F32) + thirds[1][r].astype(F32)).astype(BF)


def conv_weight_grad(place_of, gathered, grads, start, count, blocks, stage, thirds=(), first=()):
    wide = grads[0].shape[1]
    cols = count + (thirds[0].shape[2] if thirds else 0)
    half = struct((blocks // 2, wide // blocks, cols), BF)
    return call(
        "conv_weight_grad",
        functools.partial(conv_weight_kernel, blocks, stage, start, count, len(thirds)),
        [(place_of, SMEM)] + vm(*gathered, *grads, *thirds),
        vm(half, half),
        [pltpu.VMEM((wide, count), BF)],
        first=first,
    )


def finish_kernel(place_of, s0, s1, s2, s2_after, s3, s3_after, out, low, high):
    me = place_of[0]
    rows = s0.shape[1] - 2 * REACH
    ends = [s[:, 0:256] for s in (s0, s1, s2, s3)], [s[:, 768:] for s in (s0, s1)] + [s[:, 512:] for s in (s2_after, s3_after)]
    inner = [
        [s[:, 256:512] for s in (s0, s1)]
        + [a[:, 256:512] + b[:, 0:256] for a, b in ((s2, s2_after), (s3, s3_after))],
        [s[:, 512:768] for s in (s0, s1)]
        + [a[:, 512:768] + b[:, 256:512] for a, b in ((s2, s2_after), (s3, s3_after))],
    ]
    parts = [in_order(p, me) for p in (ends[0], inner[0], inner[1], ends[1])]
    out[...] = jnp.zeros(out.shape, F32)
    for q in range(4):
        for i, part in enumerate(parts):
            at = slice(q * rows + i * 256, q * rows + (i + 1) * 256)
            out[:, at] = out[:, at] + part[q]
    low[...] = out[:, :REACH].astype(BF)
    high[...] = out[:, out.shape[1] - REACH :].astype(BF)


def finish(place_of, spreads, first=()):
    width, span = spreads[0].shape
    total = 4 * (span - 2 * REACH) + 2 * REACH
    return call(
        "finish",
        finish_kernel,
        [(place_of, SMEM)] + vm(*spreads),
        [(struct((width, total), F32), VMEM)] + [(struct((width, REACH), BF), VMEM)] * 2,
        first=first,
    )


def rows_out_kernel(place_of, inside, below, above, block, own, near, far, cross, block_out, out):
    rows, width = own.shape
    me = place_of[0]
    pieces = in_order([block[...], near[:, :width], far[:, :width], cross[:, width : 2 * width]], me)
    for q in range(4):
        block_out[q * rows : (q + 1) * rows, :] = pieces[q]
    pieces = [own[...], near[:, width:], far[:, 2 * width : 3 * width], cross[:, 3 * width :]]
    pieces = in_order(pieces, me)
    for q in range(4):
        total = inside[:, REACH + q * rows : REACH + (q + 1) * rows].T + pieces[q].astype(F32)
        out[q * rows : (q + 1) * rows, :] = total
    out[:REACH, :] = out[:REACH, :] + below[...].astype(F32).T
    last = out.shape[0] - REACH
    out[last:, :] = out[last:, :] + above[...].astype(F32).T


def rows_out(place_of, inside, below, above, block, own, near, far, cross, first=()):
    rows, width = own.shape
    return call(
        "rows_out",
        rows_out_kernel,
        [(place_of, SMEM)] + vm(inside, below, above, block, own, near, far, cross),
        vm(struct((4 * rows, width), BF), struct((4 * rows, width), F32)),
        first=first,
    )


def three_rows(high, middle, low):
    spots = lax.broadcasted_iota(jnp.int32, (16, high.shape[1]), 0)
    picked = jnp.where(
        spots == 0,
        high.astype(F32),
        jnp.where(spots == 1, middle.astype(F32), jnp.where(spots == 2, low.astype(F32), 0.0)),
    )
    return picked.astype(BF)


def one_rows(length, count):
    spots = lax.broadcasted_iota(jnp.int32, (16, length), 0)
    return jnp.where(spots < count, 1.0, 0.0).astype(BF)


def patch_codes(patch):
    shape = (32, patch.shape[1])
    spots = lax.broadcasted_iota(jnp.int32, shape, 0)
    bits = jnp.bitwise_and(
        lax.shift_right_logical(jnp.broadcast_to(patch, shape), jnp.bitwise_and(spots, 15)), 1
    )
    bits = jnp.where(spots < 16, bits, 1 - bits)
    return jnp.where(bits == 1, 1.0, 0.0).astype(BF), jnp.where(bits == 1, 0.0, -1e30).astype(BF)


def fixed_rows(patch, query_side, key_side):
    length = patch.shape[1]
    left, right = patch_codes(patch)
    key_side[48:64, :] = one_rows(length, 3)
    key_side[64:96, :] = left
    query_side[64:96, :] = right
    key_side[96:128, :] = jnp.zeros((32, length), BF)
    query_side[96:128, :] = jnp.zeros((32, length), BF)


def column(row):
    return jnp.broadcast_to(row, (128, 128)).T[:, 0:1]


def triple_rows(values, weights, smalls, out, cols):
    width = out.shape[1] // 2
    for t in range(3):
        for i in range(2):
            piece = dot(weights[i][t * width : (t + 1) * width, :], values, NT)
            if t != 1:
                piece = piece + column(smalls[i][14 + t // 2 : 15 + t // 2, :])
            out[t, i * width : (i + 1) * width, cols] = piece.astype(BF)


def triple_half_kernel(plan, values, turned, away, small, out):
    smalls = (small[...], joined(away[plan.first_small :, :], small.shape[1]))
    triple_rows(values[...], (turned, away), smalls, out, slice(0, values.shape[0]))


def triple_half(plan, values, turned, away, small):
    return call(
        "triple_half",
        functools.partial(triple_half_kernel, plan),
        vm(values, turned, away, small),
        [(struct((3, 2 * small.shape[1], values.shape[0]), BF), VMEM)],
    )


def attend_forward_kernel(
    plan, heads, tile, mine, other, turned, away, small, patch, triple, total, keep, send, logs, query_side, key_side, value_side
):
    rows = mine.shape[2]
    length = 2 * rows
    for t in range(3):
        triple[t, :, :rows] = mine[t]
    smalls = (small[...], joined(away[plan.first_small :, :], small.shape[1]))
    triple_rows(other[...], (turned, away), smalls, triple, slice(rows, length))
    fixed_rows(patch[...], query_side, key_side)
    value_side[16:32, :] = one_rows(length, 1)

    @pl.loop(0, heads)
    def _(h):
        at = pl.ds(pl.multiple_of(h * HEAD_DIM, HEAD_DIM), HEAD_DIM)
        query = triple[0, at, :].astype(F32) * (HEAD_DIM**-0.5 * LOG2E)
        key = triple[1, at, :]
        high, middle, low = split3(query)
        query_side[0:16, :] = high
        query_side[16:32, :] = middle
        query_side[32:48, :] = low
        query_side[48:64, :] = jnp.zeros((16, length), BF)
        key_side[0:16, :] = key
        key_side[16:32, :] = key
        key_side[32:48, :] = key
        value_side[0:16, :] = triple[2, at, :]
        wide_key = key.astype(F32)
        bound = jnp.max(jnp.sum(query * query, axis=0)) * jnp.max(
            jnp.sum(wide_key * wide_key, axis=0)
        )
        logs[pl.ds(h, 1), :] = jnp.zeros((1, length), F32)

        @pl.when(jnp.logical_not(bound < 4096.0))
        def _():
            for t in range(length // tile):
                cols = slice(t * tile, (t + 1) * tile)
                top = jnp.max(dot(key_side[...], query_side[:, cols], TN), axis=0, keepdims=True)
                query_side[48:64, cols] = three_rows(*split3(-top))
                logs[pl.ds(h, 1), cols] = top

        for t in range(length // tile):
            cols = slice(t * tile, (t + 1) * tile)
            weights = jnp.exp2(dot(key_side[...], query_side[:, cols], TN)).astype(BF)
            mixed = dot(value_side[...], weights, NN)
            sums = mixed[16:17, :]
            mixed = mixed[0:16, :] * (1.0 / sums)
            total[at, cols] = mixed
            if t * tile < rows:
                keep[at, cols] = mixed.astype(BF)
            else:
                send[at, t * tile - rows : (t + 1) * tile - rows] = mixed.astype(BF)
            logs[pl.ds(h, 1), cols] = logs[pl.ds(h, 1), cols] + jnp.log2(sums)


def attend_forward(plan, mine, other, turned, away, small, patch, first=()):
    width, rows = mine.shape[1:]
    length = 2 * rows
    heads = width // HEAD_DIM
    return call(
        "attend_forward",
        functools.partial(attend_forward_kernel, plan, heads, 512),
        vm(mine, other, turned, away, small, patch),
        [
            (struct((3, width, length), BF), VMEM),
            (struct((width, length), F32), VMEM),
            (struct((width, rows), BF), VMEM),
            (struct((width, rows), BF), VMEM),
            (struct((heads, length), F32), VMEM),
        ],
        [
            pltpu.VMEM((128, length), BF),
            pltpu.VMEM((128, length), BF),
            pltpu.VMEM((32, length), BF),
        ],
        first=first,
    )


def attend_backward_kernel(
    first, heads, tile, triple, patch, mine, other, mixed, logs, out, query_side, key_side, value_side, grad_side, grad_value, grad_key
):
    length = triple.shape[2]
    fixed_rows(patch[...], query_side, key_side)
    value_side[16:32, :] = one_rows(length, 3)

    @pl.loop(0, heads)
    def _(h):
        at = pl.ds(pl.multiple_of((h + first) * HEAD_DIM, HEAD_DIM), HEAD_DIM)
        to = pl.ds(pl.multiple_of(h * HEAD_DIM, HEAD_DIM), HEAD_DIM)
        query, key = triple[0, at, :], triple[1, at, :]
        upstream = jnp.concatenate([mine[at, :], other[at, :]], axis=1)
        high, middle, low = split3(query.astype(F32) * (HEAD_DIM**-0.5 * LOG2E))
        query_side[0:16, :] = high
        query_side[16:32, :] = middle
        query_side[32:48, :] = low
        query_side[48:64, :] = three_rows(*split3(-logs[pl.ds(h + first, 1), :]))
        key_side[0:16, :] = key
        key_side[16:32, :] = key
        key_side[32:48, :] = key
        value_side[0:16, :] = triple[2, at, :]
        inner = jnp.sum(upstream.astype(F32) * mixed[at, :], axis=0, keepdims=True)
        grad_side[0:16, :] = upstream
        grad_side[16:32, :] = three_rows(*split3(-inner))
        for t in range(length // tile):
            cols = slice(t * tile, (t + 1) * tile)
            prob = jnp.exp2(dot(query_side[:, cols], key_side[...], TN))
            grad_prob = dot(grad_side[:, cols], value_side[...], TN)
            grad_score = (prob * grad_prob).astype(BF)
            value_part = dot(upstream[:, cols], prob.astype(BF), NN)
            key_part = dot(query[:, cols], grad_score, NN)
            out[0, to, cols] = (dot(key, grad_score, NT) * HEAD_DIM**-0.5).astype(BF)
            if t == 0:
                grad_value[...] = value_part
                grad_key[...] = key_part
            else:
                grad_value[...] += value_part
                grad_key[...] += key_part
        out[1, to, :] = (grad_key[...] * HEAD_DIM**-0.5).astype(BF)
        out[2, to, :] = grad_value[...].astype(BF)


def attend_backward(first_head, heads, triple, patch, mine, other, mixed, logs, first=()):
    length = triple.shape[2]
    return call(
        "attend_backward",
        functools.partial(attend_backward_kernel, first_head, heads, 512),
        vm(triple, patch, mine, other, mixed, logs),
        [(struct((3, heads * HEAD_DIM, length), BF), VMEM)],
        [
            pltpu.VMEM((128, length), BF),
            pltpu.VMEM((128, length), BF),
            pltpu.VMEM((32, length), BF),
            pltpu.VMEM((32, length), BF),
            pltpu.VMEM((16, length), F32),
            pltpu.VMEM((16, length), F32),
        ],
        mib=12,
        first=first,
    )


def norm_rows(values):
    average = jnp.mean(values, axis=1, keepdims=True)
    scaling = lax.rsqrt(
        jnp.mean(values * values, axis=1, keepdims=True) - average * average + EPS
    )
    return (values - average) * scaling, scaling


def norm_rows_back(upstream, normed, scaling, gain):
    scaled = upstream * gain
    return scaling * (
        scaled
        - jnp.mean(scaled, axis=1, keepdims=True)
        - normed * jnp.mean(scaled * normed, axis=1, keepdims=True)
    )


def cut(values):
    width = values.shape[1] // 4
    return [values[:, j * width : (j + 1) * width] for j in range(4)]


def add_rows(ref, row, values, first):
    total = jnp.sum(values, axis=0, keepdims=True)
    ref[row : row + 1, :] = total if first else ref[row : row + 1, :] + total


def small_vectors(plan, small, near, far, cross):
    width = small.shape[1]
    return [
        small[...],
        joined(near[plan.near_small :, :], width),
        joined(far[plan.first_small :, :], width),
        joined(cross[plan.first_small :, :], width),
    ]


def vectors(smalls, me):
    return jnp.concatenate(in_order(smalls, me), axis=1)


def cpe_rows(plan, weight, near, far, cross, me):
    width = weight.shape[0]
    at = slice(plan.first_cpe, plan.first_cpe + width)
    pieces = [weight[...], near[:width, :], far[at, :], cross[at, :]]
    return jnp.concatenate(in_order(pieces, me), axis=0)


def own_rows(ref, me, rows, at):
    return ref[pl.ds(pl.multiple_of(me * rows + at.start, at.stop - at.start), at.stop - at.start), :]


def first_rows_kernel(
    plan, place_of, part_low, part_high, close_low, close_high, away, points, small, weight, near, far, cross,
    layer, middle, normed_cpe, scaling_cpe, residual, normed, scaling,
):
    me = place_of[0]
    rows = 2 * part_low.shape[0]
    vec = vectors(small_vectors(plan, small, near, far, cross), me)
    vec = [vec[r : r + 1, :] for r in range(6)]
    weights = cpe_rows(plan, weight, near, far, cross, me)
    for t in range(rows // TILE):
        at = slice(t * TILE, (t + 1) * TILE)
        part, close = ((part_low, close_low), (part_high, close_high))[t * TILE * 2 // rows]
        low = (part[...] + close[...].astype(F32) + away[at, :].astype(F32) + vec[0]).astype(BF)
        middle[at, :] = low
        xhat, rate = norm_rows(dot(low, weights, NN) + vec[1])
        normed_cpe[at, :] = xhat
        scaling_cpe[at, :] = rate
        features = [
            own_rows(points, me, rows, at),
            unfolded(near, plan.near_points, at, rows),
            unfolded(far, plan.first_points, at, rows),
            unfolded(cross, plan.first_points + rows // 4, at, rows),
        ]
        features = jnp.concatenate(in_order(features, me), axis=1)
        sums = features.astype(F32) + xhat * vec[2] + vec[3]
        residual[at, :] = sums
        xhat, rate = norm_rows(sums)
        normed[at, :] = xhat
        scaling[at, :] = rate
        layer[at, :] = (xhat * vec[4] + vec[5]).astype(BF)


def first_rows(plan, place_of, parts, closes, away, points, small, weight, near, far, cross):
    rows, wide = away.shape
    full, thin, lower = struct((rows, wide), F32), struct((rows, 1), F32), struct((rows, wide), BF)
    return call(
        "first_rows",
        functools.partial(first_rows_kernel, plan),
        [(place_of, SMEM)] + vm(*parts, *closes, away, points, small, weight, near, far, cross),
        vm(lower, lower, full, thin, full, full, thin),
    )


def gelu_parts(u):
    scale = math.sqrt(2 / math.pi)
    square = u * u
    bent = jnp.tanh(u * (scale + (scale * 0.044715) * square))
    half = 0.5 + 0.5 * bent
    slope = half + u * (1.0 - bent * bent) * (0.5 * scale + (1.5 * 0.044715 * scale) * square)
    return u * half, slope


def second_rows_kernel(
    plan, place_of, keep, got, residual, out_grad, hidden, output, proj, small, near, far, cross, near2, far2, cross2,
    hidden_far, hidden_cross, block0, block1, block_far, active, before, layer, upstream, carried, low, grad_keep, grad_send, hidden_sums, sums,
):
    me = place_of[0]
    rows, wide = residual.shape
    smalls = small_vectors(plan, small, near, far, cross)
    vec = vectors(smalls, me)
    vec = {r: vec[r : r + 1, :] for r in (6, 7, 8, 9)}
    biases = [jnp.concatenate([s[10 + i : 11 + i, :] for i in range(4)], axis=1) for s in smalls]
    width = keep.shape[0] // 2
    packs = (near2, far2, cross2)
    end = wide + width
    half = wide // 2
    lower_halves = [hidden[:half, :], near2[end + half : end + wide, :], hidden_far[...], hidden_cross[...]]
    upper_halves = [hidden[half:, :]] + [p[end : end + half, :] for p in packs]
    hiddens = [jnp.concatenate(pair, axis=0) for pair in zip(lower_halves, upper_halves)]
    outputs = [output] + [p.at[0:wide, :] for p in packs]
    projs = [proj[...]] + [p[wide:end, :] for p in packs]
    mine = jnp.concatenate([projs[0], projs[2]], axis=0)
    others = jnp.concatenate([projs[1], projs[3]], axis=0)
    for t in range(rows // TILE):
        at = slice(t * TILE, (t + 1) * TILE)
        base = residual[at, :] + vec[6] + dot(keep[:, at], mine, TN) + dot(got[:, at], others, TN)
        normed, scaling = norm_rows(base)
        lower = (normed * vec[7] + vec[8]).astype(BF)
        layer[at, :] = lower
        grads = [
            own_rows(out_grad, me, rows, at),
            unfolded(near2, end + wide, at, rows),
            unfolded(far2, end + half, at, rows),
            unfolded(cross2, end + half + rows // 4, at, rows),
        ]
        grads = jnp.concatenate(in_order(grads, me), axis=1)
        upstream[at, :] = grads
        result = base + vec[9]
        grad_layer = None
        for e in range(4):
            act, slope = gelu_parts(dot(lower, hiddens[e], NN) + biases[e])
            act = act.astype(BF)
            active[e, at, :] = act
            result = result + dot(act, outputs[e][...], NN)
            pre = dot(grads, outputs[e][...], NT) * slope
            add_rows(hidden_sums, e, pre, t == 0)
            pre = pre.astype(BF)
            before[e, at, :] = pre
            piece = dot(pre, hiddens[e], NT)
            grad_layer = piece if e == 0 else grad_layer + piece
        result = in_order(cut(result.astype(BF)), me)
        block0[at, :] = result[0]
        block1[at, :] = result[1]
        block_far[at, 0:width] = result[2]
        block_far[at, width:] = result[3]
        wide_grads = grads.astype(F32)
        add_rows(sums, 0, grad_layer * normed, t == 0)
        add_rows(sums, 1, grad_layer, t == 0)
        add_rows(sums, 3, wide_grads, t == 0)
        carry = wide_grads + norm_rows_back(grad_layer, normed, scaling, vec[7])
        carried[at, :] = carry
        add_rows(sums, 2, carry, t == 0)
        carry = carry.astype(BF)
        low[at, :] = carry
        grad_keep[:, at] = dot(mine, carry, NT).astype(BF)
        grad_send[:, at] = dot(others, carry, NT).astype(BF)


def second_rows(plan, place_of, keep, got, residual, out_grad, weights, small, firsts, seconds):
    rows, wide = residual.shape
    lower, piece = struct((rows, wide), BF), struct((rows, wide // 4), BF)
    heads = struct(keep.shape, BF)
    return call(
        "second_rows",
        functools.partial(second_rows_kernel, plan),
        [(place_of, SMEM)] + vm(keep, got, residual, out_grad, *weights, small, *firsts, *seconds),
        vm(
            piece,
            piece,
            struct((rows, wide // 2), BF),
            struct((4, rows, wide), BF),
            struct((4, rows, wide), BF),
            lower,
            lower,
            struct((rows, wide), F32),
            lower,
            heads,
            heads,
            struct((4, wide), F32),
            struct((4, wide), F32),
        ),
        mib=12,
    )


def cut_rows(store, spot, cols, value, blocks):
    size = value.shape[0] // blocks
    for p in range(blocks):
        store(p ^ spot, cols, value[p * size : (p + 1) * size])


def second_weight_parts(i, e, blocks, spot, upstream, active, before, layer, low, attended, store):
    wide = layer.shape[1]
    width = attended.shape[0] // 2
    cut_rows(store, spot, slice(0, wide), dot(layer[...], before[e], TN), blocks)
    cut_rows(store, spot, slice(wide, 2 * wide), dot(upstream[...], active[e], TN), blocks)
    part = dot(attended[i * width : (i + 1) * width, :], low[...], NN)
    cut_rows(store, spot, slice(2 * wide, 2 * wide + width), part.T, blocks)


def second_send_kernel(blocks, place_of, upstream, active, before, layer, low, attended, out):
    for i, e in enumerate((1, 3)):

        def store(p, cols, value):
            out[i, p, :, cols] = value.astype(BF)

        second_weight_parts(i, e, blocks, place_of[1], upstream, active, before, layer, low, attended, store)


def second_send(place_of, blocks, upstream, active, before, layer, low, attended):
    wide = layer.shape[1]
    return call(
        "second_send",
        functools.partial(second_send_kernel, blocks),
        [(place_of, SMEM)] + vm(upstream, active, before, layer, low, attended),
        [(struct((2, blocks, wide // blocks, 2 * wide + attended.shape[0] // 2), BF), VMEM)],
    )


def second_keep_kernel(blocks, place_of, upstream, active, before, layer, low, attended, got, mine, far):
    for i, out in enumerate((mine, far)):

        def store(p, cols, value):
            out[p, :, cols] = (value + got[i, p, :, cols].astype(F32)).astype(BF)

        second_weight_parts(i, 2 * i, blocks, place_of[1], upstream, active, before, layer, low, attended, store)


def second_keep(place_of, blocks, upstream, active, before, layer, low, attended, got, first=()):
    out = struct(got.shape[1:], BF)
    return call(
        "second_keep",
        functools.partial(second_keep_kernel, blocks),
        [(place_of, SMEM)] + vm(upstream, active, before, layer, low, attended, got),
        vm(out, out),
        first=first,
    )


def third_weights_kernel(
    blocks, place_of, first_half, second_half, mine, other, cpe_keep, cpe_got, small_keep, small_got, own, far
):
    rows = mine.shape[0]
    width = first_half.shape[1]
    empty = jnp.zeros((own.shape[1] - 16, width), BF)
    for i, (grads, out) in enumerate(((first_half, own), (second_half, far))):

        def store(p, cols, value):
            out[p, :, cols] = value.astype(BF)

        for t in range(3):
            part = dot(grads[t, :, :rows], mine[...], NN) + dot(grads[t, :, rows:], other[...], NN)
            cut_rows(store, place_of[1], slice(t * width, (t + 1) * width), part.T, blocks)
        sums = [jnp.sum(grads[t].astype(F32).T, axis=0, keepdims=True) for t in (0, 2)]
        small = small_keep[i] + small_got[i] + jnp.concatenate([jnp.zeros((14, width), F32)] + sums, axis=0)
        for p in range(blocks):
            out[p, :, 3 * width : 4 * width] = (
                cpe_keep[i, p].astype(F32) + cpe_got[i, p].astype(F32)
            ).astype(BF)
            out[p, 0:16, 4 * width :] = small.astype(BF)
            if empty.shape[0]:
                out[p, 16:, 4 * width :] = empty


def third_weights(place_of, blocks, first_half, second_half, mine, other, cpe_keep, cpe_got, small_keep, small_got, first=()):
    wide = mine.shape[1]
    width = first_half.shape[1]
    out = struct((blocks, wide // blocks, 5 * width), BF)
    return call(
        "third_weights",
        functools.partial(third_weights_kernel, blocks),
        [(place_of, SMEM)] + vm(first_half, second_half, mine, other, cpe_keep, cpe_got, small_keep, small_got),
        vm(out, out),
        first=first,
    )


def layer_grad_kernel(half, first_half, second_half, turned, away, out):
    width = first_half.shape[1]
    rows = first_half.shape[2] // 2
    cols = slice(half * rows, (half + 1) * rows)
    total = None
    for t in range(3):
        at = slice(t * width, (t + 1) * width)
        for grads, weight in ((first_half, turned), (second_half, away)):
            piece = dot(grads[t, :, cols], weight[at, :], TN)
            total = piece if total is None else total + piece
    out[...] = total.astype(out.dtype)


def layer_grad(half, first_half, second_half, turned, away, kind, first=()):
    return call(
        "layer_grad",
        functools.partial(layer_grad_kernel, half),
        vm(first_half, second_half, turned, away),
        [(struct((first_half.shape[2] // 2, turned.shape[1]), kind), VMEM)],
        first=first,
    )


def third_rows_kernel(
    plan, place_of, part, close, carried, normed, scaling, normed_cpe, scaling_cpe, small, weight, near, far, cross, block1, block_far,
    conv_grad, points0, near_rows, far_rows, low, sums,
):
    me = place_of[0]
    vec = vectors(small_vectors(plan, small, near, far, cross), me)
    weights = cpe_rows(plan, weight, near, far, cross, me)
    width = points0.shape[1]
    for t in range(part.shape[0] // TILE):
        at = slice(t * TILE, (t + 1) * TILE)
        upstream = part[at, :] + close[at, :].astype(F32)
        xhat = normed[at, :]
        add_rows(sums, 4, upstream * xhat, t == 0)
        add_rows(sums, 5, upstream, t == 0)
        grads = carried[at, :] + norm_rows_back(upstream, xhat, scaling[at, :], vec[4:5, :])
        pieces = in_order(cut(grads.astype(BF)), me)
        points0[at, :] = pieces[0]
        near_rows[at, 0:width] = block1[at, :]
        near_rows[at, width:] = pieces[1]
        far_rows[at, 0 : 2 * width] = block_far[at, :]
        far_rows[at, 2 * width : 3 * width] = pieces[2]
        far_rows[at, 3 * width :] = pieces[3]
        xhat = normed_cpe[at, :]
        add_rows(sums, 2, grads * xhat, t == 0)
        add_rows(sums, 3, grads, t == 0)
        grads = norm_rows_back(grads, xhat, scaling_cpe[at, :], vec[2:3, :])
        add_rows(sums, 1, grads, t == 0)
        lower = grads.astype(BF)
        low[at, :] = lower
        result = dot(lower, weights, NT)
        add_rows(sums, 0, result, t == 0)
        conv_grad[at, :] = result.astype(BF)


def third_rows(plan, place_of, part, close, carried, normed, scaling, normed_cpe, scaling_cpe, small, weight, firsts, blocks):
    rows, wide = part.shape
    lower, piece = struct((rows, wide), BF), struct((rows, wide // 4), BF)
    return call(
        "third_rows",
        functools.partial(third_rows_kernel, plan),
        [(place_of, SMEM)]
        + vm(part, close, carried, normed, scaling, normed_cpe, scaling_cpe, small, weight, *firsts, *blocks),
        vm(lower, piece, struct((rows, wide // 2), BF), lower, lower, struct((6, wide), F32)),
    )


def cpe_weights_kernel(
    blocks, place_of, middle, low, sums_one, sums_two, hidden_sums, send, keep, small_send, small_keep
):
    me = place_of[0]
    width = middle.shape[1] // 4
    ones, twos = in_order(cut(sums_one[...]), me), in_order(cut(sums_two[...]), me)
    for e in range(4):
        out = (keep, send, keep, send)[e]

        def store(p, cols, value):
            out[e // 2, p, :, cols] = value.astype(BF)

        at = pl.ds(pl.multiple_of((e ^ me) * width, width), width)
        cut_rows(store, place_of[1], slice(0, width), dot(low[...], middle[:, at], TN), blocks)
        out = (small_keep, small_send, small_keep, small_send)[e]
        out[e // 2, 0:6, :] = ones[e]
        out[e // 2, 6:10, :] = twos[e]
        for i in range(4):
            out[e // 2, 10 + i : 11 + i, :] = hidden_sums[e : e + 1, i * width : (i + 1) * width]
        out[e // 2, 14:16, :] = jnp.zeros((2, width), F32)


def cpe_weights(blocks, place_of, middle, low, sums_one, sums_two, hidden_sums, first=()):
    wide = middle.shape[1]
    out = struct((2, blocks, wide // blocks, wide // 4), BF)
    small = struct((2, 16, wide // 4), F32)
    return call(
        "cpe_weights",
        functools.partial(cpe_weights_kernel, blocks),
        [(place_of, SMEM)] + vm(middle, low, sums_one, sums_two, hidden_sums),
        vm(out, out, small, small),
        first=first,
    )


def fold_kernel(keep, send, mine, got, kept, sent):
    for out, slots in ((sent, send), (kept, keep)):
        for i, j in enumerate(slots):
            out[i] = (mine[j].astype(F32) + got[j].astype(F32)).astype(BF)


def fold(mine, got, keep, send, first=()):
    out = struct((len(keep), *mine.shape[1:]), BF)
    return call("fold", functools.partial(fold_kernel, keep, send), vm(mine, got), vm(out, out), first=first)


def second_out_kernel(mine, got, hidden, output, proj):
    total = mine[0].astype(F32) + got[0].astype(F32)
    wide = hidden.shape[1]
    hidden[...] = total[:, :wide]
    output[...] = total[:, wide : 2 * wide]
    proj[...] = total[:, 2 * wide :]


def second_out(mine, got, wide):
    size, cols = mine.shape[1:]
    return call(
        "second_out",
        second_out_kernel,
        vm(mine, got),
        vm(struct((size, wide), F32), struct((size, wide), F32), struct((size, cols - 2 * wide), F32)),
    )


def grads_out_kernel(chunk, m0, g0, m1, g1, m2, g2, conv, cpe, qkv, *lines):
    width = cpe.shape[1]
    for i, (mine, got) in enumerate(((m0, g0), (m1, g1), (m2, g2))):
        part = mine[0, :, :chunk].astype(F32) + got[0, :, :chunk].astype(F32)
        for k in range(chunk // width):
            conv[i * (chunk // width) + k] = part[:, k * width : (k + 1) * width]
    third = m1[0, :, chunk:].astype(F32) + g1[0, :, chunk:].astype(F32)
    for t in range(3):
        qkv[t] = third[:, t * width : (t + 1) * width]
    cpe[...] = third[:, 3 * width : 4 * width]
    small = third[:16, 4 * width :]
    for r in range(VECTORS):
        lines[r][...] = small[r : r + 1, :]
    for i in range(4):
        lines[VECTORS][:, i * width : (i + 1) * width] = small[VECTORS + i : VECTORS + i + 1, :]
    lines[VECTORS + 1][...] = small[VECTORS + 4 :, :]


def grads_out(sums, chunk, width):
    size = sums[0].mine.shape[1]
    line = struct((1, width), F32)
    return call(
        "grads_out",
        functools.partial(grads_out_kernel, chunk),
        vm(*[a for s in sums for a in (s.mine, s.got)]),
        vm(struct((KERNEL, size, width), F32), struct((size, width), F32), struct((3, size, width), F32))
        + vm(*[line] * VECTORS, struct((1, 4 * width), F32), struct((2, width), F32)),
    )


def swap(values, e, axis="blk"):
    return lax.ppermute(values, axis, [(i, i ^ e) for i in range(lax.axis_size(axis))])


def after(values, *first):
    return lax.optimization_barrier((values, *first))[0]


def total_of(first, second):
    return (first.astype(F32) + second.astype(F32)).astype(BF)


class Scatter:
    def __init__(self, mine, theirs, count, stage):
        self.mine, self.theirs = mine, theirs
        self.numbers, _ = halves(count, stage)
        self.order = [stage] + [b for b in range(count.bit_length() - 1) if b != stage]
        self.got = swap(theirs, 1 << stage, "pts")

    def advance(self, *first):
        bit = self.order[1]
        keep = [j for j, r in enumerate(self.numbers) if not (r >> bit) & 1]
        send = [self.numbers.index(self.numbers[j] ^ (1 << bit)) for j in keep]
        self.mine, self.theirs = fold(self.mine, self.got, keep, send, first)
        self.numbers = [self.numbers[j] for j in keep]
        self.order = self.order[1:]
        self.got = swap(self.theirs, 1 << bit, "pts")
        return self.theirs

    def finish(self):
        while len(self.order) > 1:
            self.advance()
        return self


def shards(
    points, neighbours, patch_ids, conv_weight, conv_bias, cpe_weight, cpe_bias, cpe_gain, cpe_shift, first_gain,
    first_shift, qkv_weight, query_value_bias, proj_weight, proj_bias, second_gain, second_shift, hidden_weight,
    hidden_bias, output_weight, output_bias, out_grad,
):
    row_count, width = points.shape
    wide = conv_weight.shape[2]
    mine = row_count // 4
    shard_count = lax.axis_size("pts")
    me = lax.axis_index("blk")
    place_of = jnp.stack([me, lax.axis_index("pts")]).astype(jnp.int32)
    plan = Plan(mine, width)
    ups = [(i, i + 1) for i in range(shard_count - 1)]
    downs = [(i + 1, i) for i in range(shard_count - 1)]

    low = lax.ppermute(points[row_count - REACH :], "pts", ups)
    high = lax.ppermute(points[:REACH], "pts", downs)
    kernel_rows = conv_weight.reshape(KERNEL * width, wide)
    lookup = neighbours.T
    away_pack, near_pack, turned, small, patch_row = prepare(
        plan,
        place_of,
        qkv_weight.transpose(1, 0, 2),
        cpe_weight,
        points,
        patch_ids,
        (conv_bias, cpe_bias, cpe_gain, cpe_shift, first_gain, first_shift, proj_bias, second_gain, second_shift, output_bias),
        hidden_bias,
        query_value_bias,
        first=(low,),
    )
    hidden_far = swap(hidden_weight[: wide // 2], 2)
    far = swap(away_pack, 2)
    near = swap(near_pack, 1)

    *part3, gathered3, away_pack, near_pack = conv_forward(
        3, place_of, low, points, high, lookup, kernel_rows, BF, (hidden_weight, output_weight, proj_weight, out_grad),
        first=(hidden_far,),
    )
    got3 = [swap(p, 1) for p in part3]
    *part2, gathered2 = conv_forward(2, place_of, low, points, high, lookup, kernel_rows, BF, first=(part3[0],))
    far_part = swap(jnp.concatenate([total_of(a, b) for a, b in zip(part2, got3)], axis=0), 2)
    *part1, gathered1 = conv_forward(1, place_of, low, points, high, lookup, kernel_rows, BF, first=(part2[0],))
    *part0, gathered0 = conv_forward(0, place_of, low, points, high, lookup, kernel_rows, F32, first=(part1[0],), time=0.5)
    cross = swap(after(far, part2[0]), 1)
    close_part = [swap(p, 1) for p in part1]
    firsts = (near, far, cross)
    layer_one, conv_low, normed_cpe, scaling_cpe, residual_one, normed_one, scaling_one = first_rows(
        plan, place_of, part0, close_part, far_part, points, small, cpe_weight, *firsts
    )
    other_one = swap(layer_one, 1)
    hidden_cross = swap(after(hidden_far, layer_one), 1)
    far2 = swap(after(away_pack, layer_one), 2)
    near2 = swap(near_pack, 1)


    half = triple_half(plan, layer_one, turned, far, small)
    triple, mixed, keep, send, logs = attend_forward(plan, half, other_one, turned, far, small, patch_row, first=(hidden_cross,))
    got = swap(send, 1)
    cross2 = swap(after(far2, send), 1)
    (
        block0, block1, block_far, active, before, layer_two, upstream, carried, carried_low, grad_keep, grad_send,
        sum_hidden_bias, sums_two,
    ) = second_rows(
        plan, place_of, keep, got, residual_one, out_grad, (hidden_weight, output_weight, proj_weight), small, firsts,
        (near2, far2, cross2, hidden_far, hidden_cross),
    )
    grad_got = swap(grad_send, 1)

    weights_send = second_send(place_of, shard_count, upstream, active, before, layer_two, carried_low, got)
    weights_got = swap(after(weights_send, grad_got), 1)
    heads = width // HEAD_DIM
    grad_first = attend_backward(
        0, heads, triple, patch_row, grad_keep, grad_got, mixed, logs, first=(weights_send,)
    )
    weights_mine, weights_far = second_keep(
        place_of, shard_count, upstream, active, before, layer_two, carried_low, keep, weights_got, first=(grad_first,)
    )
    weights_far = swap(weights_far, 2)
    grad_second = attend_backward(
        heads, heads, triple, patch_row, grad_keep, grad_got, mixed, logs, first=(weights_mine,)
    )
    layer_send = layer_grad(1, grad_first, grad_second, turned, far, BF)
    layer_got = swap(layer_send, 1)
    layer_part = layer_grad(0, grad_first, grad_second, turned, far, F32, first=(layer_send,))
    conv_grad, points0, near_rows, far_rows, cpe_low, sums_one = third_rows(
        plan, place_of, layer_part, layer_got, carried, normed_one, scaling_one, normed_cpe, scaling_cpe, small, cpe_weight, firsts, (block1, block_far)
    )
    grad0 = conv_grad
    grad2 = swap(grad0, 2)
    grad1 = swap(grad0, 1)
    second_mine, second_theirs = fold(weights_mine, weights_far, *halves(shard_count, 0))
    second = Scatter(second_mine, second_theirs, shard_count, 0)
    spread0 = spread(0, (0, 1), place_of, lookup, kernel_rows, grad0, first=(weights_far,), time=TINY)
    cpe_send, cpe_keep, small_send, small_keep = cpe_weights(
        shard_count, place_of, conv_low, cpe_low, sums_one, sums_two, sum_hidden_bias, first=(spread0,)
    )
    cpe_got = swap(cpe_send, 1)
    small_got = swap(small_send, 1)
    third_mine, third_far = third_weights(
        place_of, shard_count, grad_first, grad_second, layer_one, other_one, cpe_keep, cpe_got, small_keep, small_got,
        first=(spread0, grad2, second.got),
    )
    grad3 = swap(after(grad2, cpe_send), 1)

    gathered = (gathered0, gathered1, gathered2, gathered3)
    grads = (grad0, grad1, grad2, grad3)
    chunk = KERNEL // 3 * width
    third_far = swap(after(third_far, grad2), 2)
    piece0, theirs0 = conv_weight_grad(
        place_of, gathered, grads, 0, chunk, shard_count, 0, first=(third_mine,)
    )
    sum0 = Scatter(piece0, theirs0, shard_count, 0)
    second_sent = second.advance(piece0)
    spread1 = spread(1, (0, 1), place_of, lookup, kernel_rows, grad1, first=(piece0, second_sent), time=TINY)
    piece1, theirs1 = conv_weight_grad(
        place_of, gathered, grads, chunk, chunk, shard_count, 0, thirds=(third_mine, third_far), first=(spread1,)
    )
    sum1 = Scatter(piece1, theirs1, shard_count, 0)
    sent = sum0.advance(piece1)
    piece2, theirs2 = conv_weight_grad(
        place_of, gathered, grads, 2 * chunk, chunk, shard_count, 0, first=(piece1, sent)
    )
    sum2 = Scatter(piece2, theirs2, shard_count, 0)
    spread2 = spread(2, (0,), place_of, lookup, kernel_rows, grad2, first=(piece2,), time=BLOCK)
    far_rows = swap(after(far_rows, piece2), 2)
    near_rows = swap(after(near_rows, piece2), 1)
    sent = sum0.advance(spread2)
    spread2_after = spread(2, (1,), place_of, lookup, kernel_rows, grad2, first=(spread2, sent), time=BLOCK)
    second_sent = second.advance(spread2_after)
    spread3 = spread(3, (0,), place_of, lookup, kernel_rows, grad3, first=(spread2_after, second_sent), time=BLOCK)
    sent = sum1.advance(spread3)
    spread3_after = spread(3, (1,), place_of, lookup, kernel_rows, grad3, first=(spread3, sent), time=BLOCK)

    sent = sum2.advance(spread3_after)
    grad_padded, to_below, to_above = finish(
        place_of, (spread0, spread1, spread2, spread2_after, spread3, spread3_after), first=(sent,)
    )
    cross_rows = swap(after(far_rows, spread3), 1)
    from_above = lax.ppermute(to_below, "pts", downs)
    from_below = lax.ppermute(to_above, "pts", ups)
    sent = sum1.advance(grad_padded)
    sent = sum2.advance(sent)
    second = second.finish()
    grad_hidden, grad_output, grad_proj = second_out(second.mine, second.got, wide)
    block_out, grad_points = rows_out(
        place_of, grad_padded, from_below, from_above, block0, points0, near_rows, far_rows, cross_rows,
        first=(sent, grad_hidden),
    )

    grad_conv, grad_cpe, grad_qkv, *lines = grads_out([s.finish() for s in (sum0, sum1, sum2)], chunk, width)
    small = [line.reshape(-1) for line in lines[: VECTORS + 1]]
    return (
        block_out,
        grad_points,
        grad_conv.transpose(0, 2, 1),
        small[0],
        grad_cpe.T,
        *small[1:6],
        grad_qkv.transpose(1, 0, 2),
        lines[VECTORS + 1],
        grad_proj.T,
        small[8],
        small[6],
        small[7],
        grad_hidden,
        small[10],
        grad_output.T,
        small[9],
    )


def solution(mesh):
    return jax.shard_map(
        shards,
        mesh=mesh,
        in_specs=(
            P("pts", "blk"),
            P("pts", None),
            P("pts"),
            P(None, "blk", None),
            P("blk"),
            P("blk", None),
            P("blk"),
            P("blk"),
            P("blk"),
            P("blk"),
            P("blk"),
            P(None, None, "blk"),
            P(None, "blk"),
            P("blk", None),
            P("blk"),
            P("blk"),
            P("blk"),
            P(None, "blk"),
            P("blk"),
            P("blk", None),
            P("blk"),
            P("pts", "blk"),
        ),
        out_specs=(
            P("pts", "blk"),
            P("pts", "blk"),
            P(None, "blk", "pts"),
            P("blk"),
            P("blk", "pts"),
            P("blk"),
            P("blk"),
            P("blk"),
            P("blk"),
            P("blk"),
            P("pts", None, "blk"),
            P(None, "blk"),
            P("blk", "pts"),
            P("blk"),
            P("blk"),
            P("blk"),
            P("pts", "blk"),
            P("blk"),
            P("blk", "pts"),
            P("blk"),
        ),
        check_vma=False,
    )
```

```python
import functools
import math

import jax
import jax.numpy as jnp
from jax import lax
from jax.experimental import pallas as pl
from jax.experimental.pallas import tpu as pltpu
from jax.sharding import PartitionSpec as P

HEAD_DIM = 16
PATCH = 1024
KERNEL = 27
REACH = 256
EPS = 1e-05
LOG2E = math.log2(math.e)
BF = jnp.bfloat16
F32 = jnp.float32
NN = ((1,), (0,))
NT = ((1,), (1,))
TN = ((0,), (0,))
VMEM = pl.BlockSpec(memory_space=pltpu.VMEM)
SMEM = pl.BlockSpec(memory_space=pltpu.SMEM)
HBM = pl.BlockSpec(memory_space=pltpu.HBM)
ANY = pl.BlockSpec(memory_space=pl.ANY)
TILE = 256


def dot(a, b, dims):
    return lax.dot_general(a, b, (dims, ((), ())), preferred_element_type=F32)


def struct(shape, kind):
    return jax.ShapeDtypeStruct(shape, kind)


TIMES = {
    "prepare": 10,  "conv_forward": 7.5, "first_rows": 2.5, "triple_half": 2, "attend_forward": 21, "second_rows": 10,
    "second_send": 1.5, "attend_backward": 19, "second_keep": 2.5, "layer_grad": 1, "third_rows": 2.3, "cpe_weights": 0.1,
    "spread": 7, "third_weights": 0.1, "conv_weight_grad": 0.1, "finish": 1.0, "rows_out": 2.0, "fold": 0.05, "second_out": 0.1, "grads_out": 0.1,
}
FACTOR = 0.3
TINY = 0.1
BLOCK = 4.2


def call(name, kernel, inputs, outputs, scratch=(), mib=8, grid=None, first=(), time=None):
    count, extra = len(inputs), len(first)

    def body(*refs):
        kernel(*refs[:count], *refs[count + extra :])

    options = {} if grid is None else {"grid": grid}
    result = pl.pallas_call(
        body,
        out_shape=[o for o, spec in outputs],
        in_specs=[spec for a, spec in inputs] + [ANY] * extra,
        out_specs=[spec for o, spec in outputs],
        scratch_shapes=list(scratch),
        compiler_params=pltpu.CompilerParams(vmem_limit_bytes=mib * 2**20),
        cost_estimate=pl.CostEstimate(flops=int((time or TIMES[name]) * FACTOR * 1.15e9), bytes_accessed=0, transcendentals=0),
        name=name,
        **options,
    )(*[pltpu.with_memory_space_constraint(a, pltpu.HBM) if spec is HBM else a for a, spec in inputs], *first)
    return result[0] if len(result) == 1 else result


def vm(*arrays):
    return [(a, VMEM) for a in arrays]


def split3(values):
    high = values.astype(BF)
    rest = values - high.astype(F32)
    middle = rest.astype(BF)
    return high, middle, (rest - middle.astype(F32)).astype(BF)


def joined(rows, width):
    rows = rows.astype(F32)
    return (rows[:, :width] + rows[:, width : 2 * width]) + rows[:, 2 * width : 3 * width]


def in_order(pieces, me):
    core, chip = (me & 1) == 1, (me >> 1) == 1
    a, b = jnp.where(core, pieces[1], pieces[0]), jnp.where(core, pieces[0], pieces[1])
    c, d = jnp.where(core, pieces[3], pieces[2]), jnp.where(core, pieces[2], pieces[3])
    return [
        jnp.where(chip, c, a),
        jnp.where(chip, d, b),
        jnp.where(chip, a, c),
        jnp.where(chip, b, d),
    ]


def folded(source, start, target, row, sems, rows):
    part, width = rows // 4, source.shape[1]
    copies = []
    for j in range(4):
        copies.append(
            pltpu.make_async_copy(
                source.at[pl.ds(pl.multiple_of(start + j * part, 16), part), :],
                target.at[row : row + part, j * width : (j + 1) * width],
                sems(),
            )
        )
    return copies


def unfolded(pack, row, at, rows):
    part, width = rows // 4, pack.shape[1] // 4
    return jnp.concatenate(
        [
            pack[row : row + part, j * width : (j + 1) * width]
            for j in range(at.start // part, at.stop // part)
        ],
        axis=0,
    )


class Plan:
    def __init__(self, rows, width):
        fold = rows // 4
        self.first_cpe = 3 * width
        self.first_points = 4 * width
        self.first_small = 4 * width + 2 * fold
        self.first_rows = self.first_small + 16
        self.near_points = width
        self.near_small = width + fold
        self.near_rows = self.near_small + 16


def counter(sems):
    state = [0]

    def take():
        state[0] += 1
        return sems.at[state[0] - 1]

    return take


VECTORS = 10


def prepare_kernel(
    plan, rows, place_of, turned_in, cpe, points, patch, *refs
):
    vectors, refs = refs[:VECTORS], refs[VECTORS:]
    hidden_bias, query_bias, away, near, turned, small, patch_row, terms, lines, long_line, pair, straight, sems = refs
    me = place_of[0]
    width = points.shape[1]
    take = counter(sems)
    copies = [
        pltpu.make_async_copy(cpe, away.at[plan.first_cpe : plan.first_cpe + width, :], take()),
        pltpu.make_async_copy(cpe, near.at[0:width, :], take()),
    ]
    for e in (2, 3):
        copies += folded(points, (me ^ e) * rows, away, plan.first_points + (e - 2) * rows // 4, take, rows)
    copies += folded(points, (me ^ 1) * rows, near, plan.near_points, take, rows)
    straight_copy = pltpu.make_async_copy(turned_in, straight, take())
    straight_copy.start()
    for copy in copies:
        copy.start()
    loads = [pltpu.make_async_copy(vector, lines.at[r], take()) for r, vector in enumerate(vectors)]
    loads.append(pltpu.make_async_copy(hidden_bias, long_line, take()))
    loads.append(pltpu.make_async_copy(query_bias, pair, take()))
    for copy in loads:
        copy.start()
    for e in (0, 1):
        at = pl.ds(pl.multiple_of((me ^ e) * rows, rows), rows)
        loads.append(pltpu.make_async_copy(patch.at[:, at], patch_row.at[:, e * rows : (e + 1) * rows], take()))
        loads[-1].start()
    straight_copy.wait()
    for t in range(3):
        turned[t * width : (t + 1) * width, :] = straight[t].T
    for copy in loads:
        copy.wait()
    for r in range(VECTORS):
        small[r : r + 1, :] = lines[r]
    for i in range(4):
        small[VECTORS + i : VECTORS + i + 1, :] = long_line[:, i * width : (i + 1) * width]
    small[VECTORS + 4 :, :] = pair[...]
    high, middle, low = split3(small[...])
    terms[...] = jnp.concatenate([high, middle, low, jnp.zeros_like(low)], axis=1)
    last = [
        pltpu.make_async_copy(turned, away.at[0 : 3 * width, :], take()),
        pltpu.make_async_copy(terms, away.at[plan.first_small :, :], take()),
        pltpu.make_async_copy(terms, near.at[plan.near_small :, :], take()),
    ]
    for copy in last:
        copy.start()
    for copy in copies + last:
        copy.wait()


def prepare(plan, place_of, turned, cpe, points, patch, vectors, hidden_bias, query_bias, first=()):
    row_count, width = points.shape
    wide = cpe.shape[1]
    lines = [v.reshape(1, -1) for v in (*vectors, hidden_bias)]
    return call(
        "prepare",
        functools.partial(prepare_kernel, plan, row_count // 4),
        [(place_of, SMEM), (turned, HBM), (cpe, HBM), (points, HBM), (patch.reshape(1, -1), HBM)]
        + [(v, HBM) for v in (*lines, query_bias)],
        [
            (struct((plan.first_rows, wide), BF), HBM),
            (struct((plan.near_rows, wide), BF), HBM),
            (struct((3 * width, wide), BF), VMEM),
            (struct((16, width), F32), VMEM),
            (struct((1, row_count // 2), jnp.int32), VMEM),
        ],
        [
            pltpu.VMEM((16, wide), BF),
            pltpu.VMEM((VECTORS, 1, width), F32),
            pltpu.VMEM((1, 4 * width), F32),
            pltpu.VMEM((2, width), F32),
            pltpu.VMEM(turned.shape, BF),
            pltpu.SemaphoreType.DMA((17 + VECTORS + 5,)),
        ],
        first=first,
    )


def one_hot(place):
    spots = lax.broadcasted_iota(jnp.int32, (256, 256), 0)
    return jnp.where(spots == jnp.broadcast_to(place, (256, 256)), 1.0, 0.0).astype(BF)


def conv_kernel(e, packs, place_of, low, points, high, lookup, weight, *refs):
    sources, refs = refs[:packs], refs[packs:]
    conv, conv_after, gathered = refs[:3]
    away, near = refs[3:5] if packs else (None, None)
    turned, picked, sems = refs[-3:]
    me = place_of[0]
    width = points.shape[1]
    rows = picked.shape[1]
    quarter = me ^ e
    take = counter(sems)
    copies = []
    if packs:
        hidden, output, proj, upstream = sources
        wide, fold = hidden.shape[1], rows // 4
        start = 2 * wide + width
        for target in (away, near):
            copies.append(pltpu.make_async_copy(output, target.at[0:wide, :], take()))
            copies.append(pltpu.make_async_copy(proj, target.at[wide : wide + width, :], take()))
            copies.append(pltpu.make_async_copy(hidden, target.at[wide + width : start, :], take()))
        copies += folded(upstream, (me ^ 2) * rows, away, start, take, rows)
        copies += folded(upstream, (me ^ 3) * rows, away, start + fold, take, rows)
        copies += folded(upstream, (me ^ 1) * rows, near, start, take, rows)
        for copy in copies:
            copy.start()
    base = place_of[1] * points.shape[0] + quarter * rows - REACH
    last = points.shape[0] // 256 - 1
    for j in range(rows // 256 + 2):
        spot = quarter * (rows // 256) - 1 + j
        at = pl.multiple_of(jnp.clip(spot, 0, last) * 256, 256)
        piece = points[pl.ds(at, 256), :]
        piece = jnp.where(spot < 0, low[...], jnp.where(spot > last, high[...], piece))
        turned[j * width : (j + 1) * width, :] = piece.T
    step = KERNEL // 3
    for b in range(rows // 256):
        cols = slice(b * 256, (b + 1) * 256)
        left = turned[b * width : (b + 3) * width, :]
        for k in range(KERNEL):
            spot = lookup[k : k + 1, pl.ds(pl.multiple_of(quarter * rows + b * 256, 256), 256)] - base
            part = jnp.broadcast_to(lax.shift_right_logical(spot, 8) - b, (width, 256))
            three = dot(left, one_hot(jnp.bitwise_and(spot, 255)), NN)
            values = jnp.where(
                part == 0,
                three[:width],
                jnp.where(part == 1, three[width : 2 * width], three[2 * width :]),
            )
            picked[k * width : (k + 1) * width, cols] = values.astype(BF)
            if k % step == step - 1:
                at = slice((k + 1 - step) * width, (k + 1) * width)
                copies.append(pltpu.make_async_copy(picked.at[at, cols], gathered.at[at, cols], take()))
                copies[-1].start()
        (conv, conv_after)[b][...] = dot(picked[:, cols], weight[...], TN).astype(conv.dtype)
    for copy in copies:
        copy.wait()


def conv_forward(e, place_of, low, points, high, lookup, weight, kind, packs=(), first=(), time=None):
    rows, width, wide = points.shape[0] // 4, points.shape[1], weight.shape[1]
    outputs = [(struct((rows // 2, wide), kind), VMEM)] * 2 + [(struct((KERNEL * width, rows), BF), HBM)]
    if packs:
        size = 2 * wide + width + rows // 4
        outputs += [(struct((size + rows // 4, wide), BF), HBM), (struct((size, wide), BF), HBM)]
    return call(
        "conv_forward",
        functools.partial(conv_kernel, e, len(packs)),
        [(place_of, SMEM)] + vm(low, points, high, lookup, weight) + [(p, HBM) for p in packs],
        outputs,
        [
            pltpu.VMEM(((rows // 256 + 2) * width, 256), BF),
            pltpu.VMEM((KERNEL * width, rows), BF),
            pltpu.SemaphoreType.DMA((6 * rows // 512 + (18 if packs else 0),)),
        ],
        first=first,
        time=time,
    )


def spread_kernel(e, blocks, place_of, lookup, weight, grads, out, upstream):
    width = out.shape[0]
    rows = grads.shape[0]
    quarter = place_of[0] ^ e
    base = place_of[1] * lookup.shape[1] + quarter * rows - REACH
    out[...] = jnp.zeros(out.shape, F32)
    step = 9
    for n, b in enumerate(blocks):
        cols = slice(b * 256, (b + 1) * 256)
        upstream[...] = dot(weight[...], grads[cols, :], NT)
        for s in range(KERNEL // step):
            left, right = [], []
            for k in range(s * step, (s + 1) * step):
                spot = lookup[k : k + 1, pl.ds(pl.multiple_of(quarter * rows + b * 256, 256), 256)] - base
                part = jnp.broadcast_to(lax.shift_right_logical(spot, 8) - b, (width, 256))
                mine = upstream[k * width : (k + 1) * width, :]
                left.append(
                    jnp.concatenate(
                        [jnp.where(part == i, mine, 0.0).astype(BF) for i in range(3)], axis=0
                    )
                )
                right.append(one_hot(jnp.bitwise_and(spot, 255)))
            three = dot(jnp.concatenate(left, axis=1), jnp.concatenate(right, axis=1), NT)
            for i in range(3):
                at = slice((n + i) * 256, (n + i + 1) * 256)
                out[:, at] = out[:, at] + three[i * width : (i + 1) * width]


def spread(e, blocks, place_of, lookup, weight, grads, first=(), time=None):
    width = weight.shape[0] // KERNEL
    return call(
        "spread",
        functools.partial(spread_kernel, e, blocks),
        [(place_of, SMEM)] + vm(lookup, weight, grads),
        [(struct((width, 256 * len(blocks) + 2 * REACH), F32), VMEM)],
        [pltpu.VMEM((KERNEL * width, 256), F32)],
        first=first,
        time=time,
    )


def halves(count, stage):
    keep = [r for r in range(count) if not (r >> stage) & 1]
    return keep, [r ^ (1 << stage) for r in keep]


def conv_weight_kernel(blocks, stage, start, count, extra, place_of, *refs):
    gathered, grads, refs = refs[:4], refs[4:8], refs[8:]
    thirds, (mine, theirs, total) = refs[:extra], refs[extra:]
    tile = 384
    for i in range(count // tile):
        rows = slice(start + i * tile, start + (i + 1) * tile)
        cols = slice(i * tile, (i + 1) * tile)
        total[:, cols] = sum(dot(a[rows, :], g[...], NN) for a, g in zip(gathered, grads)).T.astype(BF)
    size = total.shape[0] // blocks
    for out, slots in zip((mine, theirs), halves(blocks, stage)):
        for i, r in enumerate(slots):
            at = pl.multiple_of((place_of[1] ^ r) * size, size)
            out[i, :, 0:count] = total[pl.ds(at, size), :]
            if extra:
                out[i, :, count:] = (thirds[0][r].astype(F32) + thirds[1][r].astype(F32)).astype(BF)


def conv_weight_grad(place_of, gathered, grads, start, count, blocks, stage, thirds=(), first=()):
    wide = grads[0].shape[1]
    cols = count + (thirds[0].shape[2] if thirds else 0)
    half = struct((blocks // 2, wide // blocks, cols), BF)
    return call(
        "conv_weight_grad",
        functools.partial(conv_weight_kernel, blocks, stage, start, count, len(thirds)),
        [(place_of, SMEM)] + vm(*gathered, *grads, *thirds),
        vm(half, half),
        [pltpu.VMEM((wide, count), BF)],
        first=first,
    )


def finish_kernel(place_of, s0, s1, s2, s2_after, s3, s3_after, out, low, high):
    me = place_of[0]
    rows = s0.shape[1] - 2 * REACH
    ends = [s[:, 0:256] for s in (s0, s1, s2, s3)], [s[:, 768:] for s in (s0, s1)] + [s[:, 512:] for s in (s2_after, s3_after)]
    inner = [
        [s[:, 256:512] for s in (s0, s1)]
        + [a[:, 256:512] + b[:, 0:256] for a, b in ((s2, s2_after), (s3, s3_after))],
        [s[:, 512:768] for s in (s0, s1)]
        + [a[:, 512:768] + b[:, 256:512] for a, b in ((s2, s2_after), (s3, s3_after))],
    ]
    parts = [in_order(p, me) for p in (ends[0], inner[0], inner[1], ends[1])]
    out[...] = jnp.zeros(out.shape, F32)
    for q in range(4):
        for i, part in enumerate(parts):
            at = slice(q * rows + i * 256, q * rows + (i + 1) * 256)
            out[:, at] = out[:, at] + part[q]
    low[...] = out[:, :REACH].astype(BF)
    high[...] = out[:, out.shape[1] - REACH :].astype(BF)


def finish(place_of, spreads, first=()):
    width, span = spreads[0].shape
    total = 4 * (span - 2 * REACH) + 2 * REACH
    return call(
        "finish",
        finish_kernel,
        [(place_of, SMEM)] + vm(*spreads),
        [(struct((width, total), F32), VMEM)] + [(struct((width, REACH), BF), VMEM)] * 2,
        first=first,
    )


def rows_out_kernel(place_of, inside, below, above, block, own, near, far, cross, block_out, out):
    rows, width = own.shape
    me = place_of[0]
    pieces = in_order([block[...], near[:, :width], far[:, :width], cross[:, width : 2 * width]], me)
    for q in range(4):
        block_out[q * rows : (q + 1) * rows, :] = pieces[q]
    pieces = [own[...], near[:, width:], far[:, 2 * width : 3 * width], cross[:, 3 * width :]]
    pieces = in_order(pieces, me)
    for q in range(4):
        total = inside[:, REACH + q * rows : REACH + (q + 1) * rows].T + pieces[q].astype(F32)
        out[q * rows : (q + 1) * rows, :] = total
    out[:REACH, :] = out[:REACH, :] + below[...].astype(F32).T
    last = out.shape[0] - REACH
    out[last:, :] = out[last:, :] + above[...].astype(F32).T


def rows_out(place_of, inside, below, above, block, own, near, far, cross, first=()):
    rows, width = own.shape
    return call(
        "rows_out",
        rows_out_kernel,
        [(place_of, SMEM)] + vm(inside, below, above, block, own, near, far, cross),
        vm(struct((4 * rows, width), BF), struct((4 * rows, width), F32)),
        first=first,
    )


def three_rows(high, middle, low):
    spots = lax.broadcasted_iota(jnp.int32, (16, high.shape[1]), 0)
    picked = jnp.where(
        spots == 0,
        high.astype(F32),
        jnp.where(spots == 1, middle.astype(F32), jnp.where(spots == 2, low.astype(F32), 0.0)),
    )
    return picked.astype(BF)


def one_rows(length, count):
    spots = lax.broadcasted_iota(jnp.int32, (16, length), 0)
    return jnp.where(spots < count, 1.0, 0.0).astype(BF)


def patch_codes(patch):
    shape = (32, patch.shape[1])
    spots = lax.broadcasted_iota(jnp.int32, shape, 0)
    bits = jnp.bitwise_and(
        lax.shift_right_logical(jnp.broadcast_to(patch, shape), jnp.bitwise_and(spots, 15)), 1
    )
    bits = jnp.where(spots < 16, bits, 1 - bits)
    return jnp.where(bits == 1, 1.0, 0.0).astype(BF), jnp.where(bits == 1, 0.0, -1e30).astype(BF)


def fixed_rows(patch, query_side, key_side):
    length = patch.shape[1]
    left, right = patch_codes(patch)
    key_side[48:64, :] = one_rows(length, 3)
    key_side[64:96, :] = left
    query_side[64:96, :] = right
    key_side[96:128, :] = jnp.zeros((32, length), BF)
    query_side[96:128, :] = jnp.zeros((32, length), BF)


def column(row):
    return jnp.broadcast_to(row, (128, 128)).T[:, 0:1]


def triple_rows(values, weights, smalls, out, cols):
    width = out.shape[1] // 2
    for t in range(3):
        for i in range(2):
            piece = dot(weights[i][t * width : (t + 1) * width, :], values, NT)
            if t != 1:
                piece = piece + column(smalls[i][14 + t // 2 : 15 + t // 2, :])
            out[t, i * width : (i + 1) * width, cols] = piece.astype(BF)


def triple_half_kernel(plan, values, turned, away, small, out):
    smalls = (small[...], joined(away[plan.first_small :, :], small.shape[1]))
    triple_rows(values[...], (turned, away), smalls, out, slice(0, values.shape[0]))


def triple_half(plan, values, turned, away, small):
    return call(
        "triple_half",
        functools.partial(triple_half_kernel, plan),
        vm(values, turned, away, small),
        [(struct((3, 2 * small.shape[1], values.shape[0]), BF), VMEM)],
    )


def attend_forward_kernel(
    plan, heads, tile, mine, other, turned, away, small, patch, triple, total, keep, send, logs, query_side, key_side, value_side
):
    rows = mine.shape[2]
    length = 2 * rows
    for t in range(3):
        triple[t, :, :rows] = mine[t]
    smalls = (small[...], joined(away[plan.first_small :, :], small.shape[1]))
    triple_rows(other[...], (turned, away), smalls, triple, slice(rows, length))
    fixed_rows(patch[...], query_side, key_side)
    value_side[16:32, :] = one_rows(length, 1)

    @pl.loop(0, heads)
    def _(h):
        at = pl.ds(pl.multiple_of(h * HEAD_DIM, HEAD_DIM), HEAD_DIM)
        query = triple[0, at, :].astype(F32) * (HEAD_DIM**-0.5 * LOG2E)
        key = triple[1, at, :]
        high, middle, low = split3(query)
        query_side[0:16, :] = high
        query_side[16:32, :] = middle
        query_side[32:48, :] = low
        query_side[48:64, :] = jnp.zeros((16, length), BF)
        key_side[0:16, :] = key
        key_side[16:32, :] = key
        key_side[32:48, :] = key
        value_side[0:16, :] = triple[2, at, :]
        wide_key = key.astype(F32)
        bound = jnp.max(jnp.sum(query * query, axis=0)) * jnp.max(
            jnp.sum(wide_key * wide_key, axis=0)
        )
        logs[pl.ds(h, 1), :] = jnp.zeros((1, length), F32)

        @pl.when(jnp.logical_not(bound < 4096.0))
        def _():
            for t in range(length // tile):
                cols = slice(t * tile, (t + 1) * tile)
                top = jnp.max(dot(key_side[...], query_side[:, cols], TN), axis=0, keepdims=True)
                query_side[48:64, cols] = three_rows(*split3(-top))
                logs[pl.ds(h, 1), cols] = top

        for t in range(length // tile):
            cols = slice(t * tile, (t + 1) * tile)
            weights = jnp.exp2(dot(key_side[...], query_side[:, cols], TN)).astype(BF)
            mixed = dot(value_side[...], weights, NN)
            sums = mixed[16:17, :]
            mixed = mixed[0:16, :] * (1.0 / sums)
            total[at, cols] = mixed
            if t * tile < rows:
                keep[at, cols] = mixed.astype(BF)
            else:
                send[at, t * tile - rows : (t + 1) * tile - rows] = mixed.astype(BF)
            logs[pl.ds(h, 1), cols] = logs[pl.ds(h, 1), cols] + jnp.log2(sums)


def attend_forward(plan, mine, other, turned, away, small, patch, first=()):
    width, rows = mine.shape[1:]
    length = 2 * rows
    heads = width // HEAD_DIM
    return call(
        "attend_forward",
        functools.partial(attend_forward_kernel, plan, heads, 512),
        vm(mine, other, turned, away, small, patch),
        [
            (struct((3, width, length), BF), VMEM),
            (struct((width, length), F32), VMEM),
            (struct((width, rows), BF), VMEM),
            (struct((width, rows), BF), VMEM),
            (struct((heads, length), F32), VMEM),
        ],
        [
            pltpu.VMEM((128, length), BF),
            pltpu.VMEM((128, length), BF),
            pltpu.VMEM((32, length), BF),
        ],
        first=first,
    )


def attend_backward_kernel(
    first, heads, tile, triple, patch, mine, other, mixed, logs, out, query_side, key_side, value_side, grad_side, grad_value, grad_key
):
    length = triple.shape[2]
    fixed_rows(patch[...], query_side, key_side)
    value_side[16:32, :] = one_rows(length, 3)

    @pl.loop(0, heads)
    def _(h):
        at = pl.ds(pl.multiple_of((h + first) * HEAD_DIM, HEAD_DIM), HEAD_DIM)
        to = pl.ds(pl.multiple_of(h * HEAD_DIM, HEAD_DIM), HEAD_DIM)
        query, key = triple[0, at, :], triple[1, at, :]
        upstream = jnp.concatenate([mine[at, :], other[at, :]], axis=1)
        high, middle, low = split3(query.astype(F32) * (HEAD_DIM**-0.5 * LOG2E))
        query_side[0:16, :] = high
        query_side[16:32, :] = middle
        query_side[32:48, :] = low
        query_side[48:64, :] = three_rows(*split3(-logs[pl.ds(h + first, 1), :]))
        key_side[0:16, :] = key
        key_side[16:32, :] = key
        key_side[32:48, :] = key
        value_side[0:16, :] = triple[2, at, :]
        inner = jnp.sum(upstream.astype(F32) * mixed[at, :], axis=0, keepdims=True)
        grad_side[0:16, :] = upstream
        grad_side[16:32, :] = three_rows(*split3(-inner))
        for t in range(length // tile):
            cols = slice(t * tile, (t + 1) * tile)
            prob = jnp.exp2(dot(query_side[:, cols], key_side[...], TN))
            grad_prob = dot(grad_side[:, cols], value_side[...], TN)
            grad_score = (prob * grad_prob).astype(BF)
            value_part = dot(upstream[:, cols], prob.astype(BF), NN)
            key_part = dot(query[:, cols], grad_score, NN)
            out[0, to, cols] = (dot(key, grad_score, NT) * HEAD_DIM**-0.5).astype(BF)
            if t == 0:
                grad_value[...] = value_part
                grad_key[...] = key_part
            else:
                grad_value[...] += value_part
                grad_key[...] += key_part
        out[1, to, :] = (grad_key[...] * HEAD_DIM**-0.5).astype(BF)
        out[2, to, :] = grad_value[...].astype(BF)


def attend_backward(first_head, heads, triple, patch, mine, other, mixed, logs, first=()):
    length = triple.shape[2]
    return call(
        "attend_backward",
        functools.partial(attend_backward_kernel, first_head, heads, 512),
        vm(triple, patch, mine, other, mixed, logs),
        [(struct((3, heads * HEAD_DIM, length), BF), VMEM)],
        [
            pltpu.VMEM((128, length), BF),
            pltpu.VMEM((128, length), BF),
            pltpu.VMEM((32, length), BF),
            pltpu.VMEM((32, length), BF),
            pltpu.VMEM((16, length), F32),
            pltpu.VMEM((16, length), F32),
        ],
        mib=12,
        first=first,
    )


def norm_rows(values):
    average = jnp.mean(values, axis=1, keepdims=True)
    scaling = lax.rsqrt(
        jnp.mean(values * values, axis=1, keepdims=True) - average * average + EPS
    )
    return (values - average) * scaling, scaling


def norm_rows_back(upstream, normed, scaling, gain):
    scaled = upstream * gain
    return scaling * (
        scaled
        - jnp.mean(scaled, axis=1, keepdims=True)
        - normed * jnp.mean(scaled * normed, axis=1, keepdims=True)
    )


def cut(values):
    width = values.shape[1] // 4
    return [values[:, j * width : (j + 1) * width] for j in range(4)]


def add_rows(ref, row, values, first):
    total = jnp.sum(values, axis=0, keepdims=True)
    ref[row : row + 1, :] = total if first else ref[row : row + 1, :] + total


def small_vectors(plan, small, near, far, cross):
    width = small.shape[1]
    return [
        small[...],
        joined(near[plan.near_small :, :], width),
        joined(far[plan.first_small :, :], width),
        joined(cross[plan.first_small :, :], width),
    ]


def vectors(smalls, me):
    return jnp.concatenate(in_order(smalls, me), axis=1)


def cpe_rows(plan, weight, near, far, cross, me):
    width = weight.shape[0]
    at = slice(plan.first_cpe, plan.first_cpe + width)
    pieces = [weight[...], near[:width, :], far[at, :], cross[at, :]]
    return jnp.concatenate(in_order(pieces, me), axis=0)


def own_rows(ref, me, rows, at):
    return ref[pl.ds(pl.multiple_of(me * rows + at.start, at.stop - at.start), at.stop - at.start), :]


def first_rows_kernel(
    plan, place_of, part_low, part_high, close_low, close_high, away, points, small, weight, near, far, cross,
    layer, middle, normed_cpe, scaling_cpe, residual, normed, scaling,
):
    me = place_of[0]
    rows = 2 * part_low.shape[0]
    vec = vectors(small_vectors(plan, small, near, far, cross), me)
    vec = [vec[r : r + 1, :] for r in range(6)]
    weights = cpe_rows(plan, weight, near, far, cross, me)
    for t in range(rows // TILE):
        at = slice(t * TILE, (t + 1) * TILE)
        part, close = ((part_low, close_low), (part_high, close_high))[t * TILE * 2 // rows]
        low = (part[...] + close[...].astype(F32) + away[at, :].astype(F32) + vec[0]).astype(BF)
        middle[at, :] = low
        xhat, rate = norm_rows(dot(low, weights, NN) + vec[1])
        normed_cpe[at, :] = xhat
        scaling_cpe[at, :] = rate
        features = [
            own_rows(points, me, rows, at),
            unfolded(near, plan.near_points, at, rows),
            unfolded(far, plan.first_points, at, rows),
            unfolded(cross, plan.first_points + rows // 4, at, rows),
        ]
        features = jnp.concatenate(in_order(features, me), axis=1)
        sums = features.astype(F32) + xhat * vec[2] + vec[3]
        residual[at, :] = sums
        xhat, rate = norm_rows(sums)
        normed[at, :] = xhat
        scaling[at, :] = rate
        layer[at, :] = (xhat * vec[4] + vec[5]).astype(BF)


def first_rows(plan, place_of, parts, closes, away, points, small, weight, near, far, cross):
    rows, wide = away.shape
    full, thin, lower = struct((rows, wide), F32), struct((rows, 1), F32), struct((rows, wide), BF)
    return call(
        "first_rows",
        functools.partial(first_rows_kernel, plan),
        [(place_of, SMEM)] + vm(*parts, *closes, away, points, small, weight, near, far, cross),
        vm(lower, lower, full, thin, full, full, thin),
    )


def gelu_parts(u):
    scale = math.sqrt(2 / math.pi)
    square = u * u
    bent = jnp.tanh(u * (scale + (scale * 0.044715) * square))
    half = 0.5 + 0.5 * bent
    slope = half + u * (1.0 - bent * bent) * (0.5 * scale + (1.5 * 0.044715 * scale) * square)
    return u * half, slope


def second_rows_kernel(
    plan, place_of, keep, got, residual, out_grad, hidden, output, proj, small, near, far, cross, near2, far2, cross2,
    block0, block1, block_far, active, before, layer, upstream, carried, low, grad_keep, grad_send, hidden_sums, sums,
):
    me = place_of[0]
    rows, wide = residual.shape
    smalls = small_vectors(plan, small, near, far, cross)
    vec = vectors(smalls, me)
    vec = {r: vec[r : r + 1, :] for r in (6, 7, 8, 9)}
    biases = [jnp.concatenate([s[10 + i : 11 + i, :] for i in range(4)], axis=1) for s in smalls]
    width = keep.shape[0] // 2
    packs = (near2, far2, cross2)
    end = wide + width
    hiddens = [hidden] + [p.at[end : end + wide, :] for p in packs]
    last = end + wide
    outputs = [output] + [p.at[0:wide, :] for p in packs]
    projs = [proj[...]] + [p[wide:end, :] for p in packs]
    mine = jnp.concatenate([projs[0], projs[2]], axis=0)
    others = jnp.concatenate([projs[1], projs[3]], axis=0)
    for t in range(rows // TILE):
        at = slice(t * TILE, (t + 1) * TILE)
        base = residual[at, :] + vec[6] + dot(keep[:, at], mine, TN) + dot(got[:, at], others, TN)
        normed, scaling = norm_rows(base)
        lower = (normed * vec[7] + vec[8]).astype(BF)
        layer[at, :] = lower
        grads = [
            own_rows(out_grad, me, rows, at),
            unfolded(near2, last, at, rows),
            unfolded(far2, last, at, rows),
            unfolded(cross2, last + rows // 4, at, rows),
        ]
        grads = jnp.concatenate(in_order(grads, me), axis=1)
        upstream[at, :] = grads
        result = base + vec[9]
        grad_layer = None
        for e in range(4):
            act, slope = gelu_parts(dot(lower, hiddens[e][...], NN) + biases[e])
            act = act.astype(BF)
            active[e, at, :] = act
            result = result + dot(act, outputs[e][...], NN)
            pre = dot(grads, outputs[e][...], NT) * slope
            add_rows(hidden_sums, e, pre, t == 0)
            pre = pre.astype(BF)
            before[e, at, :] = pre
            piece = dot(pre, hiddens[e][...], NT)
            grad_layer = piece if e == 0 else grad_layer + piece
        result = in_order(cut(result.astype(BF)), me)
        block0[at, :] = result[0]
        block1[at, :] = result[1]
        block_far[at, 0:width] = result[2]
        block_far[at, width:] = result[3]
        wide_grads = grads.astype(F32)
        add_rows(sums, 0, grad_layer * normed, t == 0)
        add_rows(sums, 1, grad_layer, t == 0)
        add_rows(sums, 3, wide_grads, t == 0)
        carry = wide_grads + norm_rows_back(grad_layer, normed, scaling, vec[7])
        carried[at, :] = carry
        add_rows(sums, 2, carry, t == 0)
        carry = carry.astype(BF)
        low[at, :] = carry
        grad_keep[:, at] = dot(mine, carry, NT).astype(BF)
        grad_send[:, at] = dot(others, carry, NT).astype(BF)


def second_rows(plan, place_of, keep, got, residual, out_grad, weights, small, firsts, seconds):
    rows, wide = residual.shape
    lower, piece = struct((rows, wide), BF), struct((rows, wide // 4), BF)
    heads = struct(keep.shape, BF)
    return call(
        "second_rows",
        functools.partial(second_rows_kernel, plan),
        [(place_of, SMEM)] + vm(keep, got, residual, out_grad, *weights, small, *firsts, *seconds),
        vm(
            piece,
            piece,
            struct((rows, wide // 2), BF),
            struct((4, rows, wide), BF),
            struct((4, rows, wide), BF),
            lower,
            lower,
            struct((rows, wide), F32),
            lower,
            heads,
            heads,
            struct((4, wide), F32),
            struct((4, wide), F32),
        ),
        mib=12,
    )


def cut_rows(store, spot, cols, value, blocks):
    size = value.shape[0] // blocks
    for p in range(blocks):
        store(p ^ spot, cols, value[p * size : (p + 1) * size])


def second_weight_parts(i, e, blocks, spot, upstream, active, before, layer, low, attended, store):
    wide = layer.shape[1]
    width = attended.shape[0] // 2
    cut_rows(store, spot, slice(0, wide), dot(layer[...], before[e], TN), blocks)
    cut_rows(store, spot, slice(wide, 2 * wide), dot(upstream[...], active[e], TN), blocks)
    part = dot(attended[i * width : (i + 1) * width, :], low[...], NN)
    cut_rows(store, spot, slice(2 * wide, 2 * wide + width), part.T, blocks)


def second_send_kernel(blocks, place_of, upstream, active, before, layer, low, attended, out):
    for i, e in enumerate((1, 3)):

        def store(p, cols, value):
            out[i, p, :, cols] = value.astype(BF)

        second_weight_parts(i, e, blocks, place_of[1], upstream, active, before, layer, low, attended, store)


def second_send(place_of, blocks, upstream, active, before, layer, low, attended):
    wide = layer.shape[1]
    return call(
        "second_send",
        functools.partial(second_send_kernel, blocks),
        [(place_of, SMEM)] + vm(upstream, active, before, layer, low, attended),
        [(struct((2, blocks, wide // blocks, 2 * wide + attended.shape[0] // 2), BF), VMEM)],
    )


def second_keep_kernel(blocks, place_of, upstream, active, before, layer, low, attended, got, mine, far):
    for i, out in enumerate((mine, far)):

        def store(p, cols, value):
            out[p, :, cols] = (value + got[i, p, :, cols].astype(F32)).astype(BF)

        second_weight_parts(i, 2 * i, blocks, place_of[1], upstream, active, before, layer, low, attended, store)


def second_keep(place_of, blocks, upstream, active, before, layer, low, attended, got, first=()):
    out = struct(got.shape[1:], BF)
    return call(
        "second_keep",
        functools.partial(second_keep_kernel, blocks),
        [(place_of, SMEM)] + vm(upstream, active, before, layer, low, attended, got),
        vm(out, out),
        first=first,
    )


def third_weights_kernel(
    blocks, place_of, first_half, second_half, mine, other, cpe_keep, cpe_got, small_keep, own, far
):
    rows = mine.shape[0]
    width = first_half.shape[1]
    size = own.shape[1]
    empty = jnp.zeros((size - 16, width), BF)
    for i, (grads, out) in enumerate(((first_half, own), (second_half, far))):

        def store(p, cols, value):
            out[p, :, cols] = value.astype(BF)

        for t in range(3):
            part = dot(grads[t, :, :rows], mine[...], NN) + dot(grads[t, :, rows:], other[...], NN)
            cut_rows(store, place_of[1], slice(t * width, (t + 1) * width), part.T, blocks)
        sums = [jnp.sum(grads[t].astype(F32).T, axis=0, keepdims=True) for t in (0, 2)]
        small_got = sum(cpe_got[i, slot, size:, :].astype(F32) for slot in range(3))
        small = small_keep[i] + small_got + jnp.concatenate([jnp.zeros((14, width), F32)] + sums, axis=0)
        for p in range(blocks):
            out[p, :, 3 * width : 4 * width] = (
                cpe_keep[i, p].astype(F32) + cpe_got[i, p, :size, :].astype(F32)
            ).astype(BF)
            out[p, 0:16, 4 * width :] = small.astype(BF)
            if empty.shape[0]:
                out[p, 16:, 4 * width :] = empty


def third_weights(place_of, blocks, first_half, second_half, mine, other, cpe_keep, cpe_got, small_keep, first=()):
    wide = mine.shape[1]
    width = first_half.shape[1]
    out = struct((blocks, wide // blocks, 5 * width), BF)
    return call(
        "third_weights",
        functools.partial(third_weights_kernel, blocks),
        [(place_of, SMEM)] + vm(first_half, second_half, mine, other, cpe_keep, cpe_got, small_keep),
        vm(out, out),
        first=first,
    )


def layer_grad_kernel(half, first_half, second_half, turned, away, out):
    width = first_half.shape[1]
    rows = first_half.shape[2] // 2
    cols = slice(half * rows, (half + 1) * rows)
    total = None
    for t in range(3):
        at = slice(t * width, (t + 1) * width)
        for grads, weight in ((first_half, turned), (second_half, away)):
            piece = dot(grads[t, :, cols], weight[at, :], TN)
            total = piece if total is None else total + piece
    out[...] = total.astype(out.dtype)


def layer_grad(half, first_half, second_half, turned, away, kind, first=()):
    return call(
        "layer_grad",
        functools.partial(layer_grad_kernel, half),
        vm(first_half, second_half, turned, away),
        [(struct((first_half.shape[2] // 2, turned.shape[1]), kind), VMEM)],
        first=first,
    )


def third_rows_kernel(
    plan, place_of, part, close, carried, normed, scaling, normed_cpe, scaling_cpe, small, weight, near, far, cross, block1, block_far,
    conv_grad, points0, near_rows, far_rows, low, sums,
):
    me = place_of[0]
    vec = vectors(small_vectors(plan, small, near, far, cross), me)
    weights = cpe_rows(plan, weight, near, far, cross, me)
    width = points0.shape[1]
    for t in range(part.shape[0] // TILE):
        at = slice(t * TILE, (t + 1) * TILE)
        upstream = part[at, :] + close[at, :].astype(F32)
        xhat = normed[at, :]
        add_rows(sums, 4, upstream * xhat, t == 0)
        add_rows(sums, 5, upstream, t == 0)
        grads = carried[at, :] + norm_rows_back(upstream, xhat, scaling[at, :], vec[4:5, :])
        pieces = in_order(cut(grads.astype(BF)), me)
        points0[at, :] = pieces[0]
        near_rows[at, 0:width] = block1[at, :]
        near_rows[at, width:] = pieces[1]
        far_rows[at, 0 : 2 * width] = block_far[at, :]
        far_rows[at, 2 * width : 3 * width] = pieces[2]
        far_rows[at, 3 * width :] = pieces[3]
        xhat = normed_cpe[at, :]
        add_rows(sums, 2, grads * xhat, t == 0)
        add_rows(sums, 3, grads, t == 0)
        grads = norm_rows_back(grads, xhat, scaling_cpe[at, :], vec[2:3, :])
        add_rows(sums, 1, grads, t == 0)
        lower = grads.astype(BF)
        low[at, :] = lower
        result = dot(lower, weights, NT)
        add_rows(sums, 0, result, t == 0)
        conv_grad[at, :] = result.astype(BF)


def third_rows(plan, place_of, part, close, carried, normed, scaling, normed_cpe, scaling_cpe, small, weight, firsts, blocks):
    rows, wide = part.shape
    lower, piece = struct((rows, wide), BF), struct((rows, wide // 4), BF)
    return call(
        "third_rows",
        functools.partial(third_rows_kernel, plan),
        [(place_of, SMEM)]
        + vm(part, close, carried, normed, scaling, normed_cpe, scaling_cpe, small, weight, *firsts, *blocks),
        vm(lower, piece, struct((rows, wide // 2), BF), lower, lower, struct((6, wide), F32)),
    )


def cpe_weights_kernel(
    blocks, place_of, middle, low, sums_one, sums_two, hidden_sums, send, keep, small_keep, small_send
):
    me = place_of[0]
    width = middle.shape[1] // 4
    ones, twos = in_order(cut(sums_one[...]), me), in_order(cut(sums_two[...]), me)
    for e in range(4):
        out = (keep, send, keep, send)[e]

        def store(p, cols, value):
            out[e // 2, p, : value.shape[0], cols] = value.astype(BF)

        at = pl.ds(pl.multiple_of((e ^ me) * width, width), width)
        cut_rows(store, place_of[1], slice(0, width), dot(low[...], middle[:, at], TN), blocks)
        out = (small_keep, small_send, small_keep, small_send)[e]
        out[e // 2, 0:6, :] = ones[e]
        out[e // 2, 6:10, :] = twos[e]
        for i in range(4):
            out[e // 2, 10 + i : 11 + i, :] = hidden_sums[e : e + 1, i * width : (i + 1) * width]
        out[e // 2, 14:16, :] = jnp.zeros((2, width), F32)
    size = send.shape[2] - 16
    for i in range(2):
        for slot, term in enumerate(split3(small_send[i])):
            send[i, slot, size:, :] = term
        send[i, 3:, size:, :] = jnp.zeros((blocks - 3, 16, width), BF)


def cpe_weights(blocks, place_of, middle, low, sums_one, sums_two, hidden_sums, first=()):
    wide = middle.shape[1]
    send = struct((2, blocks, wide // blocks + 16, wide // 4), BF)
    keep = struct((2, blocks, wide // blocks, wide // 4), BF)
    small = (2, 16, wide // 4)
    return call(
        "cpe_weights",
        functools.partial(cpe_weights_kernel, blocks),
        [(place_of, SMEM)] + vm(middle, low, sums_one, sums_two, hidden_sums),
        vm(send, keep, struct(small, F32)),
        [pltpu.VMEM(small, F32)],
        first=first,
    )


def fold_kernel(keep, send, mine, got, kept, sent):
    for out, slots in ((sent, send), (kept, keep)):
        for i, j in enumerate(slots):
            out[i] = (mine[j].astype(F32) + got[j].astype(F32)).astype(BF)


def fold(mine, got, keep, send, first=()):
    out = struct((len(keep), *mine.shape[1:]), BF)
    return call("fold", functools.partial(fold_kernel, keep, send), vm(mine, got), vm(out, out), first=first)


def second_out_kernel(mine, got, hidden, output, proj):
    total = mine[0].astype(F32) + got[0].astype(F32)
    wide = hidden.shape[1]
    hidden[...] = total[:, :wide]
    output[...] = total[:, wide : 2 * wide]
    proj[...] = total[:, 2 * wide :]


def second_out(mine, got, wide):
    size, cols = mine.shape[1:]
    return call(
        "second_out",
        second_out_kernel,
        vm(mine, got),
        vm(struct((size, wide), F32), struct((size, wide), F32), struct((size, cols - 2 * wide), F32)),
    )


def grads_out_kernel(chunk, m0, g0, m1, g1, m2, g2, conv, cpe, qkv, *lines):
    width = cpe.shape[1]
    for i, (mine, got) in enumerate(((m0, g0), (m1, g1), (m2, g2))):
        part = mine[0, :, :chunk].astype(F32) + got[0, :, :chunk].astype(F32)
        for k in range(chunk // width):
            conv[i * (chunk // width) + k] = part[:, k * width : (k + 1) * width]
    third = m1[0, :, chunk:].astype(F32) + g1[0, :, chunk:].astype(F32)
    for t in range(3):
        qkv[t] = third[:, t * width : (t + 1) * width]
    cpe[...] = third[:, 3 * width : 4 * width]
    small = third[:16, 4 * width :]
    for r in range(VECTORS):
        lines[r][...] = small[r : r + 1, :]
    for i in range(4):
        lines[VECTORS][:, i * width : (i + 1) * width] = small[VECTORS + i : VECTORS + i + 1, :]
    lines[VECTORS + 1][...] = small[VECTORS + 4 :, :]


def grads_out(sums, chunk, width):
    size = sums[0].mine.shape[1]
    line = struct((1, width), F32)
    return call(
        "grads_out",
        functools.partial(grads_out_kernel, chunk),
        vm(*[a for s in sums for a in (s.mine, s.got)]),
        vm(struct((KERNEL, size, width), F32), struct((size, width), F32), struct((3, size, width), F32))
        + vm(*[line] * VECTORS, struct((1, 4 * width), F32), struct((2, width), F32)),
    )


def swap(values, e, axis="blk"):
    return lax.ppermute(values, axis, [(i, i ^ e) for i in range(lax.axis_size(axis))])


def after(values, *first):
    return lax.optimization_barrier((values, *first))[0]


def total_of(first, second):
    return (first.astype(F32) + second.astype(F32)).astype(BF)


class Scatter:
    def __init__(self, mine, theirs, count, stage):
        self.mine, self.theirs = mine, theirs
        self.numbers, _ = halves(count, stage)
        self.order = [stage] + [b for b in range(count.bit_length() - 1) if b != stage]
        self.got = swap(theirs, 1 << stage, "pts")

    def advance(self, *first):
        bit = self.order[1]
        keep = [j for j, r in enumerate(self.numbers) if not (r >> bit) & 1]
        send = [self.numbers.index(self.numbers[j] ^ (1 << bit)) for j in keep]
        self.mine, self.theirs = fold(self.mine, self.got, keep, send, first)
        self.numbers = [self.numbers[j] for j in keep]
        self.order = self.order[1:]
        self.got = swap(self.theirs, 1 << bit, "pts")
        return self.theirs

    def finish(self):
        while len(self.order) > 1:
            self.advance()
        return self


def shards(
    points, neighbours, patch_ids, conv_weight, conv_bias, cpe_weight, cpe_bias, cpe_gain, cpe_shift, first_gain,
    first_shift, qkv_weight, query_value_bias, proj_weight, proj_bias, second_gain, second_shift, hidden_weight,
    hidden_bias, output_weight, output_bias, out_grad,
):
    row_count, width = points.shape
    wide = conv_weight.shape[2]
    mine = row_count // 4
    shard_count = lax.axis_size("pts")
    me = lax.axis_index("blk")
    place_of = jnp.stack([me, lax.axis_index("pts")]).astype(jnp.int32)
    plan = Plan(mine, width)
    ups = [(i, i + 1) for i in range(shard_count - 1)]
    downs = [(i + 1, i) for i in range(shard_count - 1)]

    low = lax.ppermute(points[row_count - REACH :], "pts", ups)
    high = lax.ppermute(points[:REACH], "pts", downs)
    kernel_rows = conv_weight.reshape(KERNEL * width, wide)
    lookup = neighbours.T
    away_pack, near_pack, turned, small, patch_row = prepare(
        plan,
        place_of,
        qkv_weight.transpose(1, 0, 2),
        cpe_weight,
        points,
        patch_ids,
        (conv_bias, cpe_bias, cpe_gain, cpe_shift, first_gain, first_shift, proj_bias, second_gain, second_shift, output_bias),
        hidden_bias,
        query_value_bias,
        first=(low,),
    )
    far = swap(away_pack, 2)
    near = swap(near_pack, 1)

    *part3, gathered3, away_pack, near_pack = conv_forward(
        3, place_of, low, points, high, lookup, kernel_rows, BF, (hidden_weight, output_weight, proj_weight, out_grad),
    )
    got3 = [swap(p, 1) for p in part3]
    *part2, gathered2 = conv_forward(2, place_of, low, points, high, lookup, kernel_rows, BF, first=(part3[0],))
    far_part = swap(jnp.concatenate([total_of(a, b) for a, b in zip(part2, got3)], axis=0), 2)
    *part1, gathered1 = conv_forward(1, place_of, low, points, high, lookup, kernel_rows, BF, first=(part2[0],))
    *part0, gathered0 = conv_forward(0, place_of, low, points, high, lookup, kernel_rows, F32, first=(part1[0],), time=0.5)
    cross = swap(after(far, part2[0]), 1)
    close_part = [swap(p, 1) for p in part1]
    firsts = (near, far, cross)
    layer_one, conv_low, normed_cpe, scaling_cpe, residual_one, normed_one, scaling_one = first_rows(
        plan, place_of, part0, close_part, far_part, points, small, cpe_weight, *firsts
    )
    other_one = swap(layer_one, 1)
    far2 = swap(after(away_pack, layer_one), 2)
    near2 = swap(near_pack, 1)


    half = triple_half(plan, layer_one, turned, far, small)
    triple, mixed, keep, send, logs = attend_forward(plan, half, other_one, turned, far, small, patch_row)
    got = swap(send, 1)
    cross2 = swap(after(far2, send), 1)
    (
        block0, block1, block_far, active, before, layer_two, upstream, carried, carried_low, grad_keep, grad_send,
        sum_hidden_bias, sums_two,
    ) = second_rows(
        plan, place_of, keep, got, residual_one, out_grad, (hidden_weight, output_weight, proj_weight), small, firsts,
        (near2, far2, cross2),
    )
    grad_got = swap(grad_send, 1)

    weights_send = second_send(place_of, shard_count, upstream, active, before, layer_two, carried_low, got)
    weights_got = swap(after(weights_send, grad_got), 1)
    heads = width // HEAD_DIM
    grad_first = attend_backward(
        0, heads, triple, patch_row, grad_keep, grad_got, mixed, logs, first=(weights_send,)
    )
    weights_mine, weights_far = second_keep(
        place_of, shard_count, upstream, active, before, layer_two, carried_low, keep, weights_got, first=(grad_first,)
    )
    weights_far = swap(weights_far, 2)
    grad_second = attend_backward(
        heads, heads, triple, patch_row, grad_keep, grad_got, mixed, logs, first=(weights_mine,)
    )
    layer_send = layer_grad(1, grad_first, grad_second, turned, far, BF)
    layer_got = swap(layer_send, 1)
    layer_part = layer_grad(0, grad_first, grad_second, turned, far, F32, first=(layer_send,))
    conv_grad, points0, near_rows, far_rows, cpe_low, sums_one = third_rows(
        plan, place_of, layer_part, layer_got, carried, normed_one, scaling_one, normed_cpe, scaling_cpe, small, cpe_weight, firsts, (block1, block_far)
    )
    grad0 = conv_grad
    grad2 = swap(grad0, 2)
    grad1 = swap(grad0, 1)
    second_mine, second_theirs = fold(weights_mine, weights_far, *halves(shard_count, 0))
    second = Scatter(second_mine, second_theirs, shard_count, 0)
    spread0 = spread(0, (0, 1), place_of, lookup, kernel_rows, grad0, first=(weights_far,), time=TINY)
    cpe_send, cpe_keep, small_keep = cpe_weights(
        shard_count, place_of, conv_low, cpe_low, sums_one, sums_two, sum_hidden_bias, first=(spread0,)
    )
    cpe_got = swap(cpe_send, 1)
    third_mine, third_far = third_weights(
        place_of, shard_count, grad_first, grad_second, layer_one, other_one, cpe_keep, cpe_got, small_keep,
        first=(spread0, grad2, second.got),
    )
    grad3 = swap(after(grad2, cpe_send), 1)

    gathered = (gathered0, gathered1, gathered2, gathered3)
    grads = (grad0, grad1, grad2, grad3)
    chunk = KERNEL // 3 * width
    third_far = swap(after(third_far, grad2), 2)
    piece0, theirs0 = conv_weight_grad(
        place_of, gathered, grads, 0, chunk, shard_count, 0, first=(third_mine,)
    )
    sum0 = Scatter(piece0, theirs0, shard_count, 0)
    second_sent = second.advance(piece0)
    spread1 = spread(1, (0, 1), place_of, lookup, kernel_rows, grad1, first=(piece0, second_sent), time=TINY)
    piece1, theirs1 = conv_weight_grad(
        place_of, gathered, grads, chunk, chunk, shard_count, 0, thirds=(third_mine, third_far), first=(spread1,)
    )
    sum1 = Scatter(piece1, theirs1, shard_count, 0)
    sent = sum0.advance(piece1)
    piece2, theirs2 = conv_weight_grad(
        place_of, gathered, grads, 2 * chunk, chunk, shard_count, 0, first=(piece1, sent)
    )
    sum2 = Scatter(piece2, theirs2, shard_count, 0)
    spread2 = spread(2, (0,), place_of, lookup, kernel_rows, grad2, first=(piece2,), time=BLOCK)
    far_rows = swap(after(far_rows, piece2), 2)
    near_rows = swap(after(near_rows, piece2), 1)
    sent = sum0.advance(spread2)
    second_sent = second.advance(spread2)
    spread2_after = spread(2, (1,), place_of, lookup, kernel_rows, grad2, first=(spread2, sent, second_sent), time=BLOCK)
    spread3 = spread(3, (0,), place_of, lookup, kernel_rows, grad3, first=(spread2_after,), time=BLOCK)
    sent = sum1.advance(spread3)
    spread3_after = spread(3, (1,), place_of, lookup, kernel_rows, grad3, first=(spread3, sent, sum0.got, second.got), time=BLOCK)

    sent = sum2.advance(spread3_after)
    second = second.finish()
    grad_hidden, grad_output, grad_proj = second_out(second.mine, second.got, wide)
    grad_padded, to_below, to_above = finish(
        place_of, (spread0, spread1, spread2, spread2_after, spread3, spread3_after), first=(sent, grad_hidden)
    )
    cross_rows = swap(after(far_rows, spread3), 1)
    from_above = lax.ppermute(to_below, "pts", downs)
    from_below = lax.ppermute(to_above, "pts", ups)
    sent = sum1.advance(grad_padded)
    sent = sum2.advance(sent)
    block_out, grad_points = rows_out(
        place_of, grad_padded, from_below, from_above, block0, points0, near_rows, far_rows, cross_rows,
        first=(sent,),
    )

    grad_conv, grad_cpe, grad_qkv, *lines = grads_out([s.finish() for s in (sum0, sum1, sum2)], chunk, width)
    small = [line.reshape(-1) for line in lines[: VECTORS + 1]]
    return (
        block_out,
        grad_points,
        grad_conv.transpose(0, 2, 1),
        small[0],
        grad_cpe.T,
        *small[1:6],
        grad_qkv.transpose(1, 0, 2),
        lines[VECTORS + 1],
        grad_proj.T,
        small[8],
        small[6],
        small[7],
        grad_hidden,
        small[10],
        grad_output.T,
        small[9],
    )


def solution(mesh):
    return jax.shard_map(
        shards,
        mesh=mesh,
        in_specs=(
            P("pts", "blk"),
            P("pts", None),
            P("pts"),
            P(None, "blk", None),
            P("blk"),
            P("blk", None),
            P("blk"),
            P("blk"),
            P("blk"),
            P("blk"),
            P("blk"),
            P(None, None, "blk"),
            P(None, "blk"),
            P("blk", None),
            P("blk"),
            P("blk"),
            P("blk"),
            P(None, "blk"),
            P("blk"),
            P("blk", None),
            P("blk"),
            P("pts", "blk"),
        ),
        out_specs=(
            P("pts", "blk"),
            P("pts", "blk"),
            P(None, "blk", "pts"),
            P("blk"),
            P("blk", "pts"),
            P("blk"),
            P("blk"),
            P("blk"),
            P("blk"),
            P("blk"),
            P("pts", None, "blk"),
            P(None, "blk"),
            P("blk", "pts"),
            P("blk"),
            P("blk"),
            P("blk"),
            P("pts", "blk"),
            P("blk"),
            P("blk", "pts"),
            P("blk"),
        ),
        check_vma=False,
    )
```

```python
import functools
import math

import jax
import jax.numpy as jnp
from jax import lax
from jax.experimental import pallas as pl
from jax.experimental.pallas import tpu as pltpu
from jax.sharding import PartitionSpec as P

HEAD_DIM = 16
PATCH = 1024
KERNEL = 27
REACH = 256
EPS = 1e-05
LOG2E = math.log2(math.e)
BF = jnp.bfloat16
F32 = jnp.float32
NN = ((1,), (0,))
NT = ((1,), (1,))
TN = ((0,), (0,))
VMEM = pl.BlockSpec(memory_space=pltpu.VMEM)
SMEM = pl.BlockSpec(memory_space=pltpu.SMEM)
HBM = pl.BlockSpec(memory_space=pltpu.HBM)
ANY = pl.BlockSpec(memory_space=pl.ANY)
TILE = 256


def dot(a, b, dims):
    return lax.dot_general(a, b, (dims, ((), ())), preferred_element_type=F32)


def struct(shape, kind):
    return jax.ShapeDtypeStruct(shape, kind)


TIMES = {
    "prepare": 10,  "conv_forward": 7.5, "first_rows": 2.5, "triple_half": 2, "attend_forward": 21, "second_rows": 10,
    "second_send": 1.5, "attend_backward": 19, "second_keep": 2.5, "layer_grad": 1, "third_rows": 2.3, "cpe_weights": 0.1,
    "spread": 7, "third_weights": 0.1, "conv_weight_grad": 0.1, "finish": 1.0, "rows_out": 2.0, "fold": 0.05, "second_out": 0.1, "grads_out": 0.1,
}
FACTOR = 0.3
TINY = 0.1
BLOCK = 4.2


def call(name, kernel, inputs, outputs, scratch=(), mib=8, grid=None, first=(), time=None):
    count, extra = len(inputs), len(first)

    def body(*refs):
        kernel(*refs[:count], *refs[count + extra :])

    options = {} if grid is None else {"grid": grid}
    result = pl.pallas_call(
        body,
        out_shape=[o for o, spec in outputs],
        in_specs=[spec for a, spec in inputs] + [ANY] * extra,
        out_specs=[spec for o, spec in outputs],
        scratch_shapes=list(scratch),
        compiler_params=pltpu.CompilerParams(vmem_limit_bytes=mib * 2**20),
        cost_estimate=pl.CostEstimate(flops=int((time or TIMES[name]) * FACTOR * 1.15e9), bytes_accessed=0, transcendentals=0),
        name=name,
        **options,
    )(*[pltpu.with_memory_space_constraint(a, pltpu.HBM) if spec is HBM else a for a, spec in inputs], *first)
    return result[0] if len(result) == 1 else result


def vm(*arrays):
    return [(a, VMEM) for a in arrays]


def split3(values):
    high = values.astype(BF)
    rest = values - high.astype(F32)
    middle = rest.astype(BF)
    return high, middle, (rest - middle.astype(F32)).astype(BF)


def joined(rows, width):
    rows = rows.astype(F32)
    return (rows[:, :width] + rows[:, width : 2 * width]) + rows[:, 2 * width : 3 * width]


def in_order(pieces, me):
    core, chip = (me & 1) == 1, (me >> 1) == 1
    a, b = jnp.where(core, pieces[1], pieces[0]), jnp.where(core, pieces[0], pieces[1])
    c, d = jnp.where(core, pieces[3], pieces[2]), jnp.where(core, pieces[2], pieces[3])
    return [
        jnp.where(chip, c, a),
        jnp.where(chip, d, b),
        jnp.where(chip, a, c),
        jnp.where(chip, b, d),
    ]


def folded(source, start, target, row, sems, rows):
    part, width = rows // 4, source.shape[1]
    copies = []
    for j in range(4):
        copies.append(
            pltpu.make_async_copy(
                source.at[pl.ds(pl.multiple_of(start + j * part, 16), part), :],
                target.at[row : row + part, j * width : (j + 1) * width],
                sems(),
            )
        )
    return copies


def unfolded(pack, row, at, rows):
    part, width = rows // 4, pack.shape[1] // 4
    return jnp.concatenate(
        [
            pack[row : row + part, j * width : (j + 1) * width]
            for j in range(at.start // part, at.stop // part)
        ],
        axis=0,
    )


class Plan:
    def __init__(self, rows, width):
        fold = rows // 4
        self.first_cpe = 3 * width
        self.first_points = 4 * width
        self.first_small = 4 * width + 2 * fold
        self.first_rows = self.first_small + 16
        self.near_points = width
        self.near_small = width + fold
        self.near_rows = self.near_small + 16


def counter(sems):
    state = [0]

    def take():
        state[0] += 1
        return sems.at[state[0] - 1]

    return take


VECTORS = 10


def prepare_kernel(
    plan, rows, place_of, turned_in, cpe, points, patch, *refs
):
    vectors, refs = refs[:VECTORS], refs[VECTORS:]
    hidden_bias, query_bias, away, near, turned, small, patch_row, terms, lines, long_line, pair, straight, sems = refs
    me = place_of[0]
    width = points.shape[1]
    take = counter(sems)
    copies = [
        pltpu.make_async_copy(cpe, away.at[plan.first_cpe : plan.first_cpe + width, :], take()),
        pltpu.make_async_copy(cpe, near.at[0:width, :], take()),
    ]
    for e in (2, 3):
        copies += folded(points, (me ^ e) * rows, away, plan.first_points + (e - 2) * rows // 4, take, rows)
    copies += folded(points, (me ^ 1) * rows, near, plan.near_points, take, rows)
    straight_copy = pltpu.make_async_copy(turned_in, straight, take())
    straight_copy.start()
    for copy in copies:
        copy.start()
    loads = [pltpu.make_async_copy(vector, lines.at[r], take()) for r, vector in enumerate(vectors)]
    loads.append(pltpu.make_async_copy(hidden_bias, long_line, take()))
    loads.append(pltpu.make_async_copy(query_bias, pair, take()))
    for copy in loads:
        copy.start()
    for e in (0, 1):
        at = pl.ds(pl.multiple_of((me ^ e) * rows, rows), rows)
        loads.append(pltpu.make_async_copy(patch.at[:, at], patch_row.at[:, e * rows : (e + 1) * rows], take()))
        loads[-1].start()
    straight_copy.wait()
    for t in range(3):
        turned[t * width : (t + 1) * width, :] = straight[t].T
    for copy in loads:
        copy.wait()
    for r in range(VECTORS):
        small[r : r + 1, :] = lines[r]
    for i in range(4):
        small[VECTORS + i : VECTORS + i + 1, :] = long_line[:, i * width : (i + 1) * width]
    small[VECTORS + 4 :, :] = pair[...]
    high, middle, low = split3(small[...])
    terms[...] = jnp.concatenate([high, middle, low, jnp.zeros_like(low)], axis=1)
    last = [
        pltpu.make_async_copy(turned, away.at[0 : 3 * width, :], take()),
        pltpu.make_async_copy(terms, away.at[plan.first_small :, :], take()),
        pltpu.make_async_copy(terms, near.at[plan.near_small :, :], take()),
    ]
    for copy in last:
        copy.start()
    for copy in copies + last:
        copy.wait()


def prepare(plan, place_of, turned, cpe, points, patch, vectors, hidden_bias, query_bias, first=()):
    row_count, width = points.shape
    wide = cpe.shape[1]
    lines = [v.reshape(1, -1) for v in (*vectors, hidden_bias)]
    return call(
        "prepare",
        functools.partial(prepare_kernel, plan, row_count // 4),
        [(place_of, SMEM), (turned, HBM), (cpe, HBM), (points, HBM), (patch.reshape(1, -1), HBM)]
        + [(v, HBM) for v in (*lines, query_bias)],
        [
            (struct((plan.first_rows, wide), BF), HBM),
            (struct((plan.near_rows, wide), BF), HBM),
            (struct((3 * width, wide), BF), VMEM),
            (struct((16, width), F32), VMEM),
            (struct((1, row_count // 2), jnp.int32), VMEM),
        ],
        [
            pltpu.VMEM((16, wide), BF),
            pltpu.VMEM((VECTORS, 1, width), F32),
            pltpu.VMEM((1, 4 * width), F32),
            pltpu.VMEM((2, width), F32),
            pltpu.VMEM(turned.shape, BF),
            pltpu.SemaphoreType.DMA((17 + VECTORS + 5,)),
        ],
        first=first,
    )


def one_hot(place):
    spots = lax.broadcasted_iota(jnp.int32, (256, 256), 0).astype(F32).astype(BF)
    place = jnp.broadcast_to(place.astype(F32).astype(BF), (256, 256))
    return jnp.where(spots == place, jnp.ones((), BF), jnp.zeros((), BF))


def conv_kernel(e, packs, place_of, low, points, high, lookup, weight, *refs):
    sources, refs = refs[:packs], refs[packs:]
    conv, conv_after, gathered = refs[:3]
    away, near = refs[3:5] if packs else (None, None)
    turned, picked, sems = refs[-3:]
    me = place_of[0]
    width = points.shape[1]
    rows = picked.shape[1]
    quarter = me ^ e
    take = counter(sems)
    copies = []
    if packs:
        hidden, output, proj, upstream = sources
        wide, fold = hidden.shape[1], rows // 4
        start = 2 * wide + width
        for target in (away, near):
            copies.append(pltpu.make_async_copy(output, target.at[0:wide, :], take()))
            copies.append(pltpu.make_async_copy(proj, target.at[wide : wide + width, :], take()))
            copies.append(pltpu.make_async_copy(hidden, target.at[wide + width : start, :], take()))
        copies += folded(upstream, (me ^ 2) * rows, away, start, take, rows)
        copies += folded(upstream, (me ^ 3) * rows, away, start + fold, take, rows)
        copies += folded(upstream, (me ^ 1) * rows, near, start, take, rows)
        for copy in copies:
            copy.start()
    base = place_of[1] * points.shape[0] + quarter * rows - REACH
    last = points.shape[0] // 256 - 1
    for j in range(rows // 256 + 2):
        spot = quarter * (rows // 256) - 1 + j
        at = pl.multiple_of(jnp.clip(spot, 0, last) * 256, 256)
        piece = points[pl.ds(at, 256), :]
        piece = jnp.where(spot < 0, low[...], jnp.where(spot > last, high[...], piece))
        turned[j * width : (j + 1) * width, :] = piece.T
    step = KERNEL // 3
    for b in range(rows // 256):
        cols = slice(b * 256, (b + 1) * 256)
        left = turned[b * width : (b + 3) * width, :]
        for k in range(KERNEL):
            spot = lookup[k : k + 1, pl.ds(pl.multiple_of(quarter * rows + b * 256, 256), 256)] - base
            part = jnp.broadcast_to(lax.shift_right_logical(spot, 8) - b, (width, 256))
            three = dot(left, one_hot(jnp.bitwise_and(spot, 255)), NN)
            values = jnp.where(
                part == 0,
                three[:width],
                jnp.where(part == 1, three[width : 2 * width], three[2 * width :]),
            )
            picked[k * width : (k + 1) * width, cols] = values.astype(BF)
            if k % step == step - 1:
                at = slice((k + 1 - step) * width, (k + 1) * width)
                copies.append(pltpu.make_async_copy(picked.at[at, cols], gathered.at[at, cols], take()))
                copies[-1].start()
        (conv, conv_after)[b][...] = dot(picked[:, cols], weight[...], TN).astype(conv.dtype)
    for copy in copies:
        copy.wait()


def conv_forward(e, place_of, low, points, high, lookup, weight, kind, packs=(), first=(), time=None):
    rows, width, wide = points.shape[0] // 4, points.shape[1], weight.shape[1]
    outputs = [(struct((rows // 2, wide), kind), VMEM)] * 2 + [(struct((KERNEL * width, rows), BF), HBM)]
    if packs:
        size = 2 * wide + width + rows // 4
        outputs += [(struct((size + rows // 4, wide), BF), HBM), (struct((size, wide), BF), HBM)]
    return call(
        "conv_forward",
        functools.partial(conv_kernel, e, len(packs)),
        [(place_of, SMEM)] + vm(low, points, high, lookup, weight) + [(p, HBM) for p in packs],
        outputs,
        [
            pltpu.VMEM(((rows // 256 + 2) * width, 256), BF),
            pltpu.VMEM((KERNEL * width, rows), BF),
            pltpu.SemaphoreType.DMA((6 * rows // 512 + (18 if packs else 0),)),
        ],
        first=first,
        time=time,
    )


def spread_kernel(e, blocks, place_of, lookup, weight, grads, out, upstream):
    width = out.shape[0]
    rows = grads.shape[0]
    quarter = place_of[0] ^ e
    base = place_of[1] * lookup.shape[1] + quarter * rows - REACH
    out[...] = jnp.zeros(out.shape, F32)
    step = 9
    for n, b in enumerate(blocks):
        cols = slice(b * 256, (b + 1) * 256)
        upstream[...] = dot(weight[...], grads[cols, :], NT)
        for s in range(KERNEL // step):
            left, right = [], []
            for k in range(s * step, (s + 1) * step):
                spot = lookup[k : k + 1, pl.ds(pl.multiple_of(quarter * rows + b * 256, 256), 256)] - base
                part = jnp.broadcast_to(lax.shift_right_logical(spot, 8) - b, (width, 256))
                mine = upstream[k * width : (k + 1) * width, :]
                left.append(
                    jnp.concatenate(
                        [jnp.where(part == i, mine, 0.0).astype(BF) for i in range(3)], axis=0
                    )
                )
                right.append(one_hot(jnp.bitwise_and(spot, 255)))
            three = dot(jnp.concatenate(left, axis=1), jnp.concatenate(right, axis=1), NT)
            for i in range(3):
                at = slice((n + i) * 256, (n + i + 1) * 256)
                out[:, at] = out[:, at] + three[i * width : (i + 1) * width]


def spread(e, blocks, place_of, lookup, weight, grads, first=(), time=None):
    width = weight.shape[0] // KERNEL
    return call(
        "spread",
        functools.partial(spread_kernel, e, blocks),
        [(place_of, SMEM)] + vm(lookup, weight, grads),
        [(struct((width, 256 * len(blocks) + 2 * REACH), F32), VMEM)],
        [pltpu.VMEM((KERNEL * width, 256), F32)],
        first=first,
        time=time,
    )


def halves(count, stage):
    keep = [r for r in range(count) if not (r >> stage) & 1]
    return keep, [r ^ (1 << stage) for r in keep]


def conv_weight_kernel(blocks, stage, start, count, extra, place_of, *refs):
    gathered, grads, refs = refs[:4], refs[4:8], refs[8:]
    thirds, (mine, theirs, total) = refs[:extra], refs[extra:]
    tile = 384
    for i in range(count // tile):
        rows = slice(start + i * tile, start + (i + 1) * tile)
        cols = slice(i * tile, (i + 1) * tile)
        total[:, cols] = sum(dot(a[rows, :], g[...], NN) for a, g in zip(gathered, grads)).T.astype(BF)
    size = total.shape[0] // blocks
    for out, slots in zip((mine, theirs), halves(blocks, stage)):
        for i, r in enumerate(slots):
            at = pl.multiple_of((place_of[1] ^ r) * size, size)
            out[i, :, 0:count] = total[pl.ds(at, size), :]
            if extra:
                out[i, :, count:] = (thirds[0][r].astype(F32) + thirds[1][r].astype(F32)).astype(BF)


def conv_weight_grad(place_of, gathered, grads, start, count, blocks, stage, thirds=(), first=()):
    wide = grads[0].shape[1]
    cols = count + (thirds[0].shape[2] if thirds else 0)
    half = struct((blocks // 2, wide // blocks, cols), BF)
    return call(
        "conv_weight_grad",
        functools.partial(conv_weight_kernel, blocks, stage, start, count, len(thirds)),
        [(place_of, SMEM)] + vm(*gathered, *grads, *thirds),
        vm(half, half),
        [pltpu.VMEM((wide, count), BF)],
        first=first,
    )


def finish_kernel(place_of, s0, s1, s2, s2_after, s3, s3_after, out, low, high):
    me = place_of[0]
    rows = s0.shape[1] - 2 * REACH
    ends = [s[:, 0:256] for s in (s0, s1, s2, s3)], [s[:, 768:] for s in (s0, s1)] + [s[:, 512:] for s in (s2_after, s3_after)]
    inner = [
        [s[:, 256:512] for s in (s0, s1)]
        + [a[:, 256:512] + b[:, 0:256] for a, b in ((s2, s2_after), (s3, s3_after))],
        [s[:, 512:768] for s in (s0, s1)]
        + [a[:, 512:768] + b[:, 256:512] for a, b in ((s2, s2_after), (s3, s3_after))],
    ]
    parts = [in_order(p, me) for p in (ends[0], inner[0], inner[1], ends[1])]
    out[...] = jnp.zeros(out.shape, F32)
    for q in range(4):
        for i, part in enumerate(parts):
            at = slice(q * rows + i * 256, q * rows + (i + 1) * 256)
            out[:, at] = out[:, at] + part[q]
    low[...] = out[:, :REACH].astype(BF)
    high[...] = out[:, out.shape[1] - REACH :].astype(BF)


def finish(place_of, spreads, first=()):
    width, span = spreads[0].shape
    total = 4 * (span - 2 * REACH) + 2 * REACH
    return call(
        "finish",
        finish_kernel,
        [(place_of, SMEM)] + vm(*spreads),
        [(struct((width, total), F32), VMEM)] + [(struct((width, REACH), BF), VMEM)] * 2,
        first=first,
    )


def rows_out_kernel(place_of, inside, below, above, block, own, near, far, cross, block_out, out):
    rows, width = own.shape
    me = place_of[0]
    pieces = in_order([block[...], near[:, :width], far[:, :width], cross[:, width : 2 * width]], me)
    for q in range(4):
        block_out[q * rows : (q + 1) * rows, :] = pieces[q]
    pieces = [own[...], near[:, width:], far[:, 2 * width : 3 * width], cross[:, 3 * width :]]
    pieces = in_order(pieces, me)
    for q in range(4):
        total = inside[:, REACH + q * rows : REACH + (q + 1) * rows].T + pieces[q].astype(F32)
        out[q * rows : (q + 1) * rows, :] = total
    out[:REACH, :] = out[:REACH, :] + below[...].astype(F32).T
    last = out.shape[0] - REACH
    out[last:, :] = out[last:, :] + above[...].astype(F32).T


def rows_out(place_of, inside, below, above, block, own, near, far, cross, first=()):
    rows, width = own.shape
    return call(
        "rows_out",
        rows_out_kernel,
        [(place_of, SMEM)] + vm(inside, below, above, block, own, near, far, cross),
        vm(struct((4 * rows, width), BF), struct((4 * rows, width), F32)),
        first=first,
    )


def three_rows(high, middle, low):
    spots = lax.broadcasted_iota(jnp.int32, (16, high.shape[1]), 0)
    picked = jnp.where(
        spots == 0,
        high.astype(F32),
        jnp.where(spots == 1, middle.astype(F32), jnp.where(spots == 2, low.astype(F32), 0.0)),
    )
    return picked.astype(BF)


def one_rows(length, count):
    spots = lax.broadcasted_iota(jnp.int32, (16, length), 0)
    return jnp.where(spots < count, 1.0, 0.0).astype(BF)


def patch_codes(patch):
    shape = (32, patch.shape[1])
    spots = lax.broadcasted_iota(jnp.int32, shape, 0)
    bits = jnp.bitwise_and(
        lax.shift_right_logical(jnp.broadcast_to(patch, shape), jnp.bitwise_and(spots, 15)), 1
    )
    bits = jnp.where(spots < 16, bits, 1 - bits)
    return jnp.where(bits == 1, 1.0, 0.0).astype(BF), jnp.where(bits == 1, 0.0, -1e30).astype(BF)


def fixed_rows(patch, query_side, key_side):
    length = patch.shape[1]
    left, right = patch_codes(patch)
    key_side[48:64, :] = one_rows(length, 3)
    key_side[64:96, :] = left
    query_side[64:96, :] = right
    key_side[96:128, :] = jnp.zeros((32, length), BF)
    query_side[96:128, :] = jnp.zeros((32, length), BF)


def column(row):
    return jnp.broadcast_to(row, (128, 128)).T[:, 0:1]


def triple_rows(values, weights, smalls, out, cols):
    width = out.shape[1] // 2
    for t in range(3):
        for i in range(2):
            piece = dot(weights[i][t * width : (t + 1) * width, :], values, NT)
            if t != 1:
                piece = piece + column(smalls[i][14 + t // 2 : 15 + t // 2, :])
            out[t, i * width : (i + 1) * width, cols] = piece.astype(BF)


def triple_half_kernel(plan, values, turned, away, small, out):
    smalls = (small[...], joined(away[plan.first_small :, :], small.shape[1]))
    triple_rows(values[...], (turned, away), smalls, out, slice(0, values.shape[0]))


def triple_half(plan, values, turned, away, small):
    return call(
        "triple_half",
        functools.partial(triple_half_kernel, plan),
        vm(values, turned, away, small),
        [(struct((3, 2 * small.shape[1], values.shape[0]), BF), VMEM)],
    )


def attend_forward_kernel(
    plan, heads, tile, mine, other, turned, away, small, patch, triple, total, keep, send, logs, query_side, key_side, value_side
):
    rows = mine.shape[2]
    length = 2 * rows
    for t in range(3):
        triple[t, :, :rows] = mine[t]
    smalls = (small[...], joined(away[plan.first_small :, :], small.shape[1]))
    triple_rows(other[...], (turned, away), smalls, triple, slice(rows, length))
    fixed_rows(patch[...], query_side, key_side)
    value_side[16:32, :] = one_rows(length, 1)

    @pl.loop(0, heads)
    def _(h):
        at = pl.ds(pl.multiple_of(h * HEAD_DIM, HEAD_DIM), HEAD_DIM)
        query = triple[0, at, :].astype(F32) * (HEAD_DIM**-0.5 * LOG2E)
        key = triple[1, at, :]
        high, middle, low = split3(query)
        query_side[0:16, :] = high
        query_side[16:32, :] = middle
        query_side[32:48, :] = low
        query_side[48:64, :] = jnp.zeros((16, length), BF)
        key_side[0:16, :] = key
        key_side[16:32, :] = key
        key_side[32:48, :] = key
        value_side[0:16, :] = triple[2, at, :]
        wide_key = key.astype(F32)
        bound = jnp.max(jnp.sum(query * query, axis=0)) * jnp.max(
            jnp.sum(wide_key * wide_key, axis=0)
        )
        logs[pl.ds(h, 1), :] = jnp.zeros((1, length), F32)

        @pl.when(jnp.logical_not(bound < 4096.0))
        def _():
            for t in range(length // tile):
                cols = slice(t * tile, (t + 1) * tile)
                top = jnp.max(dot(key_side[...], query_side[:, cols], TN), axis=0, keepdims=True)
                query_side[48:64, cols] = three_rows(*split3(-top))
                logs[pl.ds(h, 1), cols] = top

        for t in range(length // tile):
            cols = slice(t * tile, (t + 1) * tile)
            weights = jnp.exp2(dot(key_side[...], query_side[:, cols], TN)).astype(BF)
            mixed = dot(value_side[...], weights, NN)
            sums = mixed[16:17, :]
            mixed = mixed[0:16, :] * (1.0 / sums)
            total[at, cols] = mixed
            if t * tile < rows:
                keep[at, cols] = mixed.astype(BF)
            else:
                send[at, t * tile - rows : (t + 1) * tile - rows] = mixed.astype(BF)
            logs[pl.ds(h, 1), cols] = logs[pl.ds(h, 1), cols] + jnp.log2(sums)


def attend_forward(plan, mine, other, turned, away, small, patch, first=()):
    width, rows = mine.shape[1:]
    length = 2 * rows
    heads = width // HEAD_DIM
    return call(
        "attend_forward",
        functools.partial(attend_forward_kernel, plan, heads, 512),
        vm(mine, other, turned, away, small, patch),
        [
            (struct((3, width, length), BF), VMEM),
            (struct((width, length), F32), VMEM),
            (struct((width, rows), BF), VMEM),
            (struct((width, rows), BF), VMEM),
            (struct((heads, length), F32), VMEM),
        ],
        [
            pltpu.VMEM((128, length), BF),
            pltpu.VMEM((128, length), BF),
            pltpu.VMEM((32, length), BF),
        ],
        first=first,
    )


def attend_backward_kernel(
    first, heads, tile, triple, patch, mine, other, mixed, logs, out, query_side, key_side, value_side, grad_side, grad_value, grad_key
):
    length = triple.shape[2]
    fixed_rows(patch[...], query_side, key_side)
    value_side[16:32, :] = one_rows(length, 3)

    @pl.loop(0, heads)
    def _(h):
        at = pl.ds(pl.multiple_of((h + first) * HEAD_DIM, HEAD_DIM), HEAD_DIM)
        to = pl.ds(pl.multiple_of(h * HEAD_DIM, HEAD_DIM), HEAD_DIM)
        query, key = triple[0, at, :], triple[1, at, :]
        upstream = jnp.concatenate([mine[at, :], other[at, :]], axis=1)
        high, middle, low = split3(query.astype(F32) * (HEAD_DIM**-0.5 * LOG2E))
        query_side[0:16, :] = high
        query_side[16:32, :] = middle
        query_side[32:48, :] = low
        query_side[48:64, :] = three_rows(*split3(-logs[pl.ds(h + first, 1), :]))
        key_side[0:16, :] = key
        key_side[16:32, :] = key
        key_side[32:48, :] = key
        value_side[0:16, :] = triple[2, at, :]
        inner = jnp.sum(upstream.astype(F32) * mixed[at, :], axis=0, keepdims=True)
        grad_side[0:16, :] = upstream
        grad_side[16:32, :] = three_rows(*split3(-inner))
        for t in range(length // tile):
            cols = slice(t * tile, (t + 1) * tile)
            prob = jnp.exp2(dot(query_side[:, cols], key_side[...], TN))
            grad_prob = dot(grad_side[:, cols], value_side[...], TN)
            grad_score = (prob * grad_prob).astype(BF)
            value_part = dot(upstream[:, cols], prob.astype(BF), NN)
            key_part = dot(query[:, cols], grad_score, NN)
            out[0, to, cols] = (dot(key, grad_score, NT) * HEAD_DIM**-0.5).astype(BF)
            if t == 0:
                grad_value[...] = value_part
                grad_key[...] = key_part
            else:
                grad_value[...] += value_part
                grad_key[...] += key_part
        out[1, to, :] = (grad_key[...] * HEAD_DIM**-0.5).astype(BF)
        out[2, to, :] = grad_value[...].astype(BF)


def attend_backward(first_head, heads, triple, patch, mine, other, mixed, logs, first=()):
    length = triple.shape[2]
    return call(
        "attend_backward",
        functools.partial(attend_backward_kernel, first_head, heads, 512),
        vm(triple, patch, mine, other, mixed, logs),
        [(struct((3, heads * HEAD_DIM, length), BF), VMEM)],
        [
            pltpu.VMEM((128, length), BF),
            pltpu.VMEM((128, length), BF),
            pltpu.VMEM((32, length), BF),
            pltpu.VMEM((32, length), BF),
            pltpu.VMEM((16, length), F32),
            pltpu.VMEM((16, length), F32),
        ],
        mib=12,
        first=first,
    )


def norm_rows(values):
    average = jnp.mean(values, axis=1, keepdims=True)
    scaling = lax.rsqrt(
        jnp.mean(values * values, axis=1, keepdims=True) - average * average + EPS
    )
    return (values - average) * scaling, scaling


def norm_rows_back(upstream, normed, scaling, gain):
    scaled = upstream * gain
    return scaling * (
        scaled
        - jnp.mean(scaled, axis=1, keepdims=True)
        - normed * jnp.mean(scaled * normed, axis=1, keepdims=True)
    )


def cut(values):
    width = values.shape[1] // 4
    return [values[:, j * width : (j + 1) * width] for j in range(4)]


def add_rows(ref, row, values, first):
    total = jnp.sum(values, axis=0, keepdims=True)
    ref[row : row + 1, :] = total if first else ref[row : row + 1, :] + total


def small_vectors(plan, small, near, far, cross):
    width = small.shape[1]
    return [
        small[...],
        joined(near[plan.near_small :, :], width),
        joined(far[plan.first_small :, :], width),
        joined(cross[plan.first_small :, :], width),
    ]


def vectors(smalls, me):
    return jnp.concatenate(in_order(smalls, me), axis=1)


def cpe_rows(plan, weight, near, far, cross, me):
    width = weight.shape[0]
    at = slice(plan.first_cpe, plan.first_cpe + width)
    pieces = [weight[...], near[:width, :], far[at, :], cross[at, :]]
    return jnp.concatenate(in_order(pieces, me), axis=0)


def own_rows(ref, me, rows, at):
    return ref[pl.ds(pl.multiple_of(me * rows + at.start, at.stop - at.start), at.stop - at.start), :]


def first_rows_kernel(
    plan, place_of, part_low, part_high, close_low, close_high, away, points, small, weight, near, far, cross,
    layer, middle, normed_cpe, scaling_cpe, residual, normed, scaling,
):
    me = place_of[0]
    rows = 2 * part_low.shape[0]
    vec = vectors(small_vectors(plan, small, near, far, cross), me)
    vec = [vec[r : r + 1, :] for r in range(6)]
    weights = cpe_rows(plan, weight, near, far, cross, me)
    for t in range(rows // TILE):
        at = slice(t * TILE, (t + 1) * TILE)
        part, close = ((part_low, close_low), (part_high, close_high))[t * TILE * 2 // rows]
        low = (part[...] + close[...].astype(F32) + away[at, :].astype(F32) + vec[0]).astype(BF)
        middle[at, :] = low
        xhat, rate = norm_rows(dot(low, weights, NN) + vec[1])
        normed_cpe[at, :] = xhat
        scaling_cpe[at, :] = rate
        features = [
            own_rows(points, me, rows, at),
            unfolded(near, plan.near_points, at, rows),
            unfolded(far, plan.first_points, at, rows),
            unfolded(cross, plan.first_points + rows // 4, at, rows),
        ]
        features = jnp.concatenate(in_order(features, me), axis=1)
        sums = features.astype(F32) + xhat * vec[2] + vec[3]
        residual[at, :] = sums
        xhat, rate = norm_rows(sums)
        normed[at, :] = xhat
        scaling[at, :] = rate
        layer[at, :] = (xhat * vec[4] + vec[5]).astype(BF)


def first_rows(plan, place_of, parts, closes, away, points, small, weight, near, far, cross):
    rows, wide = away.shape
    full, thin, lower = struct((rows, wide), F32), struct((rows, 1), F32), struct((rows, wide), BF)
    return call(
        "first_rows",
        functools.partial(first_rows_kernel, plan),
        [(place_of, SMEM)] + vm(*parts, *closes, away, points, small, weight, near, far, cross),
        vm(lower, lower, full, thin, full, full, thin),
    )


def gelu_parts(u):
    scale = math.sqrt(2 / math.pi)
    square = u * u
    bent = jnp.tanh(u * (scale + (scale * 0.044715) * square))
    half = 0.5 + 0.5 * bent
    slope = half + u * (1.0 - bent * bent) * (0.5 * scale + (1.5 * 0.044715 * scale) * square)
    return u * half, slope


def second_rows_kernel(
    plan, place_of, keep, got, residual, out_grad, hidden, output, proj, small, near, far, cross, near2, far2, cross2,
    block0, block1, block_far, active, before, layer, upstream, carried, low, grad_keep, grad_send, hidden_sums, sums,
):
    me = place_of[0]
    rows, wide = residual.shape
    smalls = small_vectors(plan, small, near, far, cross)
    vec = vectors(smalls, me)
    vec = {r: vec[r : r + 1, :] for r in (6, 7, 8, 9)}
    biases = [jnp.concatenate([s[10 + i : 11 + i, :] for i in range(4)], axis=1) for s in smalls]
    width = keep.shape[0] // 2
    packs = (near2, far2, cross2)
    end = wide + width
    hiddens = [hidden] + [p.at[end : end + wide, :] for p in packs]
    last = end + wide
    outputs = [output] + [p.at[0:wide, :] for p in packs]
    projs = [proj[...]] + [p[wide:end, :] for p in packs]
    mine = jnp.concatenate([projs[0], projs[2]], axis=0)
    others = jnp.concatenate([projs[1], projs[3]], axis=0)
    for t in range(rows // TILE):
        at = slice(t * TILE, (t + 1) * TILE)
        base = residual[at, :] + vec[6] + dot(keep[:, at], mine, TN) + dot(got[:, at], others, TN)
        normed, scaling = norm_rows(base)
        lower = (normed * vec[7] + vec[8]).astype(BF)
        layer[at, :] = lower
        grads = [
            own_rows(out_grad, me, rows, at),
            unfolded(near2, last, at, rows),
            unfolded(far2, last, at, rows),
            unfolded(cross2, last + rows // 4, at, rows),
        ]
        grads = jnp.concatenate(in_order(grads, me), axis=1)
        upstream[at, :] = grads
        result = base + vec[9]
        grad_layer = None
        for e in range(4):
            act, slope = gelu_parts(dot(lower, hiddens[e][...], NN) + biases[e])
            act = act.astype(BF)
            active[e, at, :] = act
            result = result + dot(act, outputs[e][...], NN)
            pre = dot(grads, outputs[e][...], NT) * slope
            add_rows(hidden_sums, e, pre, t == 0)
            pre = pre.astype(BF)
            before[e, at, :] = pre
            piece = dot(pre, hiddens[e][...], NT)
            grad_layer = piece if e == 0 else grad_layer + piece
        result = in_order(cut(result.astype(BF)), me)
        block0[at, :] = result[0]
        block1[at, :] = result[1]
        block_far[at, 0:width] = result[2]
        block_far[at, width:] = result[3]
        wide_grads = grads.astype(F32)
        add_rows(sums, 0, grad_layer * normed, t == 0)
        add_rows(sums, 1, grad_layer, t == 0)
        add_rows(sums, 3, wide_grads, t == 0)
        carry = wide_grads + norm_rows_back(grad_layer, normed, scaling, vec[7])
        carried[at, :] = carry
        add_rows(sums, 2, carry, t == 0)
        carry = carry.astype(BF)
        low[at, :] = carry
        grad_keep[:, at] = dot(mine, carry, NT).astype(BF)
        grad_send[:, at] = dot(others, carry, NT).astype(BF)


def second_rows(plan, place_of, keep, got, residual, out_grad, weights, small, firsts, seconds):
    rows, wide = residual.shape
    lower, piece = struct((rows, wide), BF), struct((rows, wide // 4), BF)
    heads = struct(keep.shape, BF)
    return call(
        "second_rows",
        functools.partial(second_rows_kernel, plan),
        [(place_of, SMEM)] + vm(keep, got, residual, out_grad, *weights, small, *firsts, *seconds),
        vm(
            piece,
            piece,
            struct((rows, wide // 2), BF),
            struct((4, rows, wide), BF),
            struct((4, rows, wide), BF),
            lower,
            lower,
            struct((rows, wide), F32),
            lower,
            heads,
            heads,
            struct((4, wide), F32),
            struct((4, wide), F32),
        ),
        mib=12,
    )


def cut_rows(store, spot, cols, value, blocks):
    size = value.shape[0] // blocks
    for p in range(blocks):
        store(p ^ spot, cols, value[p * size : (p + 1) * size])


def second_weight_parts(i, e, blocks, spot, upstream, active, before, layer, low, attended, store):
    wide = layer.shape[1]
    width = attended.shape[0] // 2
    cut_rows(store, spot, slice(0, wide), dot(layer[...], before[e], TN), blocks)
    cut_rows(store, spot, slice(wide, 2 * wide), dot(upstream[...], active[e], TN), blocks)
    part = dot(attended[i * width : (i + 1) * width, :], low[...], NN)
    cut_rows(store, spot, slice(2 * wide, 2 * wide + width), part.T, blocks)


def second_send_kernel(blocks, place_of, upstream, active, before, layer, low, attended, out):
    for i, e in enumerate((1, 3)):

        def store(p, cols, value):
            out[i, p, :, cols] = value.astype(BF)

        second_weight_parts(i, e, blocks, place_of[1], upstream, active, before, layer, low, attended, store)


def second_send(place_of, blocks, upstream, active, before, layer, low, attended):
    wide = layer.shape[1]
    return call(
        "second_send",
        functools.partial(second_send_kernel, blocks),
        [(place_of, SMEM)] + vm(upstream, active, before, layer, low, attended),
        [(struct((2, blocks, wide // blocks, 2 * wide + attended.shape[0] // 2), BF), VMEM)],
    )


def second_keep_kernel(blocks, place_of, upstream, active, before, layer, low, attended, got, mine, far):
    for i, out in enumerate((mine, far)):

        def store(p, cols, value):
            out[p, :, cols] = (value + got[i, p, :, cols].astype(F32)).astype(BF)

        second_weight_parts(i, 2 * i, blocks, place_of[1], upstream, active, before, layer, low, attended, store)


def second_keep(place_of, blocks, upstream, active, before, layer, low, attended, got, first=()):
    out = struct(got.shape[1:], BF)
    return call(
        "second_keep",
        functools.partial(second_keep_kernel, blocks),
        [(place_of, SMEM)] + vm(upstream, active, before, layer, low, attended, got),
        vm(out, out),
        first=first,
    )


def third_weights_kernel(
    blocks, place_of, first_half, second_half, mine, other, cpe_keep, cpe_got, small_keep, own, far
):
    rows = mine.shape[0]
    width = first_half.shape[1]
    size = own.shape[1]
    empty = jnp.zeros((size - 16, width), BF)
    for i, (grads, out) in enumerate(((first_half, own), (second_half, far))):

        def store(p, cols, value):
            out[p, :, cols] = value.astype(BF)

        for t in range(3):
            part = dot(grads[t, :, :rows], mine[...], NN) + dot(grads[t, :, rows:], other[...], NN)
            cut_rows(store, place_of[1], slice(t * width, (t + 1) * width), part.T, blocks)
        sums = [jnp.sum(grads[t].astype(F32).T, axis=0, keepdims=True) for t in (0, 2)]
        small_got = sum(cpe_got[i, slot, size:, :].astype(F32) for slot in range(3))
        small = small_keep[i] + small_got + jnp.concatenate([jnp.zeros((14, width), F32)] + sums, axis=0)
        for p in range(blocks):
            out[p, :, 3 * width : 4 * width] = (
                cpe_keep[i, p].astype(F32) + cpe_got[i, p, :size, :].astype(F32)
            ).astype(BF)
            out[p, 0:16, 4 * width :] = small.astype(BF)
            if empty.shape[0]:
                out[p, 16:, 4 * width :] = empty


def third_weights(place_of, blocks, first_half, second_half, mine, other, cpe_keep, cpe_got, small_keep, first=()):
    wide = mine.shape[1]
    width = first_half.shape[1]
    out = struct((blocks, wide // blocks, 5 * width), BF)
    return call(
        "third_weights",
        functools.partial(third_weights_kernel, blocks),
        [(place_of, SMEM)] + vm(first_half, second_half, mine, other, cpe_keep, cpe_got, small_keep),
        vm(out, out),
        first=first,
    )


def layer_grad_kernel(half, first_half, second_half, turned, away, out):
    width = first_half.shape[1]
    rows = first_half.shape[2] // 2
    cols = slice(half * rows, (half + 1) * rows)
    total = None
    for t in range(3):
        at = slice(t * width, (t + 1) * width)
        for grads, weight in ((first_half, turned), (second_half, away)):
            piece = dot(grads[t, :, cols], weight[at, :], TN)
            total = piece if total is None else total + piece
    out[...] = total.astype(out.dtype)


def layer_grad(half, first_half, second_half, turned, away, kind, first=()):
    return call(
        "layer_grad",
        functools.partial(layer_grad_kernel, half),
        vm(first_half, second_half, turned, away),
        [(struct((first_half.shape[2] // 2, turned.shape[1]), kind), VMEM)],
        first=first,
    )


def third_rows_kernel(
    plan, place_of, part, close, carried, normed, scaling, normed_cpe, scaling_cpe, small, weight, near, far, cross, block1, block_far,
    conv_grad, points0, near_rows, far_rows, low, sums,
):
    me = place_of[0]
    vec = vectors(small_vectors(plan, small, near, far, cross), me)
    weights = cpe_rows(plan, weight, near, far, cross, me)
    width = points0.shape[1]
    for t in range(part.shape[0] // TILE):
        at = slice(t * TILE, (t + 1) * TILE)
        upstream = part[at, :] + close[at, :].astype(F32)
        xhat = normed[at, :]
        add_rows(sums, 4, upstream * xhat, t == 0)
        add_rows(sums, 5, upstream, t == 0)
        grads = carried[at, :] + norm_rows_back(upstream, xhat, scaling[at, :], vec[4:5, :])
        pieces = in_order(cut(grads.astype(BF)), me)
        points0[at, :] = pieces[0]
        near_rows[at, 0:width] = block1[at, :]
        near_rows[at, width:] = pieces[1]
        far_rows[at, 0 : 2 * width] = block_far[at, :]
        far_rows[at, 2 * width : 3 * width] = pieces[2]
        far_rows[at, 3 * width :] = pieces[3]
        xhat = normed_cpe[at, :]
        add_rows(sums, 2, grads * xhat, t == 0)
        add_rows(sums, 3, grads, t == 0)
        grads = norm_rows_back(grads, xhat, scaling_cpe[at, :], vec[2:3, :])
        add_rows(sums, 1, grads, t == 0)
        lower = grads.astype(BF)
        low[at, :] = lower
        result = dot(lower, weights, NT)
        add_rows(sums, 0, result, t == 0)
        conv_grad[at, :] = result.astype(BF)


def third_rows(plan, place_of, part, close, carried, normed, scaling, normed_cpe, scaling_cpe, small, weight, firsts, blocks):
    rows, wide = part.shape
    lower, piece = struct((rows, wide), BF), struct((rows, wide // 4), BF)
    return call(
        "third_rows",
        functools.partial(third_rows_kernel, plan),
        [(place_of, SMEM)]
        + vm(part, close, carried, normed, scaling, normed_cpe, scaling_cpe, small, weight, *firsts, *blocks),
        vm(lower, piece, struct((rows, wide // 2), BF), lower, lower, struct((6, wide), F32)),
    )


def cpe_weights_kernel(
    blocks, place_of, middle, low, sums_one, sums_two, hidden_sums, send, keep, small_keep, small_send
):
    me = place_of[0]
    width = middle.shape[1] // 4
    ones, twos = in_order(cut(sums_one[...]), me), in_order(cut(sums_two[...]), me)
    for e in range(4):
        out = (keep, send, keep, send)[e]

        def store(p, cols, value):
            out[e // 2, p, : value.shape[0], cols] = value.astype(BF)

        at = pl.ds(pl.multiple_of((e ^ me) * width, width), width)
        cut_rows(store, place_of[1], slice(0, width), dot(low[...], middle[:, at], TN), blocks)
        out = (small_keep, small_send, small_keep, small_send)[e]
        out[e // 2, 0:6, :] = ones[e]
        out[e // 2, 6:10, :] = twos[e]
        for i in range(4):
            out[e // 2, 10 + i : 11 + i, :] = hidden_sums[e : e + 1, i * width : (i + 1) * width]
        out[e // 2, 14:16, :] = jnp.zeros((2, width), F32)
    size = send.shape[2] - 16
    for i in range(2):
        for slot, term in enumerate(split3(small_send[i])):
            send[i, slot, size:, :] = term
        send[i, 3:, size:, :] = jnp.zeros((blocks - 3, 16, width), BF)


def cpe_weights(blocks, place_of, middle, low, sums_one, sums_two, hidden_sums, first=()):
    wide = middle.shape[1]
    send = struct((2, blocks, wide // blocks + 16, wide // 4), BF)
    keep = struct((2, blocks, wide // blocks, wide // 4), BF)
    small = (2, 16, wide // 4)
    return call(
        "cpe_weights",
        functools.partial(cpe_weights_kernel, blocks),
        [(place_of, SMEM)] + vm(middle, low, sums_one, sums_two, hidden_sums),
        vm(send, keep, struct(small, F32)),
        [pltpu.VMEM(small, F32)],
        first=first,
    )


def fold_kernel(keep, send, mine, got, kept, sent):
    for out, slots in ((sent, send), (kept, keep)):
        for i, j in enumerate(slots):
            out[i] = (mine[j].astype(F32) + got[j].astype(F32)).astype(BF)


def fold(mine, got, keep, send, first=()):
    out = struct((len(keep), *mine.shape[1:]), BF)
    return call("fold", functools.partial(fold_kernel, keep, send), vm(mine, got), vm(out, out), first=first)


def second_out_kernel(mine, got, hidden, output, proj):
    total = mine[0].astype(F32) + got[0].astype(F32)
    wide = hidden.shape[1]
    hidden[...] = total[:, :wide]
    output[...] = total[:, wide : 2 * wide]
    proj[...] = total[:, 2 * wide :]


def second_out(mine, got, wide):
    size, cols = mine.shape[1:]
    return call(
        "second_out",
        second_out_kernel,
        vm(mine, got),
        vm(struct((size, wide), F32), struct((size, wide), F32), struct((size, cols - 2 * wide), F32)),
    )


def grads_out_kernel(chunk, m0, g0, m1, g1, m2, g2, conv, cpe, qkv, *lines):
    width = cpe.shape[1]
    for i, (mine, got) in enumerate(((m0, g0), (m1, g1), (m2, g2))):
        part = mine[0, :, :chunk].astype(F32) + got[0, :, :chunk].astype(F32)
        for k in range(chunk // width):
            conv[i * (chunk // width) + k] = part[:, k * width : (k + 1) * width]
    third = m1[0, :, chunk:].astype(F32) + g1[0, :, chunk:].astype(F32)
    for t in range(3):
        qkv[t] = third[:, t * width : (t + 1) * width]
    cpe[...] = third[:, 3 * width : 4 * width]
    small = third[:16, 4 * width :]
    for r in range(VECTORS):
        lines[r][...] = small[r : r + 1, :]
    for i in range(4):
        lines[VECTORS][:, i * width : (i + 1) * width] = small[VECTORS + i : VECTORS + i + 1, :]
    lines[VECTORS + 1][...] = small[VECTORS + 4 :, :]


def grads_out(sums, chunk, width):
    size = sums[0].mine.shape[1]
    line = struct((1, width), F32)
    return call(
        "grads_out",
        functools.partial(grads_out_kernel, chunk),
        vm(*[a for s in sums for a in (s.mine, s.got)]),
        vm(struct((KERNEL, size, width), F32), struct((size, width), F32), struct((3, size, width), F32))
        + vm(*[line] * VECTORS, struct((1, 4 * width), F32), struct((2, width), F32)),
    )


def swap(values, e, axis="blk"):
    return lax.ppermute(values, axis, [(i, i ^ e) for i in range(lax.axis_size(axis))])


def after(values, *first):
    return lax.optimization_barrier((values, *first))[0]


def total_of(first, second):
    return (first.astype(F32) + second.astype(F32)).astype(BF)


class Scatter:
    def __init__(self, mine, theirs, count, stage):
        self.mine, self.theirs = mine, theirs
        self.numbers, _ = halves(count, stage)
        self.order = [stage] + [b for b in range(count.bit_length() - 1) if b != stage]
        self.got = swap(theirs, 1 << stage, "pts")

    def advance(self, *first):
        bit = self.order[1]
        keep = [j for j, r in enumerate(self.numbers) if not (r >> bit) & 1]
        send = [self.numbers.index(self.numbers[j] ^ (1 << bit)) for j in keep]
        self.mine, self.theirs = fold(self.mine, self.got, keep, send, first)
        self.numbers = [self.numbers[j] for j in keep]
        self.order = self.order[1:]
        self.got = swap(self.theirs, 1 << bit, "pts")
        return self.theirs

    def finish(self):
        while len(self.order) > 1:
            self.advance()
        return self


def shards(
    points, neighbours, patch_ids, conv_weight, conv_bias, cpe_weight, cpe_bias, cpe_gain, cpe_shift, first_gain,
    first_shift, qkv_weight, query_value_bias, proj_weight, proj_bias, second_gain, second_shift, hidden_weight,
    hidden_bias, output_weight, output_bias, out_grad,
):
    row_count, width = points.shape
    wide = conv_weight.shape[2]
    mine = row_count // 4
    shard_count = lax.axis_size("pts")
    me = lax.axis_index("blk")
    place_of = jnp.stack([me, lax.axis_index("pts")]).astype(jnp.int32)
    plan = Plan(mine, width)
    ups = [(i, i + 1) for i in range(shard_count - 1)]
    downs = [(i + 1, i) for i in range(shard_count - 1)]

    low = lax.ppermute(points[row_count - REACH :], "pts", ups)
    high = lax.ppermute(points[:REACH], "pts", downs)
    kernel_rows = conv_weight.reshape(KERNEL * width, wide)
    lookup = neighbours.T
    away_pack, near_pack, turned, small, patch_row = prepare(
        plan,
        place_of,
        qkv_weight.transpose(1, 0, 2),
        cpe_weight,
        points,
        patch_ids,
        (conv_bias, cpe_bias, cpe_gain, cpe_shift, first_gain, first_shift, proj_bias, second_gain, second_shift, output_bias),
        hidden_bias,
        query_value_bias,
        first=(low,),
    )
    far = swap(away_pack, 2)
    near = swap(near_pack, 1)

    *part3, gathered3, away_pack, near_pack = conv_forward(
        3, place_of, low, points, high, lookup, kernel_rows, BF, (hidden_weight, output_weight, proj_weight, out_grad),
    )
    got3 = [swap(p, 1) for p in part3]
    *part2, gathered2 = conv_forward(2, place_of, low, points, high, lookup, kernel_rows, BF, first=(part3[0],))
    far_part = swap(jnp.concatenate([total_of(a, b) for a, b in zip(part2, got3)], axis=0), 2)
    *part1, gathered1 = conv_forward(1, place_of, low, points, high, lookup, kernel_rows, BF, first=(part2[0],))
    *part0, gathered0 = conv_forward(0, place_of, low, points, high, lookup, kernel_rows, F32, first=(part1[0],), time=0.5)
    cross = swap(after(far, part2[0]), 1)
    close_part = [swap(p, 1) for p in part1]
    firsts = (near, far, cross)
    layer_one, conv_low, normed_cpe, scaling_cpe, residual_one, normed_one, scaling_one = first_rows(
        plan, place_of, part0, close_part, far_part, points, small, cpe_weight, *firsts
    )
    other_one = swap(layer_one, 1)
    far2 = swap(after(away_pack, layer_one), 2)
    near2 = swap(near_pack, 1)


    half = triple_half(plan, layer_one, turned, far, small)
    triple, mixed, keep, send, logs = attend_forward(plan, half, other_one, turned, far, small, patch_row)
    got = swap(send, 1)
    cross2 = swap(after(far2, send), 1)
    (
        block0, block1, block_far, active, before, layer_two, upstream, carried, carried_low, grad_keep, grad_send,
        sum_hidden_bias, sums_two,
    ) = second_rows(
        plan, place_of, keep, got, residual_one, out_grad, (hidden_weight, output_weight, proj_weight), small, firsts,
        (near2, far2, cross2),
    )
    grad_got = swap(grad_send, 1)

    weights_send = second_send(place_of, shard_count, upstream, active, before, layer_two, carried_low, got)
    weights_got = swap(after(weights_send, grad_got), 1)
    heads = width // HEAD_DIM
    grad_first = attend_backward(
        0, heads, triple, patch_row, grad_keep, grad_got, mixed, logs, first=(weights_send,)
    )
    weights_mine, weights_far = second_keep(
        place_of, shard_count, upstream, active, before, layer_two, carried_low, keep, weights_got, first=(grad_first,)
    )
    weights_far = swap(weights_far, 2)
    grad_second = attend_backward(
        heads, heads, triple, patch_row, grad_keep, grad_got, mixed, logs, first=(weights_mine,)
    )
    layer_send = layer_grad(1, grad_first, grad_second, turned, far, BF)
    layer_got = swap(layer_send, 1)
    layer_part = layer_grad(0, grad_first, grad_second, turned, far, F32, first=(layer_send,))
    conv_grad, points0, near_rows, far_rows, cpe_low, sums_one = third_rows(
        plan, place_of, layer_part, layer_got, carried, normed_one, scaling_one, normed_cpe, scaling_cpe, small, cpe_weight, firsts, (block1, block_far)
    )
    grad0 = conv_grad
    grad2 = swap(grad0, 2)
    grad1 = swap(grad0, 1)
    second_mine, second_theirs = fold(weights_mine, weights_far, *halves(shard_count, 0))
    second = Scatter(second_mine, second_theirs, shard_count, 0)
    spread0 = spread(0, (0, 1), place_of, lookup, kernel_rows, grad0, first=(weights_far,), time=TINY)
    cpe_send, cpe_keep, small_keep = cpe_weights(
        shard_count, place_of, conv_low, cpe_low, sums_one, sums_two, sum_hidden_bias, first=(spread0,)
    )
    cpe_got = swap(cpe_send, 1)
    third_mine, third_far = third_weights(
        place_of, shard_count, grad_first, grad_second, layer_one, other_one, cpe_keep, cpe_got, small_keep,
        first=(spread0, grad2, second.got),
    )
    grad3 = swap(after(grad2, cpe_send), 1)

    gathered = (gathered0, gathered1, gathered2, gathered3)
    grads = (grad0, grad1, grad2, grad3)
    chunk = KERNEL // 3 * width
    third_far = swap(after(third_far, grad2), 2)
    piece0, theirs0 = conv_weight_grad(
        place_of, gathered, grads, 0, chunk, shard_count, 0, first=(third_mine,)
    )
    sum0 = Scatter(piece0, theirs0, shard_count, 0)
    second_sent = second.advance(piece0)
    spread1 = spread(1, (0, 1), place_of, lookup, kernel_rows, grad1, first=(piece0, second_sent), time=TINY)
    piece1, theirs1 = conv_weight_grad(
        place_of, gathered, grads, chunk, chunk, shard_count, 0, thirds=(third_mine, third_far), first=(spread1,)
    )
    sum1 = Scatter(piece1, theirs1, shard_count, 0)
    sent = sum0.advance(piece1)
    piece2, theirs2 = conv_weight_grad(
        place_of, gathered, grads, 2 * chunk, chunk, shard_count, 0, first=(piece1, sent)
    )
    sum2 = Scatter(piece2, theirs2, shard_count, 0)
    spread2 = spread(2, (0,), place_of, lookup, kernel_rows, grad2, first=(piece2,), time=BLOCK)
    far_rows = swap(after(far_rows, piece2), 2)
    near_rows = swap(after(near_rows, piece2), 1)
    sent = sum0.advance(spread2)
    second_sent = second.advance(spread2)
    spread2_after = spread(2, (1,), place_of, lookup, kernel_rows, grad2, first=(spread2, sent, second_sent), time=BLOCK)
    spread3 = spread(3, (0,), place_of, lookup, kernel_rows, grad3, first=(spread2_after,), time=BLOCK)
    sent = sum1.advance(spread3)
    spread3_after = spread(3, (1,), place_of, lookup, kernel_rows, grad3, first=(spread3, sent, sum0.got, second.got), time=BLOCK)

    sent = sum2.advance(spread3_after)
    second = second.finish()
    grad_hidden, grad_output, grad_proj = second_out(second.mine, second.got, wide)
    grad_padded, to_below, to_above = finish(
        place_of, (spread0, spread1, spread2, spread2_after, spread3, spread3_after), first=(sent, grad_hidden)
    )
    cross_rows = swap(after(far_rows, spread3), 1)
    from_above = lax.ppermute(to_below, "pts", downs)
    from_below = lax.ppermute(to_above, "pts", ups)
    sent = sum1.advance(grad_padded)
    sent = sum2.advance(sent)
    block_out, grad_points = rows_out(
        place_of, grad_padded, from_below, from_above, block0, points0, near_rows, far_rows, cross_rows,
        first=(sent,),
    )

    grad_conv, grad_cpe, grad_qkv, *lines = grads_out([s.finish() for s in (sum0, sum1, sum2)], chunk, width)
    small = [line.reshape(-1) for line in lines[: VECTORS + 1]]
    return (
        block_out,
        grad_points,
        grad_conv.transpose(0, 2, 1),
        small[0],
        grad_cpe.T,
        *small[1:6],
        grad_qkv.transpose(1, 0, 2),
        lines[VECTORS + 1],
        grad_proj.T,
        small[8],
        small[6],
        small[7],
        grad_hidden,
        small[10],
        grad_output.T,
        small[9],
    )


def solution(mesh):
    return jax.shard_map(
        shards,
        mesh=mesh,
        in_specs=(
            P("pts", "blk"),
            P("pts", None),
            P("pts"),
            P(None, "blk", None),
            P("blk"),
            P("blk", None),
            P("blk"),
            P("blk"),
            P("blk"),
            P("blk"),
            P("blk"),
            P(None, None, "blk"),
            P(None, "blk"),
            P("blk", None),
            P("blk"),
            P("blk"),
            P("blk"),
            P(None, "blk"),
            P("blk"),
            P("blk", None),
            P("blk"),
            P("pts", "blk"),
        ),
        out_specs=(
            P("pts", "blk"),
            P("pts", "blk"),
            P(None, "blk", "pts"),
            P("blk"),
            P("blk", "pts"),
            P("blk"),
            P("blk"),
            P("blk"),
            P("blk"),
            P("blk"),
            P("pts", None, "blk"),
            P(None, "blk"),
            P("blk", "pts"),
            P("blk"),
            P("blk"),
            P("blk"),
            P("pts", "blk"),
            P("blk"),
            P("blk", "pts"),
            P("blk"),
        ),
        check_vma=False,
    )
```

```python
import functools
import math

import jax
import jax.numpy as jnp
from jax import lax
from jax.experimental import pallas as pl
from jax.experimental.pallas import tpu as pltpu
from jax.sharding import PartitionSpec as P

HEAD_DIM = 16
PATCH = 1024
KERNEL = 27
REACH = 256
EPS = 1e-05
LOG2E = math.log2(math.e)
BF = jnp.bfloat16
F32 = jnp.float32
NN = ((1,), (0,))
NT = ((1,), (1,))
TN = ((0,), (0,))
VMEM = pl.BlockSpec(memory_space=pltpu.VMEM)
SMEM = pl.BlockSpec(memory_space=pltpu.SMEM)
HBM = pl.BlockSpec(memory_space=pltpu.HBM)
ANY = pl.BlockSpec(memory_space=pl.ANY)
TILE = 256


def dot(a, b, dims):
    return lax.dot_general(a, b, (dims, ((), ())), preferred_element_type=F32)


def struct(shape, kind):
    return jax.ShapeDtypeStruct(shape, kind)


TIMES = {
    "prepare": 10,  "conv_forward": 7.5, "first_rows": 2.5, "triple_half": 2, "attend_forward": 21, "second_rows": 10,
    "second_send": 1.5, "attend_backward": 19, "second_keep": 2.5, "layer_grad": 1, "third_rows": 2.3, "cpe_weights": 0.1,
    "spread": 7, "third_weights": 0.1, "conv_weight_grad": 0.1, "finish": 1.0, "rows_out": 2.0, "fold": 0.05, "second_out": 0.1, "grads_out": 0.1,
}
FACTOR = 0.3
TINY = 0.1
BLOCK = 4.2


def call(name, kernel, inputs, outputs, scratch=(), mib=8, grid=None, first=(), time=None):
    count, extra = len(inputs), len(first)

    def body(*refs):
        kernel(*refs[:count], *refs[count + extra :])

    options = {} if grid is None else {"grid": grid}
    result = pl.pallas_call(
        body,
        out_shape=[o for o, spec in outputs],
        in_specs=[spec for a, spec in inputs] + [ANY] * extra,
        out_specs=[spec for o, spec in outputs],
        scratch_shapes=list(scratch),
        compiler_params=pltpu.CompilerParams(vmem_limit_bytes=mib * 2**20),
        cost_estimate=pl.CostEstimate(flops=int((time or TIMES[name]) * FACTOR * 1.15e9), bytes_accessed=0, transcendentals=0),
        name=name,
        **options,
    )(*[pltpu.with_memory_space_constraint(a, pltpu.HBM) if spec is HBM else a for a, spec in inputs], *first)
    return result[0] if len(result) == 1 else result


def vm(*arrays):
    return [(a, VMEM) for a in arrays]


def split3(values):
    high = values.astype(BF)
    rest = values - high.astype(F32)
    middle = rest.astype(BF)
    return high, middle, (rest - middle.astype(F32)).astype(BF)


def joined(rows, width):
    rows = rows.astype(F32)
    return (rows[:, :width] + rows[:, width : 2 * width]) + rows[:, 2 * width : 3 * width]


def in_order(pieces, me):
    core, chip = (me & 1) == 1, (me >> 1) == 1
    a, b = jnp.where(core, pieces[1], pieces[0]), jnp.where(core, pieces[0], pieces[1])
    c, d = jnp.where(core, pieces[3], pieces[2]), jnp.where(core, pieces[2], pieces[3])
    return [
        jnp.where(chip, c, a),
        jnp.where(chip, d, b),
        jnp.where(chip, a, c),
        jnp.where(chip, b, d),
    ]


def folded(source, start, target, row, sems, rows):
    part, width = rows // 4, source.shape[1]
    copies = []
    for j in range(4):
        copies.append(
            pltpu.make_async_copy(
                source.at[pl.ds(pl.multiple_of(start + j * part, 16), part), :],
                target.at[row : row + part, j * width : (j + 1) * width],
                sems(),
            )
        )
    return copies


def unfolded(pack, row, at, rows):
    part, width = rows // 4, pack.shape[1] // 4
    return jnp.concatenate(
        [
            pack[row : row + part, j * width : (j + 1) * width]
            for j in range(at.start // part, at.stop // part)
        ],
        axis=0,
    )


class Plan:
    def __init__(self, rows, width):
        fold = rows // 4
        self.first_cpe = 3 * width
        self.first_points = 4 * width
        self.first_small = 4 * width + 2 * fold
        self.first_rows = self.first_small + 16
        self.near_points = width
        self.near_small = width + fold
        self.near_rows = self.near_small + 16


def counter(sems):
    state = [0]

    def take():
        state[0] += 1
        return sems.at[state[0] - 1]

    return take


VECTORS = 10


def prepare_kernel(
    plan, rows, place_of, turned_in, cpe, points, patch, *refs
):
    vectors, refs = refs[:VECTORS], refs[VECTORS:]
    hidden_bias, query_bias, away, near, turned, small, patch_row, terms, lines, long_line, pair, straight, sems = refs
    me = place_of[0]
    width = points.shape[1]
    take = counter(sems)
    copies = [
        pltpu.make_async_copy(cpe, away.at[plan.first_cpe : plan.first_cpe + width, :], take()),
        pltpu.make_async_copy(cpe, near.at[0:width, :], take()),
    ]
    for e in (2, 3):
        copies += folded(points, (me ^ e) * rows, away, plan.first_points + (e - 2) * rows // 4, take, rows)
    copies += folded(points, (me ^ 1) * rows, near, plan.near_points, take, rows)
    straight_copy = pltpu.make_async_copy(turned_in, straight, take())
    straight_copy.start()
    for copy in copies:
        copy.start()
    loads = [pltpu.make_async_copy(vector, lines.at[r], take()) for r, vector in enumerate(vectors)]
    loads.append(pltpu.make_async_copy(hidden_bias, long_line, take()))
    loads.append(pltpu.make_async_copy(query_bias, pair, take()))
    for copy in loads:
        copy.start()
    for e in (0, 1):
        at = pl.ds(pl.multiple_of((me ^ e) * rows, rows), rows)
        loads.append(pltpu.make_async_copy(patch.at[:, at], patch_row.at[:, e * rows : (e + 1) * rows], take()))
        loads[-1].start()
    straight_copy.wait()
    for t in range(3):
        turned[t * width : (t + 1) * width, :] = straight[t].T
    for copy in loads:
        copy.wait()
    for r in range(VECTORS):
        small[r : r + 1, :] = lines[r]
    for i in range(4):
        small[VECTORS + i : VECTORS + i + 1, :] = long_line[:, i * width : (i + 1) * width]
    small[VECTORS + 4 :, :] = pair[...]
    high, middle, low = split3(small[...])
    terms[...] = jnp.concatenate([high, middle, low, jnp.zeros_like(low)], axis=1)
    last = [
        pltpu.make_async_copy(turned, away.at[0 : 3 * width, :], take()),
        pltpu.make_async_copy(terms, away.at[plan.first_small :, :], take()),
        pltpu.make_async_copy(terms, near.at[plan.near_small :, :], take()),
    ]
    for copy in last:
        copy.start()
    for copy in copies + last:
        copy.wait()


def prepare(plan, place_of, turned, cpe, points, patch, vectors, hidden_bias, query_bias, first=()):
    row_count, width = points.shape
    wide = cpe.shape[1]
    lines = [v.reshape(1, -1) for v in (*vectors, hidden_bias)]
    return call(
        "prepare",
        functools.partial(prepare_kernel, plan, row_count // 4),
        [(place_of, SMEM), (turned, HBM), (cpe, HBM), (points, HBM), (patch.reshape(1, -1), HBM)]
        + [(v, HBM) for v in (*lines, query_bias)],
        [
            (struct((plan.first_rows, wide), BF), HBM),
            (struct((plan.near_rows, wide), BF), HBM),
            (struct((3 * width, wide), BF), VMEM),
            (struct((16, width), F32), VMEM),
            (struct((1, row_count // 2), jnp.int32), VMEM),
        ],
        [
            pltpu.VMEM((16, wide), BF),
            pltpu.VMEM((VECTORS, 1, width), F32),
            pltpu.VMEM((1, 4 * width), F32),
            pltpu.VMEM((2, width), F32),
            pltpu.VMEM(turned.shape, BF),
            pltpu.SemaphoreType.DMA((17 + VECTORS + 5,)),
        ],
        first=first,
    )


def one_hot(place):
    spots = lax.broadcasted_iota(jnp.int32, (256, 256), 0).astype(F32).astype(BF)
    place = jnp.broadcast_to(place.astype(F32).astype(BF), (256, 256))
    return jnp.where(spots == place, jnp.ones((), BF), jnp.zeros((), BF))


def conv_kernel(e, packs, place_of, low, points, high, lookup, weight, *refs):
    sources, refs = refs[:packs], refs[packs:]
    conv, conv_after, gathered = refs[:3]
    away, near = refs[3:5] if packs else (None, None)
    turned, picked, sems = refs[-3:]
    me = place_of[0]
    width = points.shape[1]
    rows = picked.shape[1]
    quarter = me ^ e
    take = counter(sems)
    copies = []
    if packs:
        hidden, output, proj, upstream = sources
        wide, fold = hidden.shape[1], rows // 4
        start = 2 * wide + width
        for target in (away, near):
            copies.append(pltpu.make_async_copy(output, target.at[0:wide, :], take()))
            copies.append(pltpu.make_async_copy(proj, target.at[wide : wide + width, :], take()))
            copies.append(pltpu.make_async_copy(hidden, target.at[wide + width : start, :], take()))
        copies += folded(upstream, (me ^ 2) * rows, away, start, take, rows)
        copies += folded(upstream, (me ^ 3) * rows, away, start + fold, take, rows)
        copies += folded(upstream, (me ^ 1) * rows, near, start, take, rows)
        at = slice(start + fold, start + 3 * fold)
        copies.append(pltpu.make_async_copy(output.at[: 2 * fold, :], near.at[at, :], take()))
        for copy in copies:
            copy.start()
    base = place_of[1] * points.shape[0] + quarter * rows - REACH
    last = points.shape[0] // 256 - 1
    for j in range(rows // 256 + 2):
        spot = quarter * (rows // 256) - 1 + j
        at = pl.multiple_of(jnp.clip(spot, 0, last) * 256, 256)
        piece = points[pl.ds(at, 256), :]
        piece = jnp.where(spot < 0, low[...], jnp.where(spot > last, high[...], piece))
        turned[j * width : (j + 1) * width, :] = piece.T
    step = KERNEL // 3
    for b in range(rows // 256):
        cols = slice(b * 256, (b + 1) * 256)
        left = turned[b * width : (b + 3) * width, :]
        for k in range(KERNEL):
            spot = lookup[k : k + 1, pl.ds(pl.multiple_of(quarter * rows + b * 256, 256), 256)] - base
            part = jnp.broadcast_to(lax.shift_right_logical(spot, 8) - b, (width, 256))
            three = dot(left, one_hot(jnp.bitwise_and(spot, 255)), NN)
            values = jnp.where(
                part == 0,
                three[:width],
                jnp.where(part == 1, three[width : 2 * width], three[2 * width :]),
            )
            picked[k * width : (k + 1) * width, cols] = values.astype(BF)
            if k % step == step - 1:
                at = slice((k + 1 - step) * width, (k + 1) * width)
                copies.append(pltpu.make_async_copy(picked.at[at, cols], gathered.at[at, cols], take()))
                copies[-1].start()
        (conv, conv_after)[b][...] = dot(picked[:, cols], weight[...], TN).astype(conv.dtype)
    for copy in copies:
        copy.wait()


def conv_forward(e, place_of, low, points, high, lookup, weight, kind, packs=(), first=(), time=None):
    rows, width, wide = points.shape[0] // 4, points.shape[1], weight.shape[1]
    outputs = [(struct((rows // 2, wide), kind), VMEM)] * 2 + [(struct((KERNEL * width, rows), BF), HBM)]
    if packs:
        size = 2 * wide + width + rows // 4
        outputs += [(struct((size + rows // 4, wide), BF), HBM), (struct((size + rows // 2, wide), BF), HBM)]
    return call(
        "conv_forward",
        functools.partial(conv_kernel, e, len(packs)),
        [(place_of, SMEM)] + vm(low, points, high, lookup, weight) + [(p, HBM) for p in packs],
        outputs,
        [
            pltpu.VMEM(((rows // 256 + 2) * width, 256), BF),
            pltpu.VMEM((KERNEL * width, rows), BF),
            pltpu.SemaphoreType.DMA((6 * rows // 512 + (19 if packs else 0),)),
        ],
        first=first,
        time=time,
    )


def spread_kernel(e, blocks, place_of, lookup, weight, grads, out, upstream):
    width = out.shape[0]
    rows = grads.shape[0]
    quarter = place_of[0] ^ e
    base = place_of[1] * lookup.shape[1] + quarter * rows - REACH
    out[...] = jnp.zeros(out.shape, F32)
    step = 9
    for n, b in enumerate(blocks):
        cols = slice(b * 256, (b + 1) * 256)
        upstream[...] = dot(weight[...], grads[cols, :], NT)
        for s in range(KERNEL // step):
            left, right = [], []
            for k in range(s * step, (s + 1) * step):
                spot = lookup[k : k + 1, pl.ds(pl.multiple_of(quarter * rows + b * 256, 256), 256)] - base
                part = jnp.broadcast_to(lax.shift_right_logical(spot, 8) - b, (width, 256))
                mine = upstream[k * width : (k + 1) * width, :]
                left.append(
                    jnp.concatenate(
                        [jnp.where(part == i, mine, 0.0).astype(BF) for i in range(3)], axis=0
                    )
                )
                right.append(one_hot(jnp.bitwise_and(spot, 255)))
            three = dot(jnp.concatenate(left, axis=1), jnp.concatenate(right, axis=1), NT)
            for i in range(3):
                at = slice((n + i) * 256, (n + i + 1) * 256)
                out[:, at] = out[:, at] + three[i * width : (i + 1) * width]


def spread(e, blocks, place_of, lookup, weight, grads, first=(), time=None):
    width = weight.shape[0] // KERNEL
    return call(
        "spread",
        functools.partial(spread_kernel, e, blocks),
        [(place_of, SMEM)] + vm(lookup, weight, grads),
        [(struct((width, 256 * len(blocks) + 2 * REACH), F32), VMEM)],
        [pltpu.VMEM((KERNEL * width, 256), F32)],
        first=first,
        time=time,
    )


def halves(count, stage):
    keep = [r for r in range(count) if not (r >> stage) & 1]
    return keep, [r ^ (1 << stage) for r in keep]


def conv_weight_kernel(blocks, stage, start, count, extra, place_of, *refs):
    gathered, grads, refs = refs[:4], refs[4:8], refs[8:]
    thirds, (mine, theirs, total) = refs[:extra], refs[extra:]
    tile = 384
    for i in range(count // tile):
        rows = slice(start + i * tile, start + (i + 1) * tile)
        cols = slice(i * tile, (i + 1) * tile)
        total[:, cols] = sum(dot(a[rows, :], g[...], NN) for a, g in zip(gathered, grads)).T.astype(BF)
    size = total.shape[0] // blocks
    for out, slots in zip((mine, theirs), halves(blocks, stage)):
        for i, r in enumerate(slots):
            at = pl.multiple_of((place_of[1] ^ r) * size, size)
            out[i, :, 0:count] = total[pl.ds(at, size), :]
            if extra:
                out[i, :, count:] = (thirds[0][r].astype(F32) + thirds[1][r].astype(F32)).astype(BF)


def conv_weight_grad(place_of, gathered, grads, start, count, blocks, stage, thirds=(), first=()):
    wide = grads[0].shape[1]
    cols = count + (thirds[0].shape[2] if thirds else 0)
    half = struct((blocks // 2, wide // blocks, cols), BF)
    return call(
        "conv_weight_grad",
        functools.partial(conv_weight_kernel, blocks, stage, start, count, len(thirds)),
        [(place_of, SMEM)] + vm(*gathered, *grads, *thirds),
        vm(half, half),
        [pltpu.VMEM((wide, count), BF)],
        first=first,
    )


def finish_kernel(place_of, s0, s1, s2, s2_after, s3, s3_after, out, low, high):
    me = place_of[0]
    rows = s0.shape[1] - 2 * REACH
    ends = [s[:, 0:256] for s in (s0, s1, s2, s3)], [s[:, 768:] for s in (s0, s1)] + [s[:, 512:] for s in (s2_after, s3_after)]
    inner = [
        [s[:, 256:512] for s in (s0, s1)]
        + [a[:, 256:512] + b[:, 0:256] for a, b in ((s2, s2_after), (s3, s3_after))],
        [s[:, 512:768] for s in (s0, s1)]
        + [a[:, 512:768] + b[:, 256:512] for a, b in ((s2, s2_after), (s3, s3_after))],
    ]
    parts = [in_order(p, me) for p in (ends[0], inner[0], inner[1], ends[1])]
    out[...] = jnp.zeros(out.shape, F32)
    for q in range(4):
        for i, part in enumerate(parts):
            at = slice(q * rows + i * 256, q * rows + (i + 1) * 256)
            out[:, at] = out[:, at] + part[q]
    low[...] = out[:, :REACH].astype(BF)
    high[...] = out[:, out.shape[1] - REACH :].astype(BF)


def finish(place_of, spreads, first=()):
    width, span = spreads[0].shape
    total = 4 * (span - 2 * REACH) + 2 * REACH
    return call(
        "finish",
        finish_kernel,
        [(place_of, SMEM)] + vm(*spreads),
        [(struct((width, total), F32), VMEM)] + [(struct((width, REACH), BF), VMEM)] * 2,
        first=first,
    )


def rows_out_kernel(place_of, inside, below, above, block, own, near, far, cross, block_out, out):
    rows, width = own.shape
    me = place_of[0]
    pieces = in_order([block[...], near[:, :width], far[:, :width], cross[:, width : 2 * width]], me)
    for q in range(4):
        block_out[q * rows : (q + 1) * rows, :] = pieces[q]
    pieces = [own[...], near[:, width:], far[:, 2 * width : 3 * width], cross[:, 3 * width :]]
    pieces = in_order(pieces, me)
    for q in range(4):
        total = inside[:, REACH + q * rows : REACH + (q + 1) * rows].T + pieces[q].astype(F32)
        out[q * rows : (q + 1) * rows, :] = total
    out[:REACH, :] = out[:REACH, :] + below[...].astype(F32).T
    last = out.shape[0] - REACH
    out[last:, :] = out[last:, :] + above[...].astype(F32).T


def rows_out(place_of, inside, below, above, block, own, near, far, cross, first=()):
    rows, width = own.shape
    return call(
        "rows_out",
        rows_out_kernel,
        [(place_of, SMEM)] + vm(inside, below, above, block, own, near, far, cross),
        vm(struct((4 * rows, width), BF), struct((4 * rows, width), F32)),
        first=first,
    )


def three_rows(high, middle, low):
    spots = lax.broadcasted_iota(jnp.int32, (16, high.shape[1]), 0)
    picked = jnp.where(
        spots == 0,
        high.astype(F32),
        jnp.where(spots == 1, middle.astype(F32), jnp.where(spots == 2, low.astype(F32), 0.0)),
    )
    return picked.astype(BF)


def one_rows(length, count):
    spots = lax.broadcasted_iota(jnp.int32, (16, length), 0)
    return jnp.where(spots < count, 1.0, 0.0).astype(BF)


def patch_codes(patch):
    shape = (32, patch.shape[1])
    spots = lax.broadcasted_iota(jnp.int32, shape, 0)
    bits = jnp.bitwise_and(
        lax.shift_right_logical(jnp.broadcast_to(patch, shape), jnp.bitwise_and(spots, 15)), 1
    )
    bits = jnp.where(spots < 16, bits, 1 - bits)
    return jnp.where(bits == 1, 1.0, 0.0).astype(BF), jnp.where(bits == 1, 0.0, -1e30).astype(BF)


def fixed_rows(patch, query_side, key_side):
    length = patch.shape[1]
    left, right = patch_codes(patch)
    key_side[48:64, :] = one_rows(length, 3)
    key_side[64:96, :] = left
    query_side[64:96, :] = right
    key_side[96:128, :] = jnp.zeros((32, length), BF)
    query_side[96:128, :] = jnp.zeros((32, length), BF)


def column(row):
    return jnp.broadcast_to(row, (128, 128)).T[:, 0:1]


def triple_rows(values, weights, smalls, out, cols):
    width = out.shape[1] // 2
    for t in range(3):
        for i in range(2):
            piece = dot(weights[i][t * width : (t + 1) * width, :], values, NT)
            if t != 1:
                piece = piece + column(smalls[i][14 + t // 2 : 15 + t // 2, :])
            out[t, i * width : (i + 1) * width, cols] = piece.astype(BF)


def triple_half_kernel(plan, values, turned, away, small, out):
    smalls = (small[...], joined(away[plan.first_small :, :], small.shape[1]))
    triple_rows(values[...], (turned, away), smalls, out, slice(0, values.shape[0]))


def triple_half(plan, values, turned, away, small):
    return call(
        "triple_half",
        functools.partial(triple_half_kernel, plan),
        vm(values, turned, away, small),
        [(struct((3, 2 * small.shape[1], values.shape[0]), BF), VMEM)],
    )


def attend_forward_kernel(
    plan, heads, tile, mine, other, turned, away, small, patch, triple, total, keep, send, logs, query_side, key_side, value_side
):
    rows = mine.shape[2]
    length = 2 * rows
    for t in range(3):
        triple[t, :, :rows] = mine[t]
    smalls = (small[...], joined(away[plan.first_small :, :], small.shape[1]))
    triple_rows(other[...], (turned, away), smalls, triple, slice(rows, length))
    fixed_rows(patch[...], query_side, key_side)
    value_side[16:32, :] = one_rows(length, 1)

    @pl.loop(0, heads)
    def _(h):
        at = pl.ds(pl.multiple_of(h * HEAD_DIM, HEAD_DIM), HEAD_DIM)
        query = triple[0, at, :].astype(F32) * (HEAD_DIM**-0.5 * LOG2E)
        key = triple[1, at, :]
        high, middle, low = split3(query)
        query_side[0:16, :] = high
        query_side[16:32, :] = middle
        query_side[32:48, :] = low
        query_side[48:64, :] = jnp.zeros((16, length), BF)
        key_side[0:16, :] = key
        key_side[16:32, :] = key
        key_side[32:48, :] = key
        value_side[0:16, :] = triple[2, at, :]
        wide_key = key.astype(F32)
        bound = jnp.max(jnp.sum(query * query, axis=0)) * jnp.max(
            jnp.sum(wide_key * wide_key, axis=0)
        )
        logs[pl.ds(h, 1), :] = jnp.zeros((1, length), F32)

        @pl.when(jnp.logical_not(bound < 4096.0))
        def _():
            for t in range(length // tile):
                cols = slice(t * tile, (t + 1) * tile)
                top = jnp.max(dot(key_side[...], query_side[:, cols], TN), axis=0, keepdims=True)
                query_side[48:64, cols] = three_rows(*split3(-top))
                logs[pl.ds(h, 1), cols] = top

        for t in range(length // tile):
            cols = slice(t * tile, (t + 1) * tile)
            weights = jnp.exp2(dot(key_side[...], query_side[:, cols], TN)).astype(BF)
            mixed = dot(value_side[...], weights, NN)
            sums = mixed[16:17, :]
            mixed = mixed[0:16, :] * (1.0 / sums)
            total[at, cols] = mixed
            if t * tile < rows:
                keep[at, cols] = mixed.astype(BF)
            else:
                send[at, t * tile - rows : (t + 1) * tile - rows] = mixed.astype(BF)
            logs[pl.ds(h, 1), cols] = logs[pl.ds(h, 1), cols] + jnp.log2(sums)


def attend_forward(plan, mine, other, turned, away, small, patch, first=()):
    width, rows = mine.shape[1:]
    length = 2 * rows
    heads = width // HEAD_DIM
    return call(
        "attend_forward",
        functools.partial(attend_forward_kernel, plan, heads, 512),
        vm(mine, other, turned, away, small, patch),
        [
            (struct((3, width, length), BF), VMEM),
            (struct((width, length), F32), VMEM),
            (struct((width, rows), BF), VMEM),
            (struct((width, rows), BF), VMEM),
            (struct((heads, length), F32), VMEM),
        ],
        [
            pltpu.VMEM((128, length), BF),
            pltpu.VMEM((128, length), BF),
            pltpu.VMEM((32, length), BF),
        ],
        first=first,
    )


def attend_backward_kernel(
    first, heads, tile, triple, patch, mine, other, mixed, logs, out, query_side, key_side, value_side, grad_side, grad_value, grad_key
):
    length = triple.shape[2]
    fixed_rows(patch[...], query_side, key_side)
    value_side[16:32, :] = one_rows(length, 3)

    @pl.loop(0, heads)
    def _(h):
        at = pl.ds(pl.multiple_of((h + first) * HEAD_DIM, HEAD_DIM), HEAD_DIM)
        to = pl.ds(pl.multiple_of(h * HEAD_DIM, HEAD_DIM), HEAD_DIM)
        query, key = triple[0, at, :], triple[1, at, :]
        upstream = jnp.concatenate([mine[at, :], other[at, :]], axis=1)
        high, middle, low = split3(query.astype(F32) * (HEAD_DIM**-0.5 * LOG2E))
        query_side[0:16, :] = high
        query_side[16:32, :] = middle
        query_side[32:48, :] = low
        query_side[48:64, :] = three_rows(*split3(-logs[pl.ds(h + first, 1), :]))
        key_side[0:16, :] = key
        key_side[16:32, :] = key
        key_side[32:48, :] = key
        value_side[0:16, :] = triple[2, at, :]
        inner = jnp.sum(upstream.astype(F32) * mixed[at, :], axis=0, keepdims=True)
        grad_side[0:16, :] = upstream
        grad_side[16:32, :] = three_rows(*split3(-inner))
        for t in range(length // tile):
            cols = slice(t * tile, (t + 1) * tile)
            prob = jnp.exp2(dot(query_side[:, cols], key_side[...], TN))
            grad_prob = dot(grad_side[:, cols], value_side[...], TN)
            grad_score = (prob * grad_prob).astype(BF)
            value_part = dot(upstream[:, cols], prob.astype(BF), NN)
            key_part = dot(query[:, cols], grad_score, NN)
            out[0, to, cols] = (dot(key, grad_score, NT) * HEAD_DIM**-0.5).astype(BF)
            if t == 0:
                grad_value[...] = value_part
                grad_key[...] = key_part
            else:
                grad_value[...] += value_part
                grad_key[...] += key_part
        out[1, to, :] = (grad_key[...] * HEAD_DIM**-0.5).astype(BF)
        out[2, to, :] = grad_value[...].astype(BF)


def attend_backward(first_head, heads, triple, patch, mine, other, mixed, logs, first=()):
    length = triple.shape[2]
    return call(
        "attend_backward",
        functools.partial(attend_backward_kernel, first_head, heads, 512),
        vm(triple, patch, mine, other, mixed, logs),
        [(struct((3, heads * HEAD_DIM, length), BF), VMEM)],
        [
            pltpu.VMEM((128, length), BF),
            pltpu.VMEM((128, length), BF),
            pltpu.VMEM((32, length), BF),
            pltpu.VMEM((32, length), BF),
            pltpu.VMEM((16, length), F32),
            pltpu.VMEM((16, length), F32),
        ],
        mib=12,
        first=first,
    )


def norm_rows(values):
    average = jnp.mean(values, axis=1, keepdims=True)
    scaling = lax.rsqrt(
        jnp.mean(values * values, axis=1, keepdims=True) - average * average + EPS
    )
    return (values - average) * scaling, scaling


def norm_rows_back(upstream, normed, scaling, gain):
    scaled = upstream * gain
    return scaling * (
        scaled
        - jnp.mean(scaled, axis=1, keepdims=True)
        - normed * jnp.mean(scaled * normed, axis=1, keepdims=True)
    )


def cut(values):
    width = values.shape[1] // 4
    return [values[:, j * width : (j + 1) * width] for j in range(4)]


def add_rows(ref, row, values, first):
    total = jnp.sum(values, axis=0, keepdims=True)
    ref[row : row + 1, :] = total if first else ref[row : row + 1, :] + total


def small_vectors(plan, small, near, far, cross):
    width = small.shape[1]
    return [
        small[...],
        joined(near[plan.near_small :, :], width),
        joined(far[plan.first_small :, :], width),
        joined(cross[plan.first_small :, :], width),
    ]


def vectors(smalls, me):
    return jnp.concatenate(in_order(smalls, me), axis=1)


def cpe_rows(plan, weight, near, far, cross, me):
    width = weight.shape[0]
    at = slice(plan.first_cpe, plan.first_cpe + width)
    pieces = [weight[...], near[:width, :], far[at, :], cross[at, :]]
    return jnp.concatenate(in_order(pieces, me), axis=0)


def own_rows(ref, me, rows, at):
    return ref[pl.ds(pl.multiple_of(me * rows + at.start, at.stop - at.start), at.stop - at.start), :]


def first_rows_kernel(
    plan, place_of, part_low, part_high, close_low, close_high, away, points, small, weight, near, far, cross,
    layer, middle, normed_cpe, scaling_cpe, residual, normed, scaling,
):
    me = place_of[0]
    rows = 2 * part_low.shape[0]
    vec = vectors(small_vectors(plan, small, near, far, cross), me)
    vec = [vec[r : r + 1, :] for r in range(6)]
    weights = cpe_rows(plan, weight, near, far, cross, me)
    for t in range(rows // TILE):
        at = slice(t * TILE, (t + 1) * TILE)
        part, close = ((part_low, close_low), (part_high, close_high))[t * TILE * 2 // rows]
        low = (part[...] + close[...].astype(F32) + away[at, :].astype(F32) + vec[0]).astype(BF)
        middle[at, :] = low
        xhat, rate = norm_rows(dot(low, weights, NN) + vec[1])
        normed_cpe[at, :] = xhat
        scaling_cpe[at, :] = rate
        features = [
            own_rows(points, me, rows, at),
            unfolded(near, plan.near_points, at, rows),
            unfolded(far, plan.first_points, at, rows),
            unfolded(cross, plan.first_points + rows // 4, at, rows),
        ]
        features = jnp.concatenate(in_order(features, me), axis=1)
        sums = features.astype(F32) + xhat * vec[2] + vec[3]
        residual[at, :] = sums
        xhat, rate = norm_rows(sums)
        normed[at, :] = xhat
        scaling[at, :] = rate
        layer[at, :] = (xhat * vec[4] + vec[5]).astype(BF)


def first_rows(plan, place_of, parts, closes, away, points, small, weight, near, far, cross):
    rows, wide = away.shape
    full, thin, lower = struct((rows, wide), F32), struct((rows, 1), F32), struct((rows, wide), BF)
    return call(
        "first_rows",
        functools.partial(first_rows_kernel, plan),
        [(place_of, SMEM)] + vm(*parts, *closes, away, points, small, weight, near, far, cross),
        vm(lower, lower, full, thin, full, full, thin),
    )


def gelu_parts(u):
    scale = math.sqrt(2 / math.pi)
    square = u * u
    bent = jnp.tanh(u * (scale + (scale * 0.044715) * square))
    half = 0.5 + 0.5 * bent
    slope = half + u * (1.0 - bent * bent) * (0.5 * scale + (1.5 * 0.044715 * scale) * square)
    return u * half, slope


def second_rows_kernel(
    plan, place_of, keep, got, residual, out_grad, hidden, output, proj, small, near, far, cross, near2, far2, cross2,
    block0, block1, block_far, active, before, layer, upstream, carried, low, grad_keep, grad_send, hidden_sums, sums,
):
    me = place_of[0]
    rows, wide = residual.shape
    smalls = small_vectors(plan, small, near, far, cross)
    vec = vectors(smalls, me)
    vec = {r: vec[r : r + 1, :] for r in (6, 7, 8, 9)}
    biases = [jnp.concatenate([s[10 + i : 11 + i, :] for i in range(4)], axis=1) for s in smalls]
    width = keep.shape[0] // 2
    packs = (near2, far2, cross2)
    end = wide + width
    hiddens = [hidden] + [p.at[end : end + wide, :] for p in packs]
    last = end + wide
    outputs = [output] + [p.at[0:wide, :] for p in packs]
    projs = [proj[...]] + [p[wide:end, :] for p in packs]
    mine = jnp.concatenate([projs[0], projs[2]], axis=0)
    others = jnp.concatenate([projs[1], projs[3]], axis=0)
    for t in range(rows // TILE):
        at = slice(t * TILE, (t + 1) * TILE)
        base = residual[at, :] + vec[6] + dot(keep[:, at], mine, TN) + dot(got[:, at], others, TN)
        normed, scaling = norm_rows(base)
        lower = (normed * vec[7] + vec[8]).astype(BF)
        layer[at, :] = lower
        grads = [
            own_rows(out_grad, me, rows, at),
            unfolded(near2, last, at, rows),
            unfolded(far2, last, at, rows),
            unfolded(cross2, last + rows // 4, at, rows),
        ]
        grads = jnp.concatenate(in_order(grads, me), axis=1)
        upstream[at, :] = grads
        result = base + vec[9]
        grad_layer = None
        for e in range(4):
            act, slope = gelu_parts(dot(lower, hiddens[e][...], NN) + biases[e])
            act = act.astype(BF)
            active[e, at, :] = act
            result = result + dot(act, outputs[e][...], NN)
            pre = dot(grads, outputs[e][...], NT) * slope
            add_rows(hidden_sums, e, pre, t == 0)
            pre = pre.astype(BF)
            before[e, at, :] = pre
            piece = dot(pre, hiddens[e][...], NT)
            grad_layer = piece if e == 0 else grad_layer + piece
        result = in_order(cut(result.astype(BF)), me)
        block0[at, :] = result[0]
        block1[at, :] = result[1]
        block_far[at, 0:width] = result[2]
        block_far[at, width:] = result[3]
        wide_grads = grads.astype(F32)
        add_rows(sums, 0, grad_layer * normed, t == 0)
        add_rows(sums, 1, grad_layer, t == 0)
        add_rows(sums, 3, wide_grads, t == 0)
        carry = wide_grads + norm_rows_back(grad_layer, normed, scaling, vec[7])
        carried[at, :] = carry
        add_rows(sums, 2, carry, t == 0)
        carry = carry.astype(BF)
        low[at, :] = carry
        grad_keep[:, at] = dot(mine, carry, NT).astype(BF)
        grad_send[:, at] = dot(others, carry, NT).astype(BF)


def second_rows(plan, place_of, keep, got, residual, out_grad, weights, small, firsts, seconds):
    rows, wide = residual.shape
    lower, piece = struct((rows, wide), BF), struct((rows, wide // 4), BF)
    heads = struct(keep.shape, BF)
    return call(
        "second_rows",
        functools.partial(second_rows_kernel, plan),
        [(place_of, SMEM)] + vm(keep, got, residual, out_grad, *weights, small, *firsts, *seconds),
        vm(
            piece,
            piece,
            struct((rows, wide // 2), BF),
            struct((4, rows, wide), BF),
            struct((4, rows, wide), BF),
            lower,
            lower,
            struct((rows, wide), F32),
            lower,
            heads,
            heads,
            struct((4, wide), F32),
            struct((4, wide), F32),
        ),
        mib=12,
    )


def cut_rows(store, spot, cols, value, blocks):
    size = value.shape[0] // blocks
    for p in range(blocks):
        store(p ^ spot, cols, value[p * size : (p + 1) * size])


def second_weight_parts(i, e, blocks, spot, upstream, active, before, layer, low, attended, store):
    wide = layer.shape[1]
    width = attended.shape[0] // 2
    cut_rows(store, spot, slice(0, wide), dot(layer[...], before[e], TN), blocks)
    cut_rows(store, spot, slice(wide, 2 * wide), dot(upstream[...], active[e], TN), blocks)
    part = dot(attended[i * width : (i + 1) * width, :], low[...], NN)
    cut_rows(store, spot, slice(2 * wide, 2 * wide + width), part.T, blocks)


def second_send_kernel(blocks, place_of, upstream, active, before, layer, low, attended, out):
    for i, e in enumerate((1, 3)):

        def store(p, cols, value):
            out[i, p, :, cols] = value.astype(BF)

        second_weight_parts(i, e, blocks, place_of[1], upstream, active, before, layer, low, attended, store)


def second_send(place_of, blocks, upstream, active, before, layer, low, attended):
    wide = layer.shape[1]
    return call(
        "second_send",
        functools.partial(second_send_kernel, blocks),
        [(place_of, SMEM)] + vm(upstream, active, before, layer, low, attended),
        [(struct((2, blocks, wide // blocks, 2 * wide + attended.shape[0] // 2), BF), VMEM)],
    )


def second_keep_kernel(blocks, place_of, upstream, active, before, layer, low, attended, got, mine, far):
    for i, out in enumerate((mine, far)):

        def store(p, cols, value):
            out[p, :, cols] = (value + got[i, p, :, cols].astype(F32)).astype(BF)

        second_weight_parts(i, 2 * i, blocks, place_of[1], upstream, active, before, layer, low, attended, store)


def second_keep(place_of, blocks, upstream, active, before, layer, low, attended, got, first=()):
    out = struct(got.shape[1:], BF)
    return call(
        "second_keep",
        functools.partial(second_keep_kernel, blocks),
        [(place_of, SMEM)] + vm(upstream, active, before, layer, low, attended, got),
        vm(out, out),
        first=first,
    )


def third_weights_kernel(
    blocks, place_of, first_half, second_half, mine, other, cpe_keep, cpe_got, small_keep, own, far
):
    rows = mine.shape[0]
    width = first_half.shape[1]
    size = own.shape[1]
    empty = jnp.zeros((size - 16, width), BF)
    for i, (grads, out) in enumerate(((first_half, own), (second_half, far))):

        def store(p, cols, value):
            out[p, :, cols] = value.astype(BF)

        for t in range(3):
            part = dot(grads[t, :, :rows], mine[...], NN) + dot(grads[t, :, rows:], other[...], NN)
            cut_rows(store, place_of[1], slice(t * width, (t + 1) * width), part.T, blocks)
        sums = [jnp.sum(grads[t].astype(F32).T, axis=0, keepdims=True) for t in (0, 2)]
        small_got = sum(cpe_got[i, slot, size:, :].astype(F32) for slot in range(3))
        small = small_keep[i] + small_got + jnp.concatenate([jnp.zeros((14, width), F32)] + sums, axis=0)
        for p in range(blocks):
            out[p, :, 3 * width : 4 * width] = (
                cpe_keep[i, p].astype(F32) + cpe_got[i, p, :size, :].astype(F32)
            ).astype(BF)
            out[p, 0:16, 4 * width :] = small.astype(BF)
            if empty.shape[0]:
                out[p, 16:, 4 * width :] = empty


def third_weights(place_of, blocks, first_half, second_half, mine, other, cpe_keep, cpe_got, small_keep, first=()):
    wide = mine.shape[1]
    width = first_half.shape[1]
    out = struct((blocks, wide // blocks, 5 * width), BF)
    return call(
        "third_weights",
        functools.partial(third_weights_kernel, blocks),
        [(place_of, SMEM)] + vm(first_half, second_half, mine, other, cpe_keep, cpe_got, small_keep),
        vm(out, out),
        first=first,
    )


def layer_grad_kernel(half, first_half, second_half, turned, away, out):
    width = first_half.shape[1]
    rows = first_half.shape[2] // 2
    cols = slice(half * rows, (half + 1) * rows)
    total = None
    for t in range(3):
        at = slice(t * width, (t + 1) * width)
        for grads, weight in ((first_half, turned), (second_half, away)):
            piece = dot(grads[t, :, cols], weight[at, :], TN)
            total = piece if total is None else total + piece
    out[...] = total.astype(out.dtype)


def layer_grad(half, first_half, second_half, turned, away, kind, first=()):
    return call(
        "layer_grad",
        functools.partial(layer_grad_kernel, half),
        vm(first_half, second_half, turned, away),
        [(struct((first_half.shape[2] // 2, turned.shape[1]), kind), VMEM)],
        first=first,
    )


def third_rows_kernel(
    plan, place_of, part, close, carried, normed, scaling, normed_cpe, scaling_cpe, small, weight, near, far, cross, block1, block_far,
    conv_grad, points0, near_rows, far_rows, low, sums,
):
    me = place_of[0]
    vec = vectors(small_vectors(plan, small, near, far, cross), me)
    weights = cpe_rows(plan, weight, near, far, cross, me)
    width = points0.shape[1]
    for t in range(part.shape[0] // TILE):
        at = slice(t * TILE, (t + 1) * TILE)
        upstream = part[at, :] + close[at, :].astype(F32)
        xhat = normed[at, :]
        add_rows(sums, 4, upstream * xhat, t == 0)
        add_rows(sums, 5, upstream, t == 0)
        grads = carried[at, :] + norm_rows_back(upstream, xhat, scaling[at, :], vec[4:5, :])
        pieces = in_order(cut(grads.astype(BF)), me)
        points0[at, :] = pieces[0]
        near_rows[at, 0:width] = block1[at, :]
        near_rows[at, width:] = pieces[1]
        far_rows[at, 0 : 2 * width] = block_far[at, :]
        far_rows[at, 2 * width : 3 * width] = pieces[2]
        far_rows[at, 3 * width :] = pieces[3]
        xhat = normed_cpe[at, :]
        add_rows(sums, 2, grads * xhat, t == 0)
        add_rows(sums, 3, grads, t == 0)
        grads = norm_rows_back(grads, xhat, scaling_cpe[at, :], vec[2:3, :])
        add_rows(sums, 1, grads, t == 0)
        lower = grads.astype(BF)
        low[at, :] = lower
        result = dot(lower, weights, NT)
        add_rows(sums, 0, result, t == 0)
        conv_grad[at, :] = result.astype(BF)


def third_rows(plan, place_of, part, close, carried, normed, scaling, normed_cpe, scaling_cpe, small, weight, firsts, blocks):
    rows, wide = part.shape
    lower, piece = struct((rows, wide), BF), struct((rows, wide // 4), BF)
    return call(
        "third_rows",
        functools.partial(third_rows_kernel, plan),
        [(place_of, SMEM)]
        + vm(part, close, carried, normed, scaling, normed_cpe, scaling_cpe, small, weight, *firsts, *blocks),
        vm(lower, piece, struct((rows, wide // 2), BF), lower, lower, struct((6, wide), F32)),
    )


def cpe_weights_kernel(
    blocks, place_of, middle, low, sums_one, sums_two, hidden_sums, send, keep, small_keep, small_send
):
    me = place_of[0]
    width = middle.shape[1] // 4
    ones, twos = in_order(cut(sums_one[...]), me), in_order(cut(sums_two[...]), me)
    for e in range(4):
        out = (keep, send, keep, send)[e]

        def store(p, cols, value):
            out[e // 2, p, : value.shape[0], cols] = value.astype(BF)

        at = pl.ds(pl.multiple_of((e ^ me) * width, width), width)
        cut_rows(store, place_of[1], slice(0, width), dot(low[...], middle[:, at], TN), blocks)
        out = (small_keep, small_send, small_keep, small_send)[e]
        out[e // 2, 0:6, :] = ones[e]
        out[e // 2, 6:10, :] = twos[e]
        for i in range(4):
            out[e // 2, 10 + i : 11 + i, :] = hidden_sums[e : e + 1, i * width : (i + 1) * width]
        out[e // 2, 14:16, :] = jnp.zeros((2, width), F32)
    size = send.shape[2] - 16
    for i in range(2):
        for slot, term in enumerate(split3(small_send[i])):
            send[i, slot, size:, :] = term
        send[i, 3:, size:, :] = jnp.zeros((blocks - 3, 16, width), BF)


def cpe_weights(blocks, place_of, middle, low, sums_one, sums_two, hidden_sums, first=()):
    wide = middle.shape[1]
    send = struct((2, blocks, wide // blocks + 16, wide // 4), BF)
    keep = struct((2, blocks, wide // blocks, wide // 4), BF)
    small = (2, 16, wide // 4)
    return call(
        "cpe_weights",
        functools.partial(cpe_weights_kernel, blocks),
        [(place_of, SMEM)] + vm(middle, low, sums_one, sums_two, hidden_sums),
        vm(send, keep, struct(small, F32)),
        [pltpu.VMEM(small, F32)],
        first=first,
    )


def fold_kernel(keep, send, mine, got, kept, sent):
    for out, slots in ((sent, send), (kept, keep)):
        for i, j in enumerate(slots):
            out[i] = (mine[j].astype(F32) + got[j].astype(F32)).astype(BF)


def fold(mine, got, keep, send, first=()):
    out = struct((len(keep), *mine.shape[1:]), BF)
    return call("fold", functools.partial(fold_kernel, keep, send), vm(mine, got), vm(out, out), first=first)


def second_out_kernel(mine, got, hidden, output, proj):
    total = mine[0].astype(F32) + got[0].astype(F32)
    wide = hidden.shape[1]
    hidden[...] = total[:, :wide]
    output[...] = total[:, wide : 2 * wide]
    proj[...] = total[:, 2 * wide :]


def second_out(mine, got, wide):
    size, cols = mine.shape[1:]
    return call(
        "second_out",
        second_out_kernel,
        vm(mine, got),
        vm(struct((size, wide), F32), struct((size, wide), F32), struct((size, cols - 2 * wide), F32)),
    )


def grads_out_kernel(chunk, m0, g0, m1, g1, m2, g2, conv, cpe, qkv, *lines):
    width = cpe.shape[1]
    for i, (mine, got) in enumerate(((m0, g0), (m1, g1), (m2, g2))):
        part = mine[0, :, :chunk].astype(F32) + got[0, :, :chunk].astype(F32)
        for k in range(chunk // width):
            conv[i * (chunk // width) + k] = part[:, k * width : (k + 1) * width]
    third = m1[0, :, chunk:].astype(F32) + g1[0, :, chunk:].astype(F32)
    for t in range(3):
        qkv[t] = third[:, t * width : (t + 1) * width]
    cpe[...] = third[:, 3 * width : 4 * width]
    small = third[:16, 4 * width :]
    for r in range(VECTORS):
        lines[r][...] = small[r : r + 1, :]
    for i in range(4):
        lines[VECTORS][:, i * width : (i + 1) * width] = small[VECTORS + i : VECTORS + i + 1, :]
    lines[VECTORS + 1][...] = small[VECTORS + 4 :, :]


def grads_out(sums, chunk, width):
    size = sums[0].mine.shape[1]
    line = struct((1, width), F32)
    return call(
        "grads_out",
        functools.partial(grads_out_kernel, chunk),
        vm(*[a for s in sums for a in (s.mine, s.got)]),
        vm(struct((KERNEL, size, width), F32), struct((size, width), F32), struct((3, size, width), F32))
        + vm(*[line] * VECTORS, struct((1, 4 * width), F32), struct((2, width), F32)),
    )


def swap(values, e, axis="blk"):
    return lax.ppermute(values, axis, [(i, i ^ e) for i in range(lax.axis_size(axis))])


def after(values, *first):
    return lax.optimization_barrier((values, *first))[0]


def total_of(first, second):
    return (first.astype(F32) + second.astype(F32)).astype(BF)


class Scatter:
    def __init__(self, mine, theirs, count, stage):
        self.mine, self.theirs = mine, theirs
        self.numbers, _ = halves(count, stage)
        self.order = [stage] + [b for b in range(count.bit_length() - 1) if b != stage]
        self.got = swap(theirs, 1 << stage, "pts")

    def advance(self, *first):
        bit = self.order[1]
        keep = [j for j, r in enumerate(self.numbers) if not (r >> bit) & 1]
        send = [self.numbers.index(self.numbers[j] ^ (1 << bit)) for j in keep]
        self.mine, self.theirs = fold(self.mine, self.got, keep, send, first)
        self.numbers = [self.numbers[j] for j in keep]
        self.order = self.order[1:]
        self.got = swap(self.theirs, 1 << bit, "pts")
        return self.theirs

    def finish(self):
        while len(self.order) > 1:
            self.advance()
        return self


def shards(
    points, neighbours, patch_ids, conv_weight, conv_bias, cpe_weight, cpe_bias, cpe_gain, cpe_shift, first_gain,
    first_shift, qkv_weight, query_value_bias, proj_weight, proj_bias, second_gain, second_shift, hidden_weight,
    hidden_bias, output_weight, output_bias, out_grad,
):
    row_count, width = points.shape
    wide = conv_weight.shape[2]
    mine = row_count // 4
    shard_count = lax.axis_size("pts")
    me = lax.axis_index("blk")
    place_of = jnp.stack([me, lax.axis_index("pts")]).astype(jnp.int32)
    plan = Plan(mine, width)
    ups = [(i, i + 1) for i in range(shard_count - 1)]
    downs = [(i + 1, i) for i in range(shard_count - 1)]

    low = lax.ppermute(points[row_count - REACH :], "pts", ups)
    high = lax.ppermute(points[:REACH], "pts", downs)
    kernel_rows = conv_weight.reshape(KERNEL * width, wide)
    lookup = neighbours.T
    away_pack, near_pack, turned, small, patch_row = prepare(
        plan,
        place_of,
        qkv_weight.transpose(1, 0, 2),
        cpe_weight,
        points,
        patch_ids,
        (conv_bias, cpe_bias, cpe_gain, cpe_shift, first_gain, first_shift, proj_bias, second_gain, second_shift, output_bias),
        hidden_bias,
        query_value_bias,
        first=(low,),
    )
    far = swap(away_pack, 2)
    near = swap(near_pack, 1)

    *part3, gathered3, away_pack, near_pack = conv_forward(
        3, place_of, low, points, high, lookup, kernel_rows, BF, (hidden_weight, output_weight, proj_weight, out_grad),
    )
    got3 = [swap(p, 1) for p in part3]
    *part2, gathered2 = conv_forward(2, place_of, low, points, high, lookup, kernel_rows, BF, first=(part3[0],))
    far_part = swap(jnp.concatenate([total_of(a, b) for a, b in zip(part2, got3)], axis=0), 2)
    *part1, gathered1 = conv_forward(1, place_of, low, points, high, lookup, kernel_rows, BF, first=(part2[0],))
    *part0, gathered0 = conv_forward(0, place_of, low, points, high, lookup, kernel_rows, F32, first=(part1[0],), time=0.5)
    cross = swap(after(far, part2[0]), 1)
    close_part = [swap(p, 1) for p in part1]
    firsts = (near, far, cross)
    layer_one, conv_low, normed_cpe, scaling_cpe, residual_one, normed_one, scaling_one = first_rows(
        plan, place_of, part0, close_part, far_part, points, small, cpe_weight, *firsts
    )
    other_one = swap(layer_one, 1)
    far2 = swap(after(away_pack, part1[0]), 2)
    near2 = swap(near_pack, 1)


    half = triple_half(plan, layer_one, turned, far, small)
    triple, mixed, keep, send, logs = attend_forward(plan, half, other_one, turned, far, small, patch_row)
    got = swap(send, 1)
    cross2 = swap(after(far2, send), 1)
    (
        block0, block1, block_far, active, before, layer_two, upstream, carried, carried_low, grad_keep, grad_send,
        sum_hidden_bias, sums_two,
    ) = second_rows(
        plan, place_of, keep, got, residual_one, out_grad, (hidden_weight, output_weight, proj_weight), small, firsts,
        (near2, far2, cross2),
    )
    grad_got = swap(grad_send, 1)

    weights_send = second_send(place_of, shard_count, upstream, active, before, layer_two, carried_low, got)
    weights_got = swap(after(weights_send, grad_got), 1)
    heads = width // HEAD_DIM
    grad_first = attend_backward(
        0, heads, triple, patch_row, grad_keep, grad_got, mixed, logs, first=(weights_send,)
    )
    weights_mine, weights_far = second_keep(
        place_of, shard_count, upstream, active, before, layer_two, carried_low, keep, weights_got, first=(grad_first,)
    )
    weights_far = swap(weights_far, 2)
    grad_second = attend_backward(
        heads, heads, triple, patch_row, grad_keep, grad_got, mixed, logs, first=(weights_mine,)
    )
    layer_send = layer_grad(1, grad_first, grad_second, turned, far, BF)
    layer_got = swap(layer_send, 1)
    layer_part = layer_grad(0, grad_first, grad_second, turned, far, F32, first=(layer_send,))
    conv_grad, points0, near_rows, far_rows, cpe_low, sums_one = third_rows(
        plan, place_of, layer_part, layer_got, carried, normed_one, scaling_one, normed_cpe, scaling_cpe, small, cpe_weight, firsts, (block1, block_far)
    )
    grad0 = conv_grad
    grad2 = swap(grad0, 2)
    grad1 = swap(grad0, 1)
    second_mine, second_theirs = fold(weights_mine, weights_far, *halves(shard_count, 0))
    second = Scatter(second_mine, second_theirs, shard_count, 0)
    spread0 = spread(0, (0, 1), place_of, lookup, kernel_rows, grad0, first=(weights_far,), time=TINY)
    cpe_send, cpe_keep, small_keep = cpe_weights(
        shard_count, place_of, conv_low, cpe_low, sums_one, sums_two, sum_hidden_bias, first=(spread0,)
    )
    cpe_got = swap(cpe_send, 1)
    third_mine, third_far = third_weights(
        place_of, shard_count, grad_first, grad_second, layer_one, other_one, cpe_keep, cpe_got, small_keep,
        first=(spread0, grad2, second.got),
    )
    grad3 = swap(after(grad2, cpe_send), 1)

    gathered = (gathered0, gathered1, gathered2, gathered3)
    grads = (grad0, grad1, grad2, grad3)
    chunk = KERNEL // 3 * width
    third_far = swap(after(third_far, grad2), 2)
    piece0, theirs0 = conv_weight_grad(
        place_of, gathered, grads, 0, chunk, shard_count, 0, first=(third_mine,)
    )
    sum0 = Scatter(piece0, theirs0, shard_count, 0)
    second_sent = second.advance(piece0)
    spread1 = spread(1, (0, 1), place_of, lookup, kernel_rows, grad1, first=(piece0, second_sent), time=TINY)
    piece1, theirs1 = conv_weight_grad(
        place_of, gathered, grads, chunk, chunk, shard_count, 0, thirds=(third_mine, third_far), first=(spread1,)
    )
    sum1 = Scatter(piece1, theirs1, shard_count, 0)
    sent = sum0.advance(piece1)
    piece2, theirs2 = conv_weight_grad(
        place_of, gathered, grads, 2 * chunk, chunk, shard_count, 0, first=(piece1, sent)
    )
    sum2 = Scatter(piece2, theirs2, shard_count, 0)
    spread2 = spread(2, (0,), place_of, lookup, kernel_rows, grad2, first=(piece2,), time=BLOCK)
    far_rows = swap(after(far_rows, piece2), 2)
    near_rows = swap(after(near_rows, piece2), 1)
    sent = sum0.advance(spread2)
    second_sent = second.advance(spread2)
    spread2_after = spread(2, (1,), place_of, lookup, kernel_rows, grad2, first=(spread2, sent, second_sent), time=BLOCK)
    spread3 = spread(3, (0,), place_of, lookup, kernel_rows, grad3, first=(spread2_after,), time=BLOCK)
    sent = sum1.advance(spread3)
    spread3_after = spread(3, (1,), place_of, lookup, kernel_rows, grad3, first=(spread3, sent, sum0.got, second.got), time=BLOCK)

    sent = sum2.advance(spread3_after)
    second = second.finish()
    grad_hidden, grad_output, grad_proj = second_out(second.mine, second.got, wide)
    grad_padded, to_below, to_above = finish(
        place_of, (spread0, spread1, spread2, spread2_after, spread3, spread3_after), first=(sent, grad_hidden)
    )
    cross_rows = swap(after(far_rows, spread3), 1)
    from_above = lax.ppermute(to_below, "pts", downs)
    from_below = lax.ppermute(to_above, "pts", ups)
    sent = sum1.advance(grad_padded)
    sent = sum2.advance(sent)
    block_out, grad_points = rows_out(
        place_of, grad_padded, from_below, from_above, block0, points0, near_rows, far_rows, cross_rows,
        first=(sent,),
    )

    grad_conv, grad_cpe, grad_qkv, *lines = grads_out([s.finish() for s in (sum0, sum1, sum2)], chunk, width)
    small = [line.reshape(-1) for line in lines[: VECTORS + 1]]
    return (
        block_out,
        grad_points,
        grad_conv.transpose(0, 2, 1),
        small[0],
        grad_cpe.T,
        *small[1:6],
        grad_qkv.transpose(1, 0, 2),
        lines[VECTORS + 1],
        grad_proj.T,
        small[8],
        small[6],
        small[7],
        grad_hidden,
        small[10],
        grad_output.T,
        small[9],
    )


def solution(mesh):
    return jax.shard_map(
        shards,
        mesh=mesh,
        in_specs=(
            P("pts", "blk"),
            P("pts", None),
            P("pts"),
            P(None, "blk", None),
            P("blk"),
            P("blk", None),
            P("blk"),
            P("blk"),
            P("blk"),
            P("blk"),
            P("blk"),
            P(None, None, "blk"),
            P(None, "blk"),
            P("blk", None),
            P("blk"),
            P("blk"),
            P("blk"),
            P(None, "blk"),
            P("blk"),
            P("blk", None),
            P("blk"),
            P("pts", "blk"),
        ),
        out_specs=(
            P("pts", "blk"),
            P("pts", "blk"),
            P(None, "blk", "pts"),
            P("blk"),
            P("blk", "pts"),
            P("blk"),
            P("blk"),
            P("blk"),
            P("blk"),
            P("blk"),
            P("pts", None, "blk"),
            P(None, "blk"),
            P("blk", "pts"),
            P("blk"),
            P("blk"),
            P("blk"),
            P("pts", "blk"),
            P("blk"),
            P("blk", "pts"),
            P("blk"),
        ),
        check_vma=False,
    )
```

```python
import functools
import math

import jax
import jax.numpy as jnp
from jax import lax
from jax.experimental import pallas as pl
from jax.experimental.pallas import tpu as pltpu
from jax.sharding import PartitionSpec as P

HEAD_DIM = 16
PATCH = 1024
KERNEL = 27
REACH = 256
EPS = 1e-05
LOG2E = math.log2(math.e)
BF = jnp.bfloat16
F32 = jnp.float32
NN = ((1,), (0,))
NT = ((1,), (1,))
TN = ((0,), (0,))
VMEM = pl.BlockSpec(memory_space=pltpu.VMEM)
SMEM = pl.BlockSpec(memory_space=pltpu.SMEM)
HBM = pl.BlockSpec(memory_space=pltpu.HBM)
ANY = pl.BlockSpec(memory_space=pl.ANY)
TILE = 256


def dot(a, b, dims):
    return lax.dot_general(a, b, (dims, ((), ())), preferred_element_type=F32)


def struct(shape, kind):
    return jax.ShapeDtypeStruct(shape, kind)


TIMES = {
    "prepare": 10,  "conv_forward": 7.5, "first_rows": 2.5, "triple_half": 2, "attend_forward": 21, "second_rows": 10,
    "second_send": 1.5, "attend_backward": 19, "second_keep": 2.5, "layer_grad": 1, "third_rows": 2.3, "cpe_weights": 0.1,
    "spread": 7, "third_weights": 0.1, "conv_weight_grad": 0.1, "finish": 1.0, "rows_out": 2.0, "fold": 0.05, "second_out": 0.1, "grads_out": 0.1,
}
FACTOR = 0.3
TINY = 0.1
BLOCK = 4.2


def call(name, kernel, inputs, outputs, scratch=(), mib=8, grid=None, first=(), time=None):
    count, extra = len(inputs), len(first)

    def body(*refs):
        kernel(*refs[:count], *refs[count + extra :])

    options = {} if grid is None else {"grid": grid}
    result = pl.pallas_call(
        body,
        out_shape=[o for o, spec in outputs],
        in_specs=[spec for a, spec in inputs] + [ANY] * extra,
        out_specs=[spec for o, spec in outputs],
        scratch_shapes=list(scratch),
        compiler_params=pltpu.CompilerParams(vmem_limit_bytes=mib * 2**20),
        cost_estimate=pl.CostEstimate(flops=int((time or TIMES[name]) * FACTOR * 1.15e9), bytes_accessed=0, transcendentals=0),
        name=name,
        **options,
    )(*[pltpu.with_memory_space_constraint(a, pltpu.HBM) if spec is HBM else a for a, spec in inputs], *first)
    return result[0] if len(result) == 1 else result


def vm(*arrays):
    return [(a, VMEM) for a in arrays]


def split3(values):
    high = values.astype(BF)
    rest = values - high.astype(F32)
    middle = rest.astype(BF)
    return high, middle, (rest - middle.astype(F32)).astype(BF)


def joined(rows, width):
    rows = rows.astype(F32)
    return (rows[:, :width] + rows[:, width : 2 * width]) + rows[:, 2 * width : 3 * width]


def in_order(pieces, me):
    core, chip = (me & 1) == 1, (me >> 1) == 1
    a, b = jnp.where(core, pieces[1], pieces[0]), jnp.where(core, pieces[0], pieces[1])
    c, d = jnp.where(core, pieces[3], pieces[2]), jnp.where(core, pieces[2], pieces[3])
    return [
        jnp.where(chip, c, a),
        jnp.where(chip, d, b),
        jnp.where(chip, a, c),
        jnp.where(chip, b, d),
    ]


def folded(source, start, target, row, sems, rows):
    part, width = rows // 4, source.shape[1]
    copies = []
    for j in range(4):
        copies.append(
            pltpu.make_async_copy(
                source.at[pl.ds(pl.multiple_of(start + j * part, 16), part), :],
                target.at[row : row + part, j * width : (j + 1) * width],
                sems(),
            )
        )
    return copies


def unfolded(pack, row, at, rows):
    part, width = rows // 4, pack.shape[1] // 4
    return jnp.concatenate(
        [
            pack[row : row + part, j * width : (j + 1) * width]
            for j in range(at.start // part, at.stop // part)
        ],
        axis=0,
    )


class Plan:
    def __init__(self, rows, width):
        fold = rows // 4
        self.first_cpe = 3 * width
        self.first_points = 4 * width
        self.first_small = 4 * width + 2 * fold
        self.first_rows = self.first_small + 16
        self.near_points = width
        self.near_small = width + fold
        self.near_rows = self.near_small + 16


def counter(sems):
    state = [0]

    def take():
        state[0] += 1
        return sems.at[state[0] - 1]

    return take


VECTORS = 10


def prepare_kernel(
    plan, rows, place_of, turned_in, cpe, points, patch, *refs
):
    vectors, refs = refs[:VECTORS], refs[VECTORS:]
    hidden_bias, query_bias, away, near, turned, small, patch_row, terms, lines, long_line, pair, straight, sems = refs
    me = place_of[0]
    width = points.shape[1]
    take = counter(sems)
    copies = [
        pltpu.make_async_copy(cpe, away.at[plan.first_cpe : plan.first_cpe + width, :], take()),
        pltpu.make_async_copy(cpe, near.at[0:width, :], take()),
    ]
    for e in (2, 3):
        copies += folded(points, (me ^ e) * rows, away, plan.first_points + (e - 2) * rows // 4, take, rows)
    copies += folded(points, (me ^ 1) * rows, near, plan.near_points, take, rows)
    straight_copy = pltpu.make_async_copy(turned_in, straight, take())
    straight_copy.start()
    for copy in copies:
        copy.start()
    loads = [pltpu.make_async_copy(vector, lines.at[r], take()) for r, vector in enumerate(vectors)]
    loads.append(pltpu.make_async_copy(hidden_bias, long_line, take()))
    loads.append(pltpu.make_async_copy(query_bias, pair, take()))
    for copy in loads:
        copy.start()
    for e in (0, 1):
        at = pl.ds(pl.multiple_of((me ^ e) * rows, rows), rows)
        loads.append(pltpu.make_async_copy(patch.at[:, at], patch_row.at[:, e * rows : (e + 1) * rows], take()))
        loads[-1].start()
    straight_copy.wait()
    for t in range(3):
        turned[t * width : (t + 1) * width, :] = straight[t].T
    for copy in loads:
        copy.wait()
    for r in range(VECTORS):
        small[r : r + 1, :] = lines[r]
    for i in range(4):
        small[VECTORS + i : VECTORS + i + 1, :] = long_line[:, i * width : (i + 1) * width]
    small[VECTORS + 4 :, :] = pair[...]
    high, middle, low = split3(small[...])
    terms[...] = jnp.concatenate([high, middle, low, jnp.zeros_like(low)], axis=1)
    last = [
        pltpu.make_async_copy(turned, away.at[0 : 3 * width, :], take()),
        pltpu.make_async_copy(terms, away.at[plan.first_small :, :], take()),
        pltpu.make_async_copy(terms, near.at[plan.near_small :, :], take()),
    ]
    for copy in last:
        copy.start()
    for copy in copies + last:
        copy.wait()


def prepare(plan, place_of, turned, cpe, points, patch, vectors, hidden_bias, query_bias, first=()):
    row_count, width = points.shape
    wide = cpe.shape[1]
    lines = [v.reshape(1, -1) for v in (*vectors, hidden_bias)]
    return call(
        "prepare",
        functools.partial(prepare_kernel, plan, row_count // 4),
        [(place_of, SMEM), (turned, HBM), (cpe, HBM), (points, HBM), (patch.reshape(1, -1), HBM)]
        + [(v, HBM) for v in (*lines, query_bias)],
        [
            (struct((plan.first_rows, wide), BF), HBM),
            (struct((plan.near_rows, wide), BF), HBM),
            (struct((3 * width, wide), BF), VMEM),
            (struct((16, width), F32), VMEM),
            (struct((1, row_count // 2), jnp.int32), VMEM),
        ],
        [
            pltpu.VMEM((16, wide), BF),
            pltpu.VMEM((VECTORS, 1, width), F32),
            pltpu.VMEM((1, 4 * width), F32),
            pltpu.VMEM((2, width), F32),
            pltpu.VMEM(turned.shape, BF),
            pltpu.SemaphoreType.DMA((17 + VECTORS + 5,)),
        ],
        first=first,
    )


def one_hot(place):
    spots = lax.broadcasted_iota(jnp.int32, (256, 256), 0).astype(F32).astype(BF)
    place = jnp.broadcast_to(place.astype(F32).astype(BF), (256, 256))
    return jnp.where(spots == place, jnp.ones((), BF), jnp.zeros((), BF))


def conv_kernel(e, packs, place_of, low, points, high, lookup, weight, *refs):
    sources, refs = refs[:packs], refs[packs:]
    conv, conv_after, gathered = refs[:3]
    away, near = refs[3:5] if packs else (None, None)
    turned, picked, sems = refs[-3:]
    me = place_of[0]
    width = points.shape[1]
    rows = picked.shape[1]
    quarter = me ^ e
    take = counter(sems)
    copies = []
    if packs:
        hidden, output, proj, upstream = sources
        wide, fold = hidden.shape[1], rows // 4
        start = 2 * wide + width
        for target in (away, near):
            copies.append(pltpu.make_async_copy(output, target.at[0:wide, :], take()))
            copies.append(pltpu.make_async_copy(proj, target.at[wide : wide + width, :], take()))
            copies.append(pltpu.make_async_copy(hidden, target.at[wide + width : start, :], take()))
        copies += folded(upstream, (me ^ 2) * rows, away, start, take, rows)
        copies += folded(upstream, (me ^ 3) * rows, away, start + fold, take, rows)
        copies += folded(upstream, (me ^ 1) * rows, near, start, take, rows)
        at = slice(start + fold, start + 3 * fold)
        copies.append(pltpu.make_async_copy(output.at[: 2 * fold, :], near.at[at, :], take()))
        for copy in copies:
            copy.start()
    base = place_of[1] * points.shape[0] + quarter * rows - REACH
    last = points.shape[0] // 256 - 1
    for j in range(rows // 256 + 2):
        spot = quarter * (rows // 256) - 1 + j
        at = pl.multiple_of(jnp.clip(spot, 0, last) * 256, 256)
        piece = points[pl.ds(at, 256), :]
        piece = jnp.where(spot < 0, low[...], jnp.where(spot > last, high[...], piece))
        turned[j * width : (j + 1) * width, :] = piece.T
    step = KERNEL // 3
    for b in range(rows // 256):
        cols = slice(b * 256, (b + 1) * 256)
        left = turned[b * width : (b + 3) * width, :]
        for k in range(KERNEL):
            spot = lookup[k : k + 1, pl.ds(pl.multiple_of(quarter * rows + b * 256, 256), 256)] - base
            part = jnp.broadcast_to(lax.shift_right_logical(spot, 8) - b, (width, 256))
            three = dot(left, one_hot(jnp.bitwise_and(spot, 255)), NN)
            values = jnp.where(
                part == 0,
                three[:width],
                jnp.where(part == 1, three[width : 2 * width], three[2 * width :]),
            )
            picked[k * width : (k + 1) * width, cols] = values.astype(BF)
            if k % step == step - 1:
                at = slice((k + 1 - step) * width, (k + 1) * width)
                copies.append(pltpu.make_async_copy(picked.at[at, cols], gathered.at[at, cols], take()))
                copies[-1].start()
        (conv, conv_after)[b][...] = dot(picked[:, cols], weight[...], TN).astype(conv.dtype)
    for copy in copies:
        copy.wait()


def conv_forward(e, place_of, low, points, high, lookup, weight, kind, packs=(), first=(), time=None):
    rows, width, wide = points.shape[0] // 4, points.shape[1], weight.shape[1]
    outputs = [(struct((rows // 2, wide), kind), VMEM)] * 2 + [(struct((KERNEL * width, rows), BF), HBM)]
    if packs:
        size = 2 * wide + width + rows // 4
        outputs += [(struct((size + rows // 4, wide), BF), HBM), (struct((size + rows // 2, wide), BF), HBM)]
    return call(
        "conv_forward",
        functools.partial(conv_kernel, e, len(packs)),
        [(place_of, SMEM)] + vm(low, points, high, lookup, weight) + [(p, HBM) for p in packs],
        outputs,
        [
            pltpu.VMEM(((rows // 256 + 2) * width, 256), BF),
            pltpu.VMEM((KERNEL * width, rows), BF),
            pltpu.SemaphoreType.DMA((6 * rows // 512 + (19 if packs else 0),)),
        ],
        first=first,
        time=time,
    )


def spread_kernel(e, blocks, place_of, lookup, weight, grads, out, upstream):
    width = out.shape[0]
    rows = grads.shape[0]
    quarter = place_of[0] ^ e
    base = place_of[1] * lookup.shape[1] + quarter * rows - REACH
    out[...] = jnp.zeros(out.shape, F32)
    step = 9
    for n, b in enumerate(blocks):
        cols = slice(b * 256, (b + 1) * 256)
        upstream[...] = dot(weight[...], grads[cols, :], NT)
        for s in range(KERNEL // step):
            left, right = [], []
            for k in range(s * step, (s + 1) * step):
                spot = lookup[k : k + 1, pl.ds(pl.multiple_of(quarter * rows + b * 256, 256), 256)] - base
                part = jnp.broadcast_to(lax.shift_right_logical(spot, 8) - b, (width, 256))
                mine = upstream[k * width : (k + 1) * width, :]
                left.append(
                    jnp.concatenate(
                        [jnp.where(part == i, mine, 0.0).astype(BF) for i in range(3)], axis=0
                    )
                )
                right.append(one_hot(jnp.bitwise_and(spot, 255)))
            three = dot(jnp.concatenate(left, axis=1), jnp.concatenate(right, axis=1), NT)
            for i in range(3):
                at = slice((n + i) * 256, (n + i + 1) * 256)
                out[:, at] = out[:, at] + three[i * width : (i + 1) * width]


def spread(e, blocks, place_of, lookup, weight, grads, first=(), time=None):
    width = weight.shape[0] // KERNEL
    return call(
        "spread",
        functools.partial(spread_kernel, e, blocks),
        [(place_of, SMEM)] + vm(lookup, weight, grads),
        [(struct((width, 256 * len(blocks) + 2 * REACH), F32), VMEM)],
        [pltpu.VMEM((KERNEL * width, 256), F32)],
        first=first,
        time=time,
    )


def halves(count, stage):
    keep = [r for r in range(count) if not (r >> stage) & 1]
    return keep, [r ^ (1 << stage) for r in keep]


def conv_weight_kernel(blocks, stage, start, count, extra, place_of, *refs):
    gathered, grads, refs = refs[:4], refs[4:8], refs[8:]
    thirds, (mine, theirs, total) = refs[:extra], refs[extra:]
    tile = 384
    for i in range(count // tile):
        rows = slice(start + i * tile, start + (i + 1) * tile)
        cols = slice(i * tile, (i + 1) * tile)
        total[:, cols] = sum(dot(a[rows, :], g[...], NN) for a, g in zip(gathered, grads)).T.astype(BF)
    size = total.shape[0] // blocks
    for out, slots in zip((mine, theirs), halves(blocks, stage)):
        for i, r in enumerate(slots):
            at = pl.multiple_of((place_of[1] ^ r) * size, size)
            out[i, :, 0:count] = total[pl.ds(at, size), :]
            if extra:
                out[i, :, count:] = (thirds[0][r].astype(F32) + thirds[1][r].astype(F32)).astype(BF)


def conv_weight_grad(place_of, gathered, grads, start, count, blocks, stage, thirds=(), first=()):
    wide = grads[0].shape[1]
    cols = count + (thirds[0].shape[2] if thirds else 0)
    half = struct((blocks // 2, wide // blocks, cols), BF)
    return call(
        "conv_weight_grad",
        functools.partial(conv_weight_kernel, blocks, stage, start, count, len(thirds)),
        [(place_of, SMEM)] + vm(*gathered, *grads, *thirds),
        vm(half, half),
        [pltpu.VMEM((wide, count), BF)],
        first=first,
    )


def finish_kernel(place_of, s0, s1, s2, s2_after, s3, s3_after, out, low, high):
    me = place_of[0]
    rows = s0.shape[1] - 2 * REACH
    ends = [s[:, 0:256] for s in (s0, s1, s2, s3)], [s[:, 768:] for s in (s0, s1)] + [s[:, 512:] for s in (s2_after, s3_after)]
    inner = [
        [s[:, 256:512] for s in (s0, s1)]
        + [a[:, 256:512] + b[:, 0:256] for a, b in ((s2, s2_after), (s3, s3_after))],
        [s[:, 512:768] for s in (s0, s1)]
        + [a[:, 512:768] + b[:, 256:512] for a, b in ((s2, s2_after), (s3, s3_after))],
    ]
    parts = [in_order(p, me) for p in (ends[0], inner[0], inner[1], ends[1])]
    out[...] = jnp.zeros(out.shape, F32)
    for q in range(4):
        for i, part in enumerate(parts):
            at = slice(q * rows + i * 256, q * rows + (i + 1) * 256)
            out[:, at] = out[:, at] + part[q]
    low[...] = out[:, :REACH].astype(BF)
    high[...] = out[:, out.shape[1] - REACH :].astype(BF)


def finish(place_of, spreads, first=()):
    width, span = spreads[0].shape
    total = 4 * (span - 2 * REACH) + 2 * REACH
    return call(
        "finish",
        finish_kernel,
        [(place_of, SMEM)] + vm(*spreads),
        [(struct((width, total), F32), VMEM)] + [(struct((width, REACH), BF), VMEM)] * 2,
        first=first,
    )


def rows_out_kernel(place_of, inside, below, above, block, own, near, far, cross, block_out, out):
    rows, width = own.shape
    me = place_of[0]
    pieces = in_order([block[...], near[:, :width], far[:, :width], cross[:, width : 2 * width]], me)
    for q in range(4):
        block_out[q * rows : (q + 1) * rows, :] = pieces[q]
    pieces = [own[...], near[:, width:], far[:, 2 * width : 3 * width], cross[:, 3 * width :]]
    pieces = in_order(pieces, me)
    for q in range(4):
        total = inside[:, REACH + q * rows : REACH + (q + 1) * rows].T + pieces[q].astype(F32)
        out[q * rows : (q + 1) * rows, :] = total
    out[:REACH, :] = out[:REACH, :] + below[...].astype(F32).T
    last = out.shape[0] - REACH
    out[last:, :] = out[last:, :] + above[...].astype(F32).T


def rows_out(place_of, inside, below, above, block, own, near, far, cross, first=()):
    rows, width = own.shape
    return call(
        "rows_out",
        rows_out_kernel,
        [(place_of, SMEM)] + vm(inside, below, above, block, own, near, far, cross),
        vm(struct((4 * rows, width), BF), struct((4 * rows, width), F32)),
        first=first,
    )


def three_rows(high, middle, low):
    spots = lax.broadcasted_iota(jnp.int32, (16, high.shape[1]), 0)
    picked = jnp.where(
        spots == 0,
        high.astype(F32),
        jnp.where(spots == 1, middle.astype(F32), jnp.where(spots == 2, low.astype(F32), 0.0)),
    )
    return picked.astype(BF)


def one_rows(length, count):
    spots = lax.broadcasted_iota(jnp.int32, (16, length), 0)
    return jnp.where(spots < count, 1.0, 0.0).astype(BF)


def patch_codes(patch):
    shape = (32, patch.shape[1])
    spots = lax.broadcasted_iota(jnp.int32, shape, 0)
    bits = jnp.bitwise_and(
        lax.shift_right_logical(jnp.broadcast_to(patch, shape), jnp.bitwise_and(spots, 15)), 1
    )
    bits = jnp.where(spots < 16, bits, 1 - bits)
    return jnp.where(bits == 1, 1.0, 0.0).astype(BF), jnp.where(bits == 1, 0.0, -1e30).astype(BF)


def fixed_rows(patch, query_side, key_side):
    length = patch.shape[1]
    left, right = patch_codes(patch)
    key_side[48:64, :] = one_rows(length, 3)
    key_side[64:96, :] = left
    query_side[64:96, :] = right
    key_side[96:128, :] = jnp.zeros((32, length), BF)
    query_side[96:128, :] = jnp.zeros((32, length), BF)


def column(row):
    return jnp.broadcast_to(row, (128, 128)).T[:, 0:1]


def triple_rows(values, weights, smalls, out, cols):
    width = out.shape[1] // 2
    for t in range(3):
        for i in range(2):
            piece = dot(weights[i][t * width : (t + 1) * width, :], values, NT)
            if t != 1:
                piece = piece + column(smalls[i][14 + t // 2 : 15 + t // 2, :])
            out[t, i * width : (i + 1) * width, cols] = piece.astype(BF)


def triple_half_kernel(plan, values, turned, away, small, out):
    smalls = (small[...], joined(away[plan.first_small :, :], small.shape[1]))
    triple_rows(values[...], (turned, away), smalls, out, slice(0, values.shape[0]))


def triple_half(plan, values, turned, away, small):
    return call(
        "triple_half",
        functools.partial(triple_half_kernel, plan),
        vm(values, turned, away, small),
        [(struct((3, 2 * small.shape[1], values.shape[0]), BF), VMEM)],
    )


def attend_forward_kernel(
    plan, heads, tile, mine, other, turned, away, small, patch, triple, total, keep, send, logs, query_side, key_side, value_side
):
    rows = mine.shape[2]
    length = 2 * rows
    for t in range(3):
        triple[t, :, :rows] = mine[t]
    smalls = (small[...], joined(away[plan.first_small :, :], small.shape[1]))
    triple_rows(other[...], (turned, away), smalls, triple, slice(rows, length))
    fixed_rows(patch[...], query_side, key_side)
    value_side[16:32, :] = one_rows(length, 1)

    @pl.loop(0, heads)
    def _(h):
        at = pl.ds(pl.multiple_of(h * HEAD_DIM, HEAD_DIM), HEAD_DIM)
        query = triple[0, at, :].astype(F32) * (HEAD_DIM**-0.5 * LOG2E)
        key = triple[1, at, :]
        high, middle, low = split3(query)
        query_side[0:16, :] = high
        query_side[16:32, :] = middle
        query_side[32:48, :] = low
        query_side[48:64, :] = jnp.zeros((16, length), BF)
        key_side[0:16, :] = key
        key_side[16:32, :] = key
        key_side[32:48, :] = key
        value_side[0:16, :] = triple[2, at, :]
        wide_key = key.astype(F32)
        bound = jnp.max(jnp.sum(query * query, axis=0)) * jnp.max(
            jnp.sum(wide_key * wide_key, axis=0)
        )
        logs[pl.ds(h, 1), :] = jnp.zeros((1, length), F32)

        @pl.when(jnp.logical_not(bound < 4096.0))
        def _():
            for t in range(length // tile):
                cols = slice(t * tile, (t + 1) * tile)
                top = jnp.max(dot(key_side[...], query_side[:, cols], TN), axis=0, keepdims=True)
                query_side[48:64, cols] = three_rows(*split3(-top))
                logs[pl.ds(h, 1), cols] = top

        for t in range(length // tile):
            cols = slice(t * tile, (t + 1) * tile)
            weights = jnp.exp2(dot(key_side[...], query_side[:, cols], TN)).astype(BF)
            mixed = dot(value_side[...], weights, NN)
            sums = mixed[16:17, :]
            mixed = mixed[0:16, :] * (1.0 / sums)
            total[at, cols] = mixed
            if t * tile < rows:
                keep[at, cols] = mixed.astype(BF)
            else:
                send[at, t * tile - rows : (t + 1) * tile - rows] = mixed.astype(BF)
            logs[pl.ds(h, 1), cols] = logs[pl.ds(h, 1), cols] + jnp.log2(sums)


def attend_forward(plan, mine, other, turned, away, small, patch, first=()):
    width, rows = mine.shape[1:]
    length = 2 * rows
    heads = width // HEAD_DIM
    return call(
        "attend_forward",
        functools.partial(attend_forward_kernel, plan, heads, 512),
        vm(mine, other, turned, away, small, patch),
        [
            (struct((3, width, length), BF), VMEM),
            (struct((width, length), F32), VMEM),
            (struct((width, rows), BF), VMEM),
            (struct((width, rows), BF), VMEM),
            (struct((heads, length), F32), VMEM),
        ],
        [
            pltpu.VMEM((128, length), BF),
            pltpu.VMEM((128, length), BF),
            pltpu.VMEM((32, length), BF),
        ],
        first=first,
    )


def attend_backward_kernel(
    first, heads, tile, triple, patch, mine, other, mixed, logs, out, query_side, key_side, value_side, grad_side, grad_value, grad_key
):
    length = triple.shape[2]
    fixed_rows(patch[...], query_side, key_side)
    value_side[16:32, :] = one_rows(length, 3)

    @pl.loop(0, heads)
    def _(h):
        at = pl.ds(pl.multiple_of((h + first) * HEAD_DIM, HEAD_DIM), HEAD_DIM)
        to = pl.ds(pl.multiple_of(h * HEAD_DIM, HEAD_DIM), HEAD_DIM)
        query, key = triple[0, at, :], triple[1, at, :]
        upstream = jnp.concatenate([mine[at, :], other[at, :]], axis=1)
        high, middle, low = split3(query.astype(F32) * (HEAD_DIM**-0.5 * LOG2E))
        query_side[0:16, :] = high
        query_side[16:32, :] = middle
        query_side[32:48, :] = low
        query_side[48:64, :] = three_rows(*split3(-logs[pl.ds(h + first, 1), :]))
        key_side[0:16, :] = key
        key_side[16:32, :] = key
        key_side[32:48, :] = key
        value_side[0:16, :] = triple[2, at, :]
        inner = jnp.sum(upstream.astype(F32) * mixed[at, :], axis=0, keepdims=True)
        grad_side[0:16, :] = upstream
        grad_side[16:32, :] = three_rows(*split3(-inner))
        for t in range(length // tile):
            cols = slice(t * tile, (t + 1) * tile)
            prob = jnp.exp2(dot(query_side[:, cols], key_side[...], TN))
            grad_prob = dot(grad_side[:, cols], value_side[...], TN)
            grad_score = (prob * grad_prob).astype(BF)
            value_part = dot(upstream[:, cols], prob.astype(BF), NN)
            key_part = dot(query[:, cols], grad_score, NN)
            out[0, to, cols] = (dot(key, grad_score, NT) * HEAD_DIM**-0.5).astype(BF)
            if t == 0:
                grad_value[...] = value_part
                grad_key[...] = key_part
            else:
                grad_value[...] += value_part
                grad_key[...] += key_part
        out[1, to, :] = (grad_key[...] * HEAD_DIM**-0.5).astype(BF)
        out[2, to, :] = grad_value[...].astype(BF)


def attend_backward(first_head, heads, triple, patch, mine, other, mixed, logs, first=()):
    length = triple.shape[2]
    return call(
        "attend_backward",
        functools.partial(attend_backward_kernel, first_head, heads, 512),
        vm(triple, patch, mine, other, mixed, logs),
        [(struct((3, heads * HEAD_DIM, length), BF), VMEM)],
        [
            pltpu.VMEM((128, length), BF),
            pltpu.VMEM((128, length), BF),
            pltpu.VMEM((32, length), BF),
            pltpu.VMEM((32, length), BF),
            pltpu.VMEM((16, length), F32),
            pltpu.VMEM((16, length), F32),
        ],
        mib=12,
        first=first,
    )


def norm_rows(values):
    average = jnp.mean(values, axis=1, keepdims=True)
    scaling = lax.rsqrt(
        jnp.mean(values * values, axis=1, keepdims=True) - average * average + EPS
    )
    return (values - average) * scaling, scaling


def norm_rows_back(upstream, normed, scaling, gain):
    scaled = upstream * gain
    return scaling * (
        scaled
        - jnp.mean(scaled, axis=1, keepdims=True)
        - normed * jnp.mean(scaled * normed, axis=1, keepdims=True)
    )


def cut(values):
    width = values.shape[1] // 4
    return [values[:, j * width : (j + 1) * width] for j in range(4)]


def add_rows(ref, row, values, first):
    total = jnp.sum(values, axis=0, keepdims=True)
    ref[row : row + 1, :] = total if first else ref[row : row + 1, :] + total


def small_vectors(plan, small, near, far, cross):
    width = small.shape[1]
    return [
        small[...],
        joined(near[plan.near_small :, :], width),
        joined(far[plan.first_small :, :], width),
        joined(cross[plan.first_small :, :], width),
    ]


def vectors(smalls, me):
    return jnp.concatenate(in_order(smalls, me), axis=1)


def cpe_rows(plan, weight, near, far, cross, me):
    width = weight.shape[0]
    at = slice(plan.first_cpe, plan.first_cpe + width)
    pieces = [weight[...], near[:width, :], far[at, :], cross[at, :]]
    return jnp.concatenate(in_order(pieces, me), axis=0)


def own_rows(ref, me, rows, at):
    return ref[pl.ds(pl.multiple_of(me * rows + at.start, at.stop - at.start), at.stop - at.start), :]


def first_rows_kernel(
    plan, place_of, part_low, part_high, close_low, close_high, away, points, small, weight, near, far, cross,
    layer, middle, normed_cpe, scaling_cpe, residual, normed, scaling,
):
    me = place_of[0]
    rows = 2 * part_low.shape[0]
    vec = vectors(small_vectors(plan, small, near, far, cross), me)
    vec = [vec[r : r + 1, :] for r in range(6)]
    weights = cpe_rows(plan, weight, near, far, cross, me)
    for t in range(rows // TILE):
        at = slice(t * TILE, (t + 1) * TILE)
        part, close = ((part_low, close_low), (part_high, close_high))[t * TILE * 2 // rows]
        low = (part[...] + close[...].astype(F32) + away[at, :].astype(F32) + vec[0]).astype(BF)
        middle[at, :] = low
        xhat, rate = norm_rows(dot(low, weights, NN) + vec[1])
        normed_cpe[at, :] = xhat
        scaling_cpe[at, :] = rate
        features = [
            own_rows(points, me, rows, at),
            unfolded(near, plan.near_points, at, rows),
            unfolded(far, plan.first_points, at, rows),
            unfolded(cross, plan.first_points + rows // 4, at, rows),
        ]
        features = jnp.concatenate(in_order(features, me), axis=1)
        sums = features.astype(F32) + xhat * vec[2] + vec[3]
        residual[at, :] = sums
        xhat, rate = norm_rows(sums)
        normed[at, :] = xhat
        scaling[at, :] = rate
        layer[at, :] = (xhat * vec[4] + vec[5]).astype(BF)


def first_rows(plan, place_of, parts, closes, away, points, small, weight, near, far, cross):
    rows, wide = away.shape
    full, thin, lower = struct((rows, wide), F32), struct((rows, 1), F32), struct((rows, wide), BF)
    return call(
        "first_rows",
        functools.partial(first_rows_kernel, plan),
        [(place_of, SMEM)] + vm(*parts, *closes, away, points, small, weight, near, far, cross),
        vm(lower, lower, full, thin, full, full, thin),
    )


def gelu_parts(u):
    scale = math.sqrt(2 / math.pi)
    square = u * u
    bent = jnp.tanh(u * (scale + (scale * 0.044715) * square))
    half = 0.5 + 0.5 * bent
    slope = half + u * (1.0 - bent * bent) * (0.5 * scale + (1.5 * 0.044715 * scale) * square)
    return u * half, slope


def second_rows_kernel(
    plan, place_of, keep, got, residual, out_grad, hidden, output, proj, small, near, far, cross, near2, far2, cross2,
    block0, block1, block_far, active, before, layer, upstream, carried, low, grad_keep, grad_send, hidden_sums, sums,
):
    me = place_of[0]
    rows, wide = residual.shape
    smalls = small_vectors(plan, small, near, far, cross)
    vec = vectors(smalls, me)
    vec = {r: vec[r : r + 1, :] for r in (6, 7, 8, 9)}
    biases = [jnp.concatenate([s[10 + i : 11 + i, :] for i in range(4)], axis=1) for s in smalls]
    width = keep.shape[0] // 2
    packs = (near2, far2, cross2)
    end = wide + width
    hiddens = [hidden] + [p.at[end : end + wide, :] for p in packs]
    last = end + wide
    outputs = [output] + [p.at[0:wide, :] for p in packs]
    projs = [proj[...]] + [p[wide:end, :] for p in packs]
    mine = jnp.concatenate([projs[0], projs[2]], axis=0)
    others = jnp.concatenate([projs[1], projs[3]], axis=0)
    for t in range(rows // TILE):
        at = slice(t * TILE, (t + 1) * TILE)
        base = residual[at, :] + vec[6] + dot(keep[:, at], mine, TN) + dot(got[:, at], others, TN)
        normed, scaling = norm_rows(base)
        lower = (normed * vec[7] + vec[8]).astype(BF)
        layer[at, :] = lower
        grads = [
            own_rows(out_grad, me, rows, at),
            unfolded(near2, last, at, rows),
            unfolded(far2, last, at, rows),
            unfolded(cross2, last + rows // 4, at, rows),
        ]
        grads = jnp.concatenate(in_order(grads, me), axis=1)
        upstream[at, :] = grads
        result = base + vec[9]
        grad_layer = None
        for e in range(4):
            act, slope = gelu_parts(dot(lower, hiddens[e][...], NN) + biases[e])
            act = act.astype(BF)
            active[e, at, :] = act
            result = result + dot(act, outputs[e][...], NN)
            pre = dot(grads, outputs[e][...], NT) * slope
            add_rows(hidden_sums, e, pre, t == 0)
            pre = pre.astype(BF)
            before[e, at, :] = pre
            piece = dot(pre, hiddens[e][...], NT)
            grad_layer = piece if e == 0 else grad_layer + piece
        result = in_order(cut(result.astype(BF)), me)
        block0[at, :] = result[0]
        block1[at, :] = result[1]
        block_far[at, 0:width] = result[2]
        block_far[at, width:] = result[3]
        wide_grads = grads.astype(F32)
        add_rows(sums, 0, grad_layer * normed, t == 0)
        add_rows(sums, 1, grad_layer, t == 0)
        add_rows(sums, 3, wide_grads, t == 0)
        carry = wide_grads + norm_rows_back(grad_layer, normed, scaling, vec[7])
        carried[at, :] = carry
        add_rows(sums, 2, carry, t == 0)
        carry = carry.astype(BF)
        low[at, :] = carry
        grad_keep[:, at] = dot(mine, carry, NT).astype(BF)
        grad_send[:, at] = dot(others, carry, NT).astype(BF)


def second_rows(plan, place_of, keep, got, residual, out_grad, weights, small, firsts, seconds):
    rows, wide = residual.shape
    lower, piece = struct((rows, wide), BF), struct((rows, wide // 4), BF)
    heads = struct(keep.shape, BF)
    return call(
        "second_rows",
        functools.partial(second_rows_kernel, plan),
        [(place_of, SMEM)] + vm(keep, got, residual, out_grad, *weights, small, *firsts, *seconds),
        vm(
            piece,
            piece,
            struct((rows, wide // 2), BF),
            struct((4, rows, wide), BF),
            struct((4, rows, wide), BF),
            lower,
            lower,
            struct((rows, wide), F32),
            lower,
            heads,
            heads,
            struct((4, wide), F32),
            struct((4, wide), F32),
        ),
        mib=12,
    )


def cut_rows(store, spot, cols, value, blocks):
    size = value.shape[0] // blocks
    for p in range(blocks):
        store(p ^ spot, cols, value[p * size : (p + 1) * size])


def second_weight_parts(i, e, blocks, spot, upstream, active, before, layer, low, attended, store):
    wide = layer.shape[1]
    width = attended.shape[0] // 2
    cut_rows(store, spot, slice(0, wide), dot(layer[...], before[e], TN), blocks)
    cut_rows(store, spot, slice(wide, 2 * wide), dot(upstream[...], active[e], TN), blocks)
    part = dot(attended[i * width : (i + 1) * width, :], low[...], NN)
    cut_rows(store, spot, slice(2 * wide, 2 * wide + width), part.T, blocks)


def second_send_kernel(blocks, place_of, upstream, active, before, layer, low, attended, out):
    for i, e in enumerate((1, 3)):

        def store(p, cols, value):
            out[i, p, :, cols] = value.astype(BF)

        second_weight_parts(i, e, blocks, place_of[1], upstream, active, before, layer, low, attended, store)


def second_send(place_of, blocks, upstream, active, before, layer, low, attended):
    wide = layer.shape[1]
    return call(
        "second_send",
        functools.partial(second_send_kernel, blocks),
        [(place_of, SMEM)] + vm(upstream, active, before, layer, low, attended),
        [(struct((2, blocks, wide // blocks, 2 * wide + attended.shape[0] // 2), BF), VMEM)],
    )


def second_keep_kernel(blocks, place_of, upstream, active, before, layer, low, attended, got, mine, far):
    for i, out in enumerate((mine, far)):

        def store(p, cols, value):
            out[p, :, cols] = (value + got[i, p, :, cols].astype(F32)).astype(BF)

        second_weight_parts(i, 2 * i, blocks, place_of[1], upstream, active, before, layer, low, attended, store)


def second_keep(place_of, blocks, upstream, active, before, layer, low, attended, got, first=()):
    out = struct(got.shape[1:], BF)
    return call(
        "second_keep",
        functools.partial(second_keep_kernel, blocks),
        [(place_of, SMEM)] + vm(upstream, active, before, layer, low, attended, got),
        vm(out, out),
        first=first,
    )


def third_weights_kernel(
    blocks, place_of, first_half, second_half, mine, other, cpe_keep, cpe_got, small_keep, own, far
):
    rows = mine.shape[0]
    width = first_half.shape[1]
    size = own.shape[1]
    empty = jnp.zeros((size - 16, width), BF)
    for i, (grads, out) in enumerate(((first_half, own), (second_half, far))):

        def store(p, cols, value):
            out[p, :, cols] = value.astype(BF)

        for t in range(3):
            part = dot(grads[t, :, :rows], mine[...], NN) + dot(grads[t, :, rows:], other[...], NN)
            cut_rows(store, place_of[1], slice(t * width, (t + 1) * width), part.T, blocks)
        sums = [jnp.sum(grads[t].astype(F32).T, axis=0, keepdims=True) for t in (0, 2)]
        small_got = sum(cpe_got[i, slot, size:, :].astype(F32) for slot in range(3))
        small = small_keep[i] + small_got + jnp.concatenate([jnp.zeros((14, width), F32)] + sums, axis=0)
        for p in range(blocks):
            out[p, :, 3 * width : 4 * width] = (
                cpe_keep[i, p].astype(F32) + cpe_got[i, p, :size, :].astype(F32)
            ).astype(BF)
            out[p, 0:16, 4 * width :] = small.astype(BF)
            if empty.shape[0]:
                out[p, 16:, 4 * width :] = empty


def third_weights(place_of, blocks, first_half, second_half, mine, other, cpe_keep, cpe_got, small_keep, first=()):
    wide = mine.shape[1]
    width = first_half.shape[1]
    out = struct((blocks, wide // blocks, 5 * width), BF)
    return call(
        "third_weights",
        functools.partial(third_weights_kernel, blocks),
        [(place_of, SMEM)] + vm(first_half, second_half, mine, other, cpe_keep, cpe_got, small_keep),
        vm(out, out),
        first=first,
    )


def layer_grad_kernel(half, first_half, second_half, turned, away, out):
    width = first_half.shape[1]
    rows = first_half.shape[2] // 2
    cols = slice(half * rows, (half + 1) * rows)
    total = None
    for t in range(3):
        at = slice(t * width, (t + 1) * width)
        for grads, weight in ((first_half, turned), (second_half, away)):
            piece = dot(grads[t, :, cols], weight[at, :], TN)
            total = piece if total is None else total + piece
    out[...] = total.astype(out.dtype)


def layer_grad(half, first_half, second_half, turned, away, kind, first=()):
    return call(
        "layer_grad",
        functools.partial(layer_grad_kernel, half),
        vm(first_half, second_half, turned, away),
        [(struct((first_half.shape[2] // 2, turned.shape[1]), kind), VMEM)],
        first=first,
    )


def third_rows_kernel(
    plan, place_of, part, close, carried, normed, scaling, normed_cpe, scaling_cpe, small, weight, near, far, cross, block1, block_far,
    conv_grad, points0, near_rows, far_rows, low, sums,
):
    me = place_of[0]
    vec = vectors(small_vectors(plan, small, near, far, cross), me)
    weights = cpe_rows(plan, weight, near, far, cross, me)
    width = points0.shape[1]
    for t in range(part.shape[0] // TILE):
        at = slice(t * TILE, (t + 1) * TILE)
        upstream = part[at, :] + close[at, :].astype(F32)
        xhat = normed[at, :]
        add_rows(sums, 4, upstream * xhat, t == 0)
        add_rows(sums, 5, upstream, t == 0)
        grads = carried[at, :] + norm_rows_back(upstream, xhat, scaling[at, :], vec[4:5, :])
        pieces = in_order(cut(grads.astype(BF)), me)
        points0[at, :] = pieces[0]
        near_rows[at, 0:width] = block1[at, :]
        near_rows[at, width:] = pieces[1]
        far_rows[at, 0 : 2 * width] = block_far[at, :]
        far_rows[at, 2 * width : 3 * width] = pieces[2]
        far_rows[at, 3 * width :] = pieces[3]
        xhat = normed_cpe[at, :]
        add_rows(sums, 2, grads * xhat, t == 0)
        add_rows(sums, 3, grads, t == 0)
        grads = norm_rows_back(grads, xhat, scaling_cpe[at, :], vec[2:3, :])
        add_rows(sums, 1, grads, t == 0)
        lower = grads.astype(BF)
        low[at, :] = lower
        result = dot(lower, weights, NT)
        add_rows(sums, 0, result, t == 0)
        conv_grad[at, :] = result.astype(BF)


def third_rows(plan, place_of, part, close, carried, normed, scaling, normed_cpe, scaling_cpe, small, weight, firsts, blocks):
    rows, wide = part.shape
    lower, piece = struct((rows, wide), BF), struct((rows, wide // 4), BF)
    return call(
        "third_rows",
        functools.partial(third_rows_kernel, plan),
        [(place_of, SMEM)]
        + vm(part, close, carried, normed, scaling, normed_cpe, scaling_cpe, small, weight, *firsts, *blocks),
        vm(lower, piece, struct((rows, wide // 2), BF), lower, lower, struct((6, wide), F32)),
    )


def cpe_weights_kernel(
    blocks, place_of, middle, low, sums_one, sums_two, hidden_sums, send, keep, small_keep, small_send
):
    me = place_of[0]
    width = middle.shape[1] // 4
    ones, twos = in_order(cut(sums_one[...]), me), in_order(cut(sums_two[...]), me)
    for e in range(4):
        out = (keep, send, keep, send)[e]

        def store(p, cols, value):
            out[e // 2, p, : value.shape[0], cols] = value.astype(BF)

        at = pl.ds(pl.multiple_of((e ^ me) * width, width), width)
        cut_rows(store, place_of[1], slice(0, width), dot(low[...], middle[:, at], TN), blocks)
        out = (small_keep, small_send, small_keep, small_send)[e]
        out[e // 2, 0:6, :] = ones[e]
        out[e // 2, 6:10, :] = twos[e]
        for i in range(4):
            out[e // 2, 10 + i : 11 + i, :] = hidden_sums[e : e + 1, i * width : (i + 1) * width]
        out[e // 2, 14:16, :] = jnp.zeros((2, width), F32)
    size = send.shape[2] - 16
    for i in range(2):
        for slot, term in enumerate(split3(small_send[i])):
            send[i, slot, size:, :] = term
        send[i, 3:, size:, :] = jnp.zeros((blocks - 3, 16, width), BF)


def cpe_weights(blocks, place_of, middle, low, sums_one, sums_two, hidden_sums, first=()):
    wide = middle.shape[1]
    send = struct((2, blocks, wide // blocks + 16, wide // 4), BF)
    keep = struct((2, blocks, wide // blocks, wide // 4), BF)
    small = (2, 16, wide // 4)
    return call(
        "cpe_weights",
        functools.partial(cpe_weights_kernel, blocks),
        [(place_of, SMEM)] + vm(middle, low, sums_one, sums_two, hidden_sums),
        vm(send, keep, struct(small, F32)),
        [pltpu.VMEM(small, F32)],
        first=first,
    )


def fold_kernel(keep, send, mine, got, kept, sent):
    for out, slots in ((sent, send), (kept, keep)):
        for i, j in enumerate(slots):
            out[i] = (mine[j].astype(F32) + got[j].astype(F32)).astype(BF)


def fold(mine, got, keep, send, first=()):
    out = struct((len(keep), *mine.shape[1:]), BF)
    return call("fold", functools.partial(fold_kernel, keep, send), vm(mine, got), vm(out, out), first=first)


def second_out_kernel(mine, got, hidden, output, proj):
    total = mine[0].astype(F32) + got[0].astype(F32)
    wide = hidden.shape[1]
    hidden[...] = total[:, :wide]
    output[...] = total[:, wide : 2 * wide]
    proj[...] = total[:, 2 * wide :]


def second_out(mine, got, wide):
    size, cols = mine.shape[1:]
    return call(
        "second_out",
        second_out_kernel,
        vm(mine, got),
        vm(struct((size, wide), F32), struct((size, wide), F32), struct((size, cols - 2 * wide), F32)),
    )


def grads_out_kernel(chunk, m0, g0, m1, g1, m2, g2, conv, cpe, qkv, *lines):
    width = cpe.shape[1]
    for i, (mine, got) in enumerate(((m0, g0), (m1, g1), (m2, g2))):
        part = mine[0, :, :chunk].astype(F32) + got[0, :, :chunk].astype(F32)
        for k in range(chunk // width):
            conv[i * (chunk // width) + k] = part[:, k * width : (k + 1) * width]
    third = m1[0, :, chunk:].astype(F32) + g1[0, :, chunk:].astype(F32)
    for t in range(3):
        qkv[t] = third[:, t * width : (t + 1) * width]
    cpe[...] = third[:, 3 * width : 4 * width]
    small = third[:16, 4 * width :]
    for r in range(VECTORS):
        lines[r][...] = small[r : r + 1, :]
    for i in range(4):
        lines[VECTORS][:, i * width : (i + 1) * width] = small[VECTORS + i : VECTORS + i + 1, :]
    lines[VECTORS + 1][...] = small[VECTORS + 4 :, :]


def grads_out(sums, chunk, width):
    size = sums[0].mine.shape[1]
    line = struct((1, width), F32)
    return call(
        "grads_out",
        functools.partial(grads_out_kernel, chunk),
        vm(*[a for s in sums for a in (s.mine, s.got)]),
        vm(struct((KERNEL, size, width), F32), struct((size, width), F32), struct((3, size, width), F32))
        + vm(*[line] * VECTORS, struct((1, 4 * width), F32), struct((2, width), F32)),
    )


def swap(values, e, axis="blk"):
    return lax.ppermute(values, axis, [(i, i ^ e) for i in range(lax.axis_size(axis))])


def after(values, *first):
    return lax.optimization_barrier((values, *first))[0]


def total_of(first, second):
    return (first.astype(F32) + second.astype(F32)).astype(BF)


class Scatter:
    def __init__(self, mine, theirs, count, stage):
        self.mine, self.theirs = mine, theirs
        self.numbers, _ = halves(count, stage)
        self.order = [stage] + [b for b in range(count.bit_length() - 1) if b != stage]
        self.got = swap(theirs, 1 << stage, "pts")

    def advance(self, *first):
        bit = self.order[1]
        keep = [j for j, r in enumerate(self.numbers) if not (r >> bit) & 1]
        send = [self.numbers.index(self.numbers[j] ^ (1 << bit)) for j in keep]
        self.mine, self.theirs = fold(self.mine, self.got, keep, send, first)
        self.numbers = [self.numbers[j] for j in keep]
        self.order = self.order[1:]
        self.got = swap(self.theirs, 1 << bit, "pts")
        return self.theirs

    def finish(self):
        while len(self.order) > 1:
            self.advance()
        return self


def shards(
    points, neighbours, patch_ids, conv_weight, conv_bias, cpe_weight, cpe_bias, cpe_gain, cpe_shift, first_gain,
    first_shift, qkv_weight, query_value_bias, proj_weight, proj_bias, second_gain, second_shift, hidden_weight,
    hidden_bias, output_weight, output_bias, out_grad,
):
    row_count, width = points.shape
    wide = conv_weight.shape[2]
    mine = row_count // 4
    shard_count = lax.axis_size("pts")
    me = lax.axis_index("blk")
    place_of = jnp.stack([me, lax.axis_index("pts")]).astype(jnp.int32)
    plan = Plan(mine, width)
    ups = [(i, i + 1) for i in range(shard_count - 1)]
    downs = [(i + 1, i) for i in range(shard_count - 1)]

    low = lax.ppermute(points[row_count - REACH :], "pts", ups)
    high = lax.ppermute(points[:REACH], "pts", downs)
    kernel_rows = conv_weight.reshape(KERNEL * width, wide)
    lookup = neighbours.T
    away_pack, near_pack, turned, small, patch_row = prepare(
        plan,
        place_of,
        qkv_weight.transpose(1, 0, 2),
        cpe_weight,
        points,
        patch_ids,
        (conv_bias, cpe_bias, cpe_gain, cpe_shift, first_gain, first_shift, proj_bias, second_gain, second_shift, output_bias),
        hidden_bias,
        query_value_bias,
        first=(high,),
    )
    far = swap(away_pack, 2)
    near = swap(near_pack, 1)

    *part3, gathered3, away_pack, near_pack = conv_forward(
        3, place_of, low, points, high, lookup, kernel_rows, BF, (hidden_weight, output_weight, proj_weight, out_grad),
    )
    got3 = [swap(p, 1) for p in part3]
    *part2, gathered2 = conv_forward(2, place_of, low, points, high, lookup, kernel_rows, BF, first=(part3[0],))
    far_part = swap(jnp.concatenate([total_of(a, b) for a, b in zip(part2, got3)], axis=0), 2)
    *part1, gathered1 = conv_forward(1, place_of, low, points, high, lookup, kernel_rows, BF, first=(part2[0],))
    *part0, gathered0 = conv_forward(0, place_of, low, points, high, lookup, kernel_rows, F32, first=(part1[0],), time=0.5)
    cross = swap(after(far, part2[0]), 1)
    close_part = [swap(p, 1) for p in part1]
    firsts = (near, far, cross)
    layer_one, conv_low, normed_cpe, scaling_cpe, residual_one, normed_one, scaling_one = first_rows(
        plan, place_of, part0, close_part, far_part, points, small, cpe_weight, *firsts
    )
    other_one = swap(layer_one, 1)
    far2 = swap(after(away_pack, part1[0]), 2)
    near2 = swap(near_pack, 1)


    half = triple_half(plan, layer_one, turned, far, small)
    triple, mixed, keep, send, logs = attend_forward(plan, half, other_one, turned, far, small, patch_row)
    got = swap(send, 1)
    cross2 = swap(after(far2, send), 1)
    (
        block0, block1, block_far, active, before, layer_two, upstream, carried, carried_low, grad_keep, grad_send,
        sum_hidden_bias, sums_two,
    ) = second_rows(
        plan, place_of, keep, got, residual_one, out_grad, (hidden_weight, output_weight, proj_weight), small, firsts,
        (near2, far2, cross2),
    )
    grad_got = swap(grad_send, 1)

    weights_send = second_send(place_of, shard_count, upstream, active, before, layer_two, carried_low, got)
    weights_got = swap(after(weights_send, grad_got), 1)
    heads = width // HEAD_DIM
    grad_first = attend_backward(
        0, heads, triple, patch_row, grad_keep, grad_got, mixed, logs, first=(weights_send,)
    )
    weights_mine, weights_far = second_keep(
        place_of, shard_count, upstream, active, before, layer_two, carried_low, keep, weights_got, first=(grad_first,)
    )
    weights_far = swap(weights_far, 2)
    grad_second = attend_backward(
        heads, heads, triple, patch_row, grad_keep, grad_got, mixed, logs, first=(weights_mine,)
    )
    layer_send = layer_grad(1, grad_first, grad_second, turned, far, BF)
    layer_got = swap(layer_send, 1)
    layer_part = layer_grad(0, grad_first, grad_second, turned, far, F32, first=(layer_send,))
    conv_grad, points0, near_rows, far_rows, cpe_low, sums_one = third_rows(
        plan, place_of, layer_part, layer_got, carried, normed_one, scaling_one, normed_cpe, scaling_cpe, small, cpe_weight, firsts, (block1, block_far)
    )
    grad0 = conv_grad
    grad2 = swap(grad0, 2)
    grad1 = swap(grad0, 1)
    second_mine, second_theirs = fold(weights_mine, weights_far, *halves(shard_count, 0))
    second = Scatter(second_mine, second_theirs, shard_count, 0)
    spread0 = spread(0, (0, 1), place_of, lookup, kernel_rows, grad0, first=(weights_far,), time=TINY)
    cpe_send, cpe_keep, small_keep = cpe_weights(
        shard_count, place_of, conv_low, cpe_low, sums_one, sums_two, sum_hidden_bias, first=(spread0,)
    )
    cpe_got = swap(cpe_send, 1)
    third_mine, third_far = third_weights(
        place_of, shard_count, grad_first, grad_second, layer_one, other_one, cpe_keep, cpe_got, small_keep,
        first=(spread0, grad2, second.got),
    )
    grad3 = swap(after(grad2, cpe_send), 1)

    gathered = (gathered0, gathered1, gathered2, gathered3)
    grads = (grad0, grad1, grad2, grad3)
    chunk = KERNEL // 3 * width
    third_far = swap(after(third_far, grad2), 2)
    piece0, theirs0 = conv_weight_grad(
        place_of, gathered, grads, 0, chunk, shard_count, 0, first=(third_mine,)
    )
    sum0 = Scatter(piece0, theirs0, shard_count, 0)
    second_sent = second.advance(piece0)
    spread1 = spread(1, (0, 1), place_of, lookup, kernel_rows, grad1, first=(piece0, second_sent), time=TINY)
    piece1, theirs1 = conv_weight_grad(
        place_of, gathered, grads, chunk, chunk, shard_count, 0, thirds=(third_mine, third_far), first=(spread1,)
    )
    sum1 = Scatter(piece1, theirs1, shard_count, 0)
    sent = sum0.advance(piece1)
    piece2, theirs2 = conv_weight_grad(
        place_of, gathered, grads, 2 * chunk, chunk, shard_count, 0, first=(piece1, sent)
    )
    sum2 = Scatter(piece2, theirs2, shard_count, 0)
    spread2 = spread(2, (0,), place_of, lookup, kernel_rows, grad2, first=(piece2,), time=BLOCK)
    far_rows = swap(after(far_rows, piece2), 2)
    near_rows = swap(after(near_rows, piece2), 1)
    sent = sum0.advance(spread2)
    second_sent = second.advance(spread2)
    spread2_after = spread(2, (1,), place_of, lookup, kernel_rows, grad2, first=(spread2, sent, second_sent), time=BLOCK)
    spread3 = spread(3, (0,), place_of, lookup, kernel_rows, grad3, first=(spread2_after,), time=BLOCK)
    sent = sum1.advance(spread3)
    spread3_after = spread(3, (1,), place_of, lookup, kernel_rows, grad3, first=(spread3, sent, sum0.got, second.got), time=BLOCK)

    sent = sum2.advance(spread3_after)
    second = second.finish()
    grad_hidden, grad_output, grad_proj = second_out(second.mine, second.got, wide)
    grad_padded, to_below, to_above = finish(
        place_of, (spread0, spread1, spread2, spread2_after, spread3, spread3_after), first=(sent, grad_hidden)
    )
    cross_rows = swap(after(far_rows, spread3), 1)
    from_above = lax.ppermute(to_below, "pts", downs)
    from_below = lax.ppermute(to_above, "pts", ups)
    sent = sum1.advance(grad_padded)
    sent = sum2.advance(sent)
    block_out, grad_points = rows_out(
        place_of, grad_padded, from_below, from_above, block0, points0, near_rows, far_rows, cross_rows,
        first=(sent,),
    )

    grad_conv, grad_cpe, grad_qkv, *lines = grads_out([s.finish() for s in (sum0, sum1, sum2)], chunk, width)
    small = [line.reshape(-1) for line in lines[: VECTORS + 1]]
    return (
        block_out,
        grad_points,
        grad_conv.transpose(0, 2, 1),
        small[0],
        grad_cpe.T,
        *small[1:6],
        grad_qkv.transpose(1, 0, 2),
        lines[VECTORS + 1],
        grad_proj.T,
        small[8],
        small[6],
        small[7],
        grad_hidden,
        small[10],
        grad_output.T,
        small[9],
    )


def solution(mesh):
    return jax.shard_map(
        shards,
        mesh=mesh,
        in_specs=(
            P("pts", "blk"),
            P("pts", None),
            P("pts"),
            P(None, "blk", None),
            P("blk"),
            P("blk", None),
            P("blk"),
            P("blk"),
            P("blk"),
            P("blk"),
            P("blk"),
            P(None, None, "blk"),
            P(None, "blk"),
            P("blk", None),
            P("blk"),
            P("blk"),
            P("blk"),
            P(None, "blk"),
            P("blk"),
            P("blk", None),
            P("blk"),
            P("pts", "blk"),
        ),
        out_specs=(
            P("pts", "blk"),
            P("pts", "blk"),
            P(None, "blk", "pts"),
            P("blk"),
            P("blk", "pts"),
            P("blk"),
            P("blk"),
            P("blk"),
            P("blk"),
            P("blk"),
            P("pts", None, "blk"),
            P(None, "blk"),
            P("blk", "pts"),
            P("blk"),
            P("blk"),
            P("blk"),
            P("pts", "blk"),
            P("blk"),
            P("blk", "pts"),
            P("blk"),
        ),
        check_vma=False,
    )
```
